32 devices in a mesh: gx: 4 (over x, core), gy: 8 (over z, y).
Axes of the slice: x: 2, y: 2, z: 4, core: 2. Of those that a mesh axis runs over, the one named last changes fastest.
Arguments:
- forcing: float32 [8, 8, 8, 4, 8, 128], P(None, None, None, 'gx', 'gy'), may hold values from -6 to 6
- coefficient: float32 [8, 8, 8, 4, 8, 128], P(None, None, None, 'gx', 'gy'), may hold values from 0.3 to 3
Outputs:
- pressure: float32 [8, 8, 8, 4, 8, 128], P(None, None, None, 'gx', 'gy')
- residual: float32 [8, 8, 8, 4, 8, 128], P(None, None, None, 'gx', 'gy')
The draws below stay inside these ranges and needn't reach their ends.
All inputs are finite; a program needn't handle non-finite values.
Results may differ from the reference program's by a relative error of at most 0.0003.
Values sent between devices are 32-bit elements; how exact they have to be, the bound alone decides.
A program may use at most 64 MiB of HBM per device.

```python
import math
import jax
import jax.numpy as jnp
from jax import lax

NP = 8
EZ = 128
ITERS = 2
EX = 4
EY = 8


def draw_forcing(key, part):
    node_key = jax.random.fold_in(key, 11)
    elem_key = jax.random.fold_in(key, 12)
    full_shape = (NP, NP, NP, EX, EY, EZ)
    nodal = jax.random.normal(node_key, full_shape, jnp.float32)
    element_part = 0.5 * jax.random.normal(elem_key, (EX, EY, EZ), jnp.float32)
    field = nodal + element_part[None, None, None]
    return jnp.clip(field, -6.0, 6.0).astype(jnp.float32)


def shard_levels(rng, dims, cuts, smallest, top_value):
    loudness = 1.0
    for dim, blocks in cuts:
        steps = jax.random.uniform(jax.random.fold_in(jax.random.fold_in(rng, 6), dim), (blocks,), jnp.float32, smallest / len(cuts), top_value / len(cuts))
        loudness = loudness * jnp.repeat(jnp.exp(steps), dims[dim] // blocks).reshape((-1,) + (1,) * (len(dims) - 1 - dim))
    return loudness


def setup_inputs(seed: int = 0) -> dict:
    seeds = jax.random.split(jax.random.key(seed), 3)
    forcing = draw_forcing(jax.random.fold_in(seeds[2], 71), 0)
    coefficient = jnp.clip(jnp.exp(math.log(3.0) - 2.3025851 * jax.random.uniform(seeds[1], (NP, NP, NP, EX, EY, EZ), jnp.float32) ** shard_levels(seeds[1], (NP, NP, NP, EX, EY, EZ), ((3, 4), (4, 8)), -0.2, 0.2)), 0.3, 3.0)
    return dict(forcing=forcing, coefficient=coefficient)


stretch = (1.0, 64.0, 1.0)

def legendre_value(order, position):
    prev_value = 1.0
    this_value = position
    for degree_now in range(2, order + 1):
        next_value = ((2 * degree_now - 1) * position * this_value - (degree_now - 1) * prev_value) / degree_now
        prev_value = this_value
        this_value = next_value
    return this_value

def gll_points():
    points = [-1.0]
    for node_index in range(1, 7):
        position = -math.cos(math.pi * node_index / 7.0)
        for newton_step in range(60):
            target = legendre_value(8, position) - legendre_value(6, position)
            slope = 15.0 * legendre_value(7, position)
            position = position - target / slope
        points.append(position)
    points.append(1.0)
    return points

def jacobi_eigen(matrix_in):
    order_n = len(matrix_in)
    work_mat = [list(one_row) for one_row in matrix_in]
    vectors = [[1.0 if row_index == col_index else 0.0 for col_index in range(order_n)] for row_index in range(order_n)]
    for sweep_index in range(40):
        for first_idx in range(order_n):
            for second_idx in range(first_idx + 1, order_n):
                rotation = 0.5 * math.atan2(2.0 * work_mat[first_idx][second_idx], work_mat[second_idx][second_idx] - work_mat[first_idx][first_idx])
                cosine = math.cos(rotation)
                sine_part = math.sin(rotation)
                for other in range(order_n):
                    left_val = work_mat[other][first_idx]
                    right_val = work_mat[other][second_idx]
                    work_mat[other][first_idx] = cosine * left_val - sine_part * right_val
                    work_mat[other][second_idx] = sine_part * left_val + cosine * right_val
                for other in range(order_n):
                    left_val = work_mat[first_idx][other]
                    right_val = work_mat[second_idx][other]
                    work_mat[first_idx][other] = cosine * left_val - sine_part * right_val
                    work_mat[second_idx][other] = sine_part * left_val + cosine * right_val
                for other in range(order_n):
                    left_val = vectors[other][first_idx]
                    right_val = vectors[other][second_idx]
                    vectors[other][first_idx] = cosine * left_val - sine_part * right_val
                    vectors[other][second_idx] = sine_part * left_val + cosine * right_val
    return ([work_mat[diag_index][diag_index] for diag_index in range(order_n)], vectors)

def spectral_tables():
    nodes = gll_points()
    values_at = [legendre_value(7, position) for position in nodes]
    weights = [2.0 / (56.0 * value_now * value_now) for value_now in values_at]
    derivative = [[0.0] * 8 for row_index in range(8)]
    for row_index in range(8):
        for col_index in range(8):
            if row_index != col_index:
                derivative[row_index][col_index] = values_at[row_index] / (values_at[col_index] * (nodes[row_index] - nodes[col_index]))
    derivative[0][0] = -14.0
    derivative[7][7] = 14.0
    stiffness = [[sum((derivative[mid][row_index] * weights[mid] * derivative[mid][col_index] for mid in range(8))) for col_index in range(8)] for row_index in range(8)]
    stiffness[0][0] = 2.0 * stiffness[0][0]
    stiffness[7][7] = 2.0 * stiffness[7][7]
    inv_root = [1.0 / math.sqrt(weight_now) for weight_now in weights]
    symmetric = [[inv_root[row_index] * stiffness[row_index][col_index] * inv_root[col_index] for col_index in range(8)] for row_index in range(8)]
    eigen_values, eigen_vectors = jacobi_eigen(symmetric)
    fdm_basis = [[inv_root[row_index] * eigen_vectors[row_index][col_index] for col_index in range(8)] for row_index in range(8)]
    linear_hat = [[(1.0 - position) / 2.0 for position in nodes], [(1.0 + position) / 2.0 for position in nodes]]
    return tuple((jnp.asarray(one_table, dtype=jnp.float32) for one_table in (weights, derivative, fdm_basis, eigen_values, linear_hat)))

def contract(form, table, field):
    return jnp.einsum(form, table, field, precision=lax.Precision.HIGHEST)

def edge_factors(local_count, offset, total_count):
    node_ids = jnp.arange(8, dtype=jnp.int32)[:, None]
    element_ids = offset + jnp.arange(local_count, dtype=jnp.int32)[None, :]
    at_first = node_ids == 0
    at_last = node_ids == 7
    outside = at_first & (element_ids == 0) | at_last & (element_ids == total_count - 1)
    shared = at_first & (element_ids > 0) | at_last & (element_ids < total_count - 1)
    keep_factor = jnp.where(outside, 0.0, 1.0).astype(jnp.float32)
    share_factor = jnp.where(shared, 0.5, 1.0).astype(jnp.float32)
    return (keep_factor, share_factor)

def node_masks(counts, offsets, totals):
    keep_x, share_x = edge_factors(counts[0], offsets[0], totals[0])
    keep_y, share_y = edge_factors(counts[1], offsets[1], totals[1])
    keep_z, share_z = edge_factors(counts[2], offsets[2], totals[2])
    keep_mask = (keep_x[:, None, None, :, None, None], keep_y[None, :, None, None, :, None], keep_z[None, None, :, None, None, :])
    inv_mult = (share_x[:, None, None, :, None, None], share_y[None, :, None, None, :, None], share_z[None, None, :, None, None, :])
    return (keep_mask, inv_mult)

def apply_factors(field, factors):
    return field * factors[0] * factors[1] * factors[2]

def no_neighbours(first_rim, last_rim, elem_dim):
    return (jnp.zeros_like(last_rim), jnp.zeros_like(first_rim))

def pair_sum(field, node_dim, remote):
    elem_dim = node_dim + 2
    first = jnp.take(field, 0, axis=node_dim)
    last_face = jnp.take(field, 7, axis=node_dim)
    count = first.shape[elem_dim]
    first_rim = lax.index_in_dim(first, 0, elem_dim, keepdims=False)
    last_rim = lax.index_in_dim(last_face, count - 1, elem_dim, keepdims=False)
    prev_last, next_first = remote(first_rim, last_rim, elem_dim)
    next_all = jnp.concatenate([lax.slice_in_dim(first, 1, count, axis=elem_dim), jnp.expand_dims(next_first, elem_dim)], axis=elem_dim)
    prev_all = jnp.concatenate([jnp.expand_dims(prev_last, elem_dim), lax.slice_in_dim(last_face, 0, count - 1, axis=elem_dim)], axis=elem_dim)
    new_first = first + prev_all
    new_last = last_face + next_all
    middle = lax.slice_in_dim(field, 1, 7, axis=node_dim)
    return jnp.concatenate([jnp.expand_dims(new_first, node_dim), middle, jnp.expand_dims(new_last, node_dim)], axis=node_dim)

def direct_sum(field, remote_x, remote_y):
    field = pair_sum(field, 0, remote_x)
    field = pair_sum(field, 1, remote_y)
    return pair_sum(field, 2, no_neighbours)

def stiffness_apply(field, coefficient, derivative, weight_cube):
    scaled = coefficient * weight_cube
    grad_i = contract('pi,ijkxyz->pjkxyz', derivative, field)
    grad_j = contract('qj,ijkxyz->iqkxyz', derivative, field)
    grad_k = contract('rk,ijkxyz->ijrxyz', derivative, field)
    result = contract('pi,pjkxyz->ijkxyz', derivative, stretch[0] * scaled * grad_i)
    result = result + contract('qj,iqkxyz->ijkxyz', derivative, stretch[1] * scaled * grad_j)
    return result + contract('rk,ijrxyz->ijkxyz', derivative, stretch[2] * scaled * grad_k)

def fdm_apply(field, fdm_basis, denominator):
    moved = contract('ip,ijkxyz->pjkxyz', fdm_basis, field)
    moved = contract('jq,pjkxyz->pqkxyz', fdm_basis, moved)
    moved = contract('kr,pqkxyz->pqrxyz', fdm_basis, moved)
    moved = moved * denominator
    moved = contract('ip,pqrxyz->iqrxyz', fdm_basis, moved)
    moved = contract('jq,iqrxyz->ijrxyz', fdm_basis, moved)
    return contract('kr,ijrxyz->ijkxyz', fdm_basis, moved)

def restrict_corners(weighted, linear_hat):
    corners = contract('ai,ijkxyz->ajkxyz', linear_hat, weighted)
    corners = contract('bj,ajkxyz->abkxyz', linear_hat, corners)
    return contract('ck,abkxyz->abcxyz', linear_hat, corners)

def vertex_sum(corners):
    total_grid = jnp.zeros((corners.shape[3] + 1, corners.shape[4] + 1, corners.shape[5] + 1), jnp.float32)
    for side_x in range(2):
        for side_y in range(2):
            for side_z in range(2):
                total_grid = total_grid + jnp.pad(corners[side_x, side_y, side_z], ((side_x, 1 - side_x), (side_y, 1 - side_y), (side_z, 1 - side_z)))
    return total_grid

def prolong(vertices, linear_hat):
    count_x = vertices.shape[0] - 1
    count_y = vertices.shape[1] - 1
    count_z = vertices.shape[2] - 1
    corner_vals = jnp.stack([jnp.stack([jnp.stack([vertices[side_x:side_x + count_x, side_y:side_y + count_y, side_z:side_z + count_z] for side_z in range(2)]) for side_y in range(2)]) for side_x in range(2)])
    nodal = contract('ck,abcxyz->abkxyz', linear_hat, corner_vals)
    nodal = contract('bj,abkxyz->ajkxyz', linear_hat, nodal)
    return contract('ai,ajkxyz->ijkxyz', linear_hat, nodal)

def sine_system(cells):
    wave_ints = jnp.arange(1, cells, dtype=jnp.int32)
    product_ids = wave_ints[:, None] * wave_ints[None, :] % (2 * cells)
    sine_table = math.sqrt(2.0 / cells) * jnp.sin(math.pi * product_ids.astype(jnp.float32) / cells)
    cosines = jnp.cos(math.pi * wave_ints.astype(jnp.float32) / cells)
    stiff_eig = (2.0 - 2.0 * cosines) / 2.0
    mass_eig = 2.0 * (4.0 + 2.0 * cosines) / 6.0
    return (sine_table, stiff_eig, mass_eig)

def coarse_solve(vertices):
    interior = vertices[1:-1, 1:-1, 1:-1]
    table_x, stiff_x, mass_x = sine_system(vertices.shape[0] - 1)
    table_y, stiff_y, mass_y = sine_system(vertices.shape[1] - 1)
    table_z, stiff_z, mass_z = sine_system(vertices.shape[2] - 1)
    moved = contract('mi,ijk->mjk', table_x, interior)
    moved = contract('nj,mjk->mnk', table_y, moved)
    moved = contract('ok,mnk->mno', table_z, moved)
    denominator = stretch[0] * stiff_x[:, None, None] * mass_y[None, :, None] * mass_z[None, None, :]
    denominator = denominator + stretch[1] * mass_x[:, None, None] * stiff_y[None, :, None] * mass_z[None, None, :]
    denominator = denominator + stretch[2] * mass_x[:, None, None] * mass_y[None, :, None] * stiff_z[None, None, :]
    moved = moved / denominator
    moved = contract('mi,mno->ino', table_x, moved)
    moved = contract('nj,ino->ijo', table_y, moved)
    moved = contract('ok,ijo->ijk', table_z, moved)
    return jnp.pad(moved, 1)

def reference(forcing, coefficient):
    weights, derivative, fdm_basis, eigen_values, linear_hat = spectral_tables()
    count_x, count_y, count_z = (forcing.shape[3], forcing.shape[4], forcing.shape[5])
    keep_mask, inv_mult = node_masks((count_x, count_y, count_z), (0, 0, 0), (count_x, count_y, count_z))
    weight_cube = (weights[:, None, None] * weights[None, :, None] * weights[None, None, :])[:, :, :, None, None, None]
    eigen_sum = stretch[0] * eigen_values[:, None, None] + stretch[1] * eigen_values[None, :, None] + stretch[2] * eigen_values[None, None, :]
    denominator = (1.0 / eigen_sum)[:, :, :, None, None, None]

    def assemble(field):
        return direct_sum(field, no_neighbours, no_neighbours)

    def operate(field):
        return apply_factors(assemble(stiffness_apply(field, coefficient, derivative, weight_cube)), keep_mask)

    def precondition(field):
        local_part = apply_factors(assemble(fdm_apply(field, fdm_basis, denominator)), keep_mask)
        vertices = vertex_sum(restrict_corners(apply_factors(field, inv_mult), linear_hat))
        return local_part + prolong(coarse_solve(vertices), linear_hat)

    def inner_sum(left, right):
        return jnp.sum(apply_factors(left * right, inv_mult))
    load_vec = apply_factors(assemble(forcing), keep_mask)
    pressure = jnp.zeros_like(load_vec)
    residual = load_vec
    smoothed = precondition(residual)
    direction = smoothed
    energy_now = inner_sum(residual, smoothed)
    for step_index in range(ITERS):
        image_dir = operate(direction)
        step_size = energy_now / inner_sum(direction, image_dir)
        pressure = pressure + step_size * direction
        residual = residual - step_size * image_dir
        if step_index + 1 < ITERS:
            smoothed = precondition(residual)
            energy_next = inner_sum(residual, smoothed)
            direction = smoothed + energy_next / energy_now * direction
            energy_now = energy_next
    return (pressure, residual)
```

```python
import functools
import math

import jax
import jax.numpy as jnp
import numpy as np
from jax import lax
from jax.experimental import pallas as pl
from jax.experimental.pallas import tpu as pltpu
from jax.sharding import PartitionSpec as P

MESH = pl.DeviceIdType.MESH
stretch = (1.0, 64.0, 1.0)
DIRS = ((-1, 0), (1, 0), (0, -1), (0, 1), (-1, -1), (-1, 1), (1, -1), (1, 1))


def legendre_value(order, position):
    prev_value = 1.0
    this_value = position
    for degree_now in range(2, order + 1):
        next_value = (
            (2 * degree_now - 1) * position * this_value - (degree_now - 1) * prev_value
        ) / degree_now
        prev_value = this_value
        this_value = next_value
    return this_value


def gll_points():
    points = [-1.0]
    for node_index in range(1, 7):
        position = -math.cos(math.pi * node_index / 7.0)
        for newton_step in range(60):
            target = legendre_value(8, position) - legendre_value(6, position)
            slope = 15.0 * legendre_value(7, position)
            position = position - target / slope
        points.append(position)
    points.append(1.0)
    return points


def jacobi_eigen(matrix_in):
    order_n = len(matrix_in)
    work_mat = [list(one_row) for one_row in matrix_in]
    vectors = [
        [1.0 if row_index == col_index else 0.0 for col_index in range(order_n)]
        for row_index in range(order_n)
    ]
    for sweep_index in range(40):
        for first_idx in range(order_n):
            for second_idx in range(first_idx + 1, order_n):
                rotation = 0.5 * math.atan2(
                    2.0 * work_mat[first_idx][second_idx],
                    work_mat[second_idx][second_idx] - work_mat[first_idx][first_idx],
                )
                cosine = math.cos(rotation)
                sine_part = math.sin(rotation)
                for other in range(order_n):
                    left_val = work_mat[other][first_idx]
                    right_val = work_mat[other][second_idx]
                    work_mat[other][first_idx] = cosine * left_val - sine_part * right_val
                    work_mat[other][second_idx] = sine_part * left_val + cosine * right_val
                for other in range(order_n):
                    left_val = work_mat[first_idx][other]
                    right_val = work_mat[second_idx][other]
                    work_mat[first_idx][other] = cosine * left_val - sine_part * right_val
                    work_mat[second_idx][other] = sine_part * left_val + cosine * right_val
                for other in range(order_n):
                    left_val = vectors[other][first_idx]
                    right_val = vectors[other][second_idx]
                    vectors[other][first_idx] = cosine * left_val - sine_part * right_val
                    vectors[other][second_idx] = sine_part * left_val + cosine * right_val
    return ([work_mat[diag_index][diag_index] for diag_index in range(order_n)], vectors)


def spectral_tables():
    nodes = gll_points()
    values_at = [legendre_value(7, position) for position in nodes]
    weights = [2.0 / (56.0 * value_now * value_now) for value_now in values_at]
    derivative = np.zeros((8, 8))
    for row in range(8):
        for col in range(8):
            if row != col:
                derivative[row, col] = values_at[row] / (
                    values_at[col] * (nodes[row] - nodes[col])
                )
    derivative[0, 0] = -14.0
    derivative[7, 7] = 14.0
    weights = np.array(weights)
    stiffness = derivative.T @ np.diag(weights) @ derivative
    stiffness[0, 0] *= 2.0
    stiffness[7, 7] *= 2.0
    inv_root = 1.0 / np.sqrt(weights)
    symmetric = inv_root[:, None] * stiffness * inv_root[None, :]
    eigen_values, eigen_vectors = jacobi_eigen(symmetric.tolist())
    fdm_basis = inv_root[:, None] * np.array(eigen_vectors)
    nodes = np.array(nodes)
    hats = np.stack([(1.0 - nodes) / 2.0, (1.0 + nodes) / 2.0])
    return weights, derivative, fdm_basis, np.array(eigen_values), hats


def sine_table(cells):
    ids = np.arange(cells + 1)
    table = math.sqrt(2.0 / cells) * np.sin(math.pi * (np.outer(ids, ids) % (2 * cells)) / cells)
    table[0] = table[-1] = 0.0
    table[:, 0] = table[:, -1] = 0.0
    return table


def mode_values(cells):
    cosines = np.cos(math.pi * np.arange(1, cells) / cells)
    return (2.0 - 2.0 * cosines) / 2.0, 2.0 * (4.0 + 2.0 * cosines) / 6.0


def round_up(value, step):
    return -(-value // step) * step


def halves(table):
    table = np.asarray(table, np.float32)
    high = table.astype(jnp.bfloat16)
    low = (table - high.astype(np.float32)).astype(jnp.bfloat16)
    return np.concatenate([high, low], axis=0)


def element_tables():
    weights, derivative, basis, eigen, hats = spectral_tables()
    eye = np.eye(8)
    cube = np.kron(np.kron(basis, basis), basis)
    total = (
        stretch[0] * eigen[:, None, None]
        + stretch[1] * eigen[None, :, None]
        + stretch[2] * eigen[None, None, :]
    ).reshape(-1)
    solve = (cube / total) @ cube.T
    along_j = np.kron(np.eye(4), np.kron(derivative, eye))
    along_k = np.kron(np.eye(4), np.kron(eye, derivative))
    forward = np.concatenate([along_j, along_k], axis=0)
    backward = np.concatenate([stretch[1] * along_j.T, stretch[2] * along_k.T], axis=1)
    corner = np.stack(
        [
            np.kron(np.kron(hats[a], hats[b]), hats[c])
            for c in range(2)
            for a in range(2)
            for b in range(2)
        ]
    )
    return weights, derivative, solve, forward, backward, corner


def coarse_tables(size_x, size_y, depth):
    sine_x, sine_y, sine_z = sine_table(size_x), sine_table(size_y), sine_table(depth)
    modes = (size_x - 1) * (size_y - 1)
    rows = round_up(modes + 2, 8)
    gather = np.zeros((rows, size_x, size_y, 4))
    for x in range(size_x):
        for y in range(size_y):
            for a in range(2):
                for b in range(2):
                    gather[:modes, x, y, 2 * a + b] = np.outer(
                        sine_x[1:-1, x + a], sine_y[1:-1, y + b]
                    ).reshape(-1)
    for q in range(2):
        gather[modes + q, :, :, q] = 1.0
    stiff_x, mass_x = mode_values(size_x)
    stiff_y, mass_y = mode_values(size_y)
    stiff_z, mass_z = mode_values(depth)
    denominator = (
        stretch[0] * stiff_x[:, None, None] * mass_y[None, :, None] * mass_z[None, None, :]
        + stretch[1] * mass_x[:, None, None] * stiff_y[None, :, None] * mass_z[None, None, :]
        + stretch[2] * mass_x[:, None, None] * mass_y[None, :, None] * stiff_z[None, None, :]
    )
    inverse = np.zeros((rows, depth))
    inverse[:modes, 1:] = (1.0 / denominator).reshape(modes, depth - 1)
    back = np.zeros((size_x, size_y, 8, rows))
    for x in range(size_x):
        for y in range(size_y):
            for c in range(2):
                for a in range(2):
                    for b in range(2):
                        back[x, y, 4 * c + 2 * a + b, :modes] = np.outer(
                            sine_x[1:-1, x + a], sine_y[1:-1, y + b]
                        ).reshape(-1)
    return (
        gather.reshape(rows, -1),
        inverse,
        back.reshape(size_x * size_y, 8, rows),
        sine_z[:depth, :depth],
    )


def parts(field):
    high = field.astype(jnp.bfloat16)
    return high, (field - high.astype(jnp.float32)).astype(jnp.bfloat16)


def both_dot(left, right):
    rows, lanes = left.shape[0], right.shape[1]
    sums = jnp.dot(
        jnp.concatenate(parts(left), axis=0),
        jnp.concatenate(parts(right), axis=1),
        preferred_element_type=jnp.float32,
    )
    return (sums[:rows, :lanes] + sums[rows:, :lanes]) + (sums[:rows, lanes:] + sums[rows:, lanes:])


def split_dot(table, field):
    lanes = field.shape[1]
    rows = table.shape[0] // 2
    high = field.astype(jnp.bfloat16)
    low = (field - high.astype(jnp.float32)).astype(jnp.bfloat16)
    both = jnp.concatenate([high, low], axis=1)
    top = jnp.dot(table[:rows], both, preferred_element_type=jnp.float32)
    bottom = jnp.dot(table[rows:], both, preferred_element_type=jnp.float32)
    return (top[:, :lanes] + bottom[:, :lanes]) + (top[:, lanes:] + bottom[:, lanes:])


def kernel(size_x, size_y, weights, derivative, modes, *refs):
    n_in = 11
    inputs, (p_ref, r_ref) = refs[:n_in], refs[n_in : n_in + 2]
    local = refs[n_in + 2 : 2 * n_in + 2]
    (
        cw, out, base, first, second, image, alpha, beta_raw, smooth,
        rx, ry, re, message_ref, got,
        in_sem, halo_send, halo_recv, all_send, all_recv,
    ) = refs[2 * n_in + 2 :]
    (
        f_ref, corner_ref, coef_ref, weight_ref, solve_ref,
        gather_ref, sine_ref, inverse_ref, back_ref, forward_ref, backward_ref,
    ) = local
    lanes = f_ref.shape[2]
    my_x = lax.axis_index("gx")
    my_y = lax.axis_index("gy")
    devices = size_x * size_y
    me = my_x * size_y + my_y

    fetches = [
        pltpu.make_async_copy(inputs[n], local[n], in_sem.at[n]) for n in range(n_in)
    ]
    for fetch in fetches:
        fetch.start()

    def exists(direction):
        dx, dy = direction
        ok = None
        for pos, size, step in ((my_x, size_x, dx), (my_y, size_y, dy)):
            if step:
                cond = pos > 0 if step < 0 else pos < size - 1
                ok = cond if ok is None else jnp.logical_and(ok, cond)
        return ok

    def peer(offset):
        other = lax.rem(me + offset, devices)
        return (other // size_y, lax.rem(other, size_y))

    barrier = pltpu.get_barrier_semaphore()

    @pl.loop(1, devices)
    def _(offset):
        pl.semaphore_signal(barrier, inc=1, device_id=peer(offset), device_id_type=MESH)

    def node_rows(step):
        return 0 if step < 0 else 7

    def source(direction):
        dx, dy = direction
        if dy == 0:
            return out.at[node_rows(dx)]
        ys = pl.ds(8 * node_rows(dy), 8)
        if dx == 0:
            return out.at[:, ys]
        return out.at[node_rows(dx), ys]

    def landing(turn, index):
        if index < 2:
            return rx.at[turn, index]
        if index < 4:
            return ry.at[turn, index - 2]
        return re.at[turn, index - 4]

    def halo_copy(turn, index):
        direction = DIRS[index]
        opposite = DIRS.index((-direction[0], -direction[1]))
        return pltpu.make_async_remote_copy(
            src_ref=source(direction),
            dst_ref=landing(turn, opposite),
            send_sem=halo_send.at[turn, index],
            recv_sem=halo_recv.at[turn, opposite],
            device_id=(my_x + direction[0], my_y + direction[1]),
            device_id_type=MESH,
        )

    def halo_arrival(turn, index):
        direction = DIRS[index]
        return pltpu.make_async_remote_copy(
            src_ref=source(direction),
            dst_ref=landing(turn, index),
            send_sem=halo_send.at[turn, index],
            recv_sem=halo_recv.at[turn, index],
            device_id=(my_x + direction[0], my_y + direction[1]),
            device_id_type=MESH,
        )

    lane = lax.broadcasted_iota(jnp.int32, (8, 8, lanes), 2)

    def sum_depth(raw):
        out[...] = raw
        head = out[:, pl.ds(0, 8, stride=8), :]
        tail = out[:, pl.ds(7, 8, stride=8), :]
        from_tail = pltpu.roll(tail.reshape(64, lanes), 1, 1).reshape(8, 8, lanes)
        from_head = pltpu.roll(head.reshape(64, lanes), lanes - 1, 1).reshape(8, 8, lanes)
        out[:, pl.ds(0, 8, stride=8), :] = jnp.where(lane == 0, 0.0, head + from_tail)
        out[:, pl.ds(7, 8, stride=8), :] = jnp.where(lane == lanes - 1, 0.0, tail + from_head)

    def send_halo(turn):
        for index in range(8):
            @pl.when(exists(DIRS[index]))
            def _(index=index):
                halo_copy(turn, index).start()

    def take_halo(turn, target):
        for index in range(8):
            @pl.when(exists(DIRS[index]))
            def _(index=index):
                halo_copy(turn, index).wait_send()
                halo_arrival(turn, index).wait_recv()

        has = [exists(direction) for direction in DIRS[:4]]
        target[pl.ds(1, 6), pl.ds(8, 48)] = out[pl.ds(1, 6), pl.ds(8, 48)]
        for side in range(2):
            i = 7 * side
            target[i, pl.ds(8, 48)] = jnp.where(
                has[side], out[i, pl.ds(8, 48)] + rx[turn, side, pl.ds(8, 48)], 0.0
            )
            target[pl.ds(1, 6), pl.ds(8 * i, 8)] = jnp.where(
                has[2 + side],
                out[pl.ds(1, 6), pl.ds(8 * i, 8)] + ry[turn, side, pl.ds(1, 6)],
                0.0,
            )
            for other in range(2):
                j = 7 * other
                target[i, pl.ds(8 * j, 8)] = jnp.where(
                    jnp.logical_and(has[side], has[2 + other]),
                    (out[i, pl.ds(8 * j, 8)] + rx[turn, side, pl.ds(8 * j, 8)])
                    + (ry[turn, other, i] + re[turn, 2 * side + other]),
                    0.0,
                )

    def send_all(turn, value):
        message_ref[turn] = value
        got[turn, me] = value

        @pl.loop(1, devices)
        def _(offset):
            pltpu.make_async_remote_copy(
                src_ref=message_ref.at[turn],
                dst_ref=got.at[turn, me],
                send_sem=all_send.at[turn],
                recv_sem=all_recv.at[turn],
                device_id=peer(offset),
                device_id_type=MESH,
            ).start()

    def take_all(turn):
        span = got.at[turn, pl.ds(0, devices - 1)]
        copy = pltpu.make_async_remote_copy(
            src_ref=span,
            dst_ref=span,
            send_sem=all_send.at[turn],
            recv_sem=all_recv.at[turn],
            device_id=peer(1),
            device_id_type=MESH,
        )
        copy.wait_send()
        copy.wait_recv()
        return got[turn]

    row = lax.broadcasted_iota(jnp.int32, (8, lanes), 0)
    row4 = lax.broadcasted_iota(jnp.int32, (4, lanes), 0)
    lane4 = lax.broadcasted_iota(jnp.int32, (4, lanes), 1)

    def corner_message(raw):
        corners = both_dot(corner_ref[...], raw)
        moved = pltpu.roll(pltpu.roll(corners, 1, 1), 4, 0)
        return (corners + moved)[:4]

    def coarse_values(turn):
        gathered = take_all(turn).reshape(devices * 4, lanes)
        combined = both_dot(gather_ref[...], gathered)
        spectral = both_dot(combined, sine_ref[...]) * inverse_ref[...]
        mine = both_dot(back_ref[me], spectral)
        columns = both_dot(mine, sine_ref[...])
        corners = jnp.where(row < 4, columns, pltpu.roll(columns, lanes - 1, 1))
        return both_dot(corner_ref[...].T, corners), combined

    def local_solve(field):
        return split_dot(solve_ref[...], field).reshape(8, 64, lanes)

    def stiffness(field_ref, target):
        for half in range(2):
            span = pl.ds(4 * half, 4)
            values = field_ref[span] - field_ref[span, pl.ds(27, 1)]
            grads = split_dot(forward_ref[...], values.reshape(256, lanes))
            factor = cw[span].reshape(256, lanes)
            flux = jnp.concatenate([grads[:256] * factor, grads[256:] * factor], axis=0)
            target[span] = split_dot(backward_ref[...], flux).reshape(4, 64, lanes)
        for part in range(8):
            span = pl.ds(8 * part, 8)
            values = [field_ref[i, span] for i in range(8)]
            flux = []
            for p in range(8):
                grad = values[0] * derivative[p][0]
                for i in range(1, 8):
                    grad = grad + values[i] * derivative[p][i]
                flux.append(grad * cw[p, span])
            for i in range(8):
                total = target[i, span]
                for p in range(8):
                    total = total + flux[p] * derivative[p][i]
                target[i, span] = total

    def partial(left, right):
        return jnp.sum((left * right).reshape(64, 8, lanes), axis=0)

    def row_sum(tile):
        return jnp.sum(tile, axis=0, keepdims=True)

    def total(rows):
        return jnp.sum(rows, axis=(0, 1), keepdims=True)

    fetches[0].wait()
    sum_depth(f_ref[...])
    pl.semaphore_wait(barrier, devices - 1)
    send_halo(0)
    fetches[1].wait()
    send_all(0, corner_message(f_ref[...].reshape(512, lanes)))
    fetches[2].wait()
    fetches[3].wait()
    for i in range(8):
        cw[i] = coef_ref[i] * (weight_ref[...] * weights[i])
    for fetch in fetches[4:]:
        fetch.wait()
    take_halo(0, base)

    sum_depth(local_solve(base[...].reshape(512, lanes)))
    send_halo(1)
    coarse, _ = coarse_values(0)
    take_halo(1, first)
    first[...] += coarse.reshape(8, 64, lanes)

    stiffness(first, alpha)
    sum_depth(alpha[...])
    send_halo(2)
    message = corner_message(alpha[...].reshape(512, lanes))
    energy = total(partial(f_ref[...], first[...]))
    curve = total(partial(alpha[...], first[...]))
    message = jnp.where(
        lane4 == 0, jnp.where(row4 == 0, energy, jnp.where(row4 == 1, curve, 0.0)), message
    )
    send_all(1, message)
    take_halo(2, image)

    sum_depth(local_solve(image[...].reshape(512, lanes)))
    send_halo(3)
    coarse, combined = coarse_values(1)
    energy = combined[modes : modes + 1, 0:1]
    curve = combined[modes + 1 : modes + 2, 0:1]
    step = energy / curve
    take_halo(3, smooth)
    step3 = step.reshape(1, 1, 1)
    second[...] = first[...] - step3 * (smooth[...] + coarse.reshape(8, 64, lanes))

    stiffness(second, beta_raw)
    sum_depth(beta_raw[...])
    send_halo(4)
    fresh = row_sum(partial(f_ref[...] - step3 * alpha[...], second[...]))
    along = row_sum(partial(beta_raw[...], second[...]))
    cross = row_sum(partial(alpha[...], second[...]))
    send_all(
        2,
        jnp.where(
            row4 == 0, fresh, jnp.where(row4 == 1, along, jnp.where(row4 == 2, cross, 0.0))
        ),
    )
    take_halo(4, smooth)
    sums = jnp.sum(take_all(2), axis=0)
    fresh = total(sums[0:1])
    ratio = fresh / energy
    along = total(sums[1:2]) + 2.0 * ratio * total(sums[2:3]) + ratio * ratio * curve
    second_step = fresh / along
    ratio3 = ratio.reshape(1, 1, 1)
    second3 = second_step.reshape(1, 1, 1)
    p_ref[...] = step3 * first[...] + second3 * (second[...] + ratio3 * first[...])
    r_ref[...] = (base[...] - step3 * image[...]) - second3 * (smooth[...] + ratio3 * image[...])


def solution(mesh):
    size_x, size_y = mesh.shape["gx"], mesh.shape["gy"]
    devices = size_x * size_y
    weights, derivative, solve, forward, backward, corner = element_tables()
    spec = P(None, None, None, "gx", "gy", None)

    def on_device(forcing, coefficient):
        shape = forcing.shape
        depth = shape[5]
        gather, inverse, back, sine = coarse_tables(size_x, size_y, depth)
        modes = (size_x - 1) * (size_y - 1)
        plane = np.outer(weights, weights).reshape(64, 1) * np.ones((1, depth))
        single = [
            np.asarray(table, np.float32)
            for table in (corner, plane, gather, sine, inverse, back)
        ]
        field = (8, 64, depth)
        operands = [
            forcing.reshape(field), single[0], coefficient.reshape(field), single[1],
            halves(solve), *single[2:], halves(forward), halves(backward),
        ]
        vmem = pl.BlockSpec(memory_space=pltpu.VMEM)
        pressure, residual = pl.pallas_call(
            functools.partial(
                kernel, size_x, size_y, weights.tolist(), derivative.tolist(), modes
            ),
            out_shape=[jax.ShapeDtypeStruct(field, jnp.float32)] * 2,
            in_specs=[pl.BlockSpec(memory_space=pltpu.HBM)] * len(operands),
            out_specs=[vmem, vmem],
            scratch_shapes=[pltpu.VMEM(op.shape, op.dtype) for op in operands]
            + [pltpu.VMEM(field, jnp.float32)] * 9
            + [
                pltpu.VMEM((5, 2, 64, depth), jnp.float32),
                pltpu.VMEM((5, 2, 8, 8, depth), jnp.float32),
                pltpu.VMEM((5, 4, 8, depth), jnp.float32),
                pltpu.VMEM((3, 4, depth), jnp.float32),
                pltpu.VMEM((3, devices, 4, depth), jnp.float32),
                pltpu.SemaphoreType.DMA((len(operands),)),
                pltpu.SemaphoreType.DMA((5, 8)),
                pltpu.SemaphoreType.DMA((5, 8)),
                pltpu.SemaphoreType.DMA((3,)),
                pltpu.SemaphoreType.DMA((3,)),
            ],
            compiler_params=pltpu.CompilerParams(
                collective_id=0, has_side_effects=True, vmem_limit_bytes=60 * 1024 * 1024
            ),
        )(*operands)
        return pressure.reshape(shape), residual.reshape(shape)

    return jax.shard_map(
        on_device, mesh=mesh, in_specs=(spec, spec), out_specs=(spec, spec), check_vma=False
    )
```

```python
import functools
import math

import jax
import jax.numpy as jnp
import numpy as np
from jax import lax
from jax.experimental import pallas as pl
from jax.experimental.pallas import tpu as pltpu
from jax.sharding import PartitionSpec as P

MESH = pl.DeviceIdType.MESH
stretch = (1.0, 64.0, 1.0)
DIRS = ((-1, 0), (1, 0), (0, -1), (0, 1), (-1, -1), (-1, 1), (1, -1), (1, 1))


def legendre_value(order, position):
    prev_value = 1.0
    this_value = position
    for degree_now in range(2, order + 1):
        next_value = (
            (2 * degree_now - 1) * position * this_value - (degree_now - 1) * prev_value
        ) / degree_now
        prev_value = this_value
        this_value = next_value
    return this_value


def gll_points():
    points = [-1.0]
    for node_index in range(1, 7):
        position = -math.cos(math.pi * node_index / 7.0)
        for newton_step in range(60):
            target = legendre_value(8, position) - legendre_value(6, position)
            slope = 15.0 * legendre_value(7, position)
            position = position - target / slope
        points.append(position)
    points.append(1.0)
    return points


def jacobi_eigen(matrix_in):
    order_n = len(matrix_in)
    work_mat = [list(one_row) for one_row in matrix_in]
    vectors = [
        [1.0 if row_index == col_index else 0.0 for col_index in range(order_n)]
        for row_index in range(order_n)
    ]
    for sweep_index in range(40):
        for first_idx in range(order_n):
            for second_idx in range(first_idx + 1, order_n):
                rotation = 0.5 * math.atan2(
                    2.0 * work_mat[first_idx][second_idx],
                    work_mat[second_idx][second_idx] - work_mat[first_idx][first_idx],
                )
                cosine = math.cos(rotation)
                sine_part = math.sin(rotation)
                for other in range(order_n):
                    left_val = work_mat[other][first_idx]
                    right_val = work_mat[other][second_idx]
                    work_mat[other][first_idx] = cosine * left_val - sine_part * right_val
                    work_mat[other][second_idx] = sine_part * left_val + cosine * right_val
                for other in range(order_n):
                    left_val = work_mat[first_idx][other]
                    right_val = work_mat[second_idx][other]
                    work_mat[first_idx][other] = cosine * left_val - sine_part * right_val
                    work_mat[second_idx][other] = sine_part * left_val + cosine * right_val
                for other in range(order_n):
                    left_val = vectors[other][first_idx]
                    right_val = vectors[other][second_idx]
                    vectors[other][first_idx] = cosine * left_val - sine_part * right_val
                    vectors[other][second_idx] = sine_part * left_val + cosine * right_val
    return ([work_mat[diag_index][diag_index] for diag_index in range(order_n)], vectors)


def spectral_tables():
    nodes = gll_points()
    values_at = [legendre_value(7, position) for position in nodes]
    weights = [2.0 / (56.0 * value_now * value_now) for value_now in values_at]
    derivative = np.zeros((8, 8))
    for row in range(8):
        for col in range(8):
            if row != col:
                derivative[row, col] = values_at[row] / (
                    values_at[col] * (nodes[row] - nodes[col])
                )
    derivative[0, 0] = -14.0
    derivative[7, 7] = 14.0
    weights = np.array(weights)
    stiffness = derivative.T @ np.diag(weights) @ derivative
    stiffness[0, 0] *= 2.0
    stiffness[7, 7] *= 2.0
    inv_root = 1.0 / np.sqrt(weights)
    symmetric = inv_root[:, None] * stiffness * inv_root[None, :]
    eigen_values, eigen_vectors = jacobi_eigen(symmetric.tolist())
    fdm_basis = inv_root[:, None] * np.array(eigen_vectors)
    nodes = np.array(nodes)
    hats = np.stack([(1.0 - nodes) / 2.0, (1.0 + nodes) / 2.0])
    return weights, derivative, fdm_basis, np.array(eigen_values), hats


def sine_table(cells):
    ids = np.arange(cells + 1)
    table = math.sqrt(2.0 / cells) * np.sin(math.pi * (np.outer(ids, ids) % (2 * cells)) / cells)
    table[0] = table[-1] = 0.0
    table[:, 0] = table[:, -1] = 0.0
    return table


def mode_values(cells):
    cosines = np.cos(math.pi * np.arange(1, cells) / cells)
    return (2.0 - 2.0 * cosines) / 2.0, 2.0 * (4.0 + 2.0 * cosines) / 6.0


def round_up(value, step):
    return -(-value // step) * step


def halves(table):
    table = np.asarray(table, np.float32)
    high = table.astype(jnp.bfloat16)
    low = (table - high.astype(np.float32)).astype(jnp.bfloat16)
    return np.concatenate([high, low], axis=0)


def pieces(table, count):
    table = np.asarray(table, np.float32)
    found = []
    for _ in range(count):
        found.append(table.astype(jnp.bfloat16))
        table = table - found[-1].astype(np.float32)
    return np.concatenate(found + [found[0]], axis=1)


def element_tables():
    weights, derivative, basis, eigen, hats = spectral_tables()
    eye = np.eye(8)
    cube = np.kron(np.kron(basis, basis), basis)
    total = (
        stretch[0] * eigen[:, None, None]
        + stretch[1] * eigen[None, :, None]
        + stretch[2] * eigen[None, None, :]
    ).reshape(-1)
    solve = (cube / total) @ cube.T
    along_j = np.kron(np.eye(4), np.kron(derivative, eye))
    along_k = np.kron(np.eye(4), np.kron(eye, derivative))
    forward = np.concatenate([along_j, along_k], axis=0)
    backward = np.concatenate([stretch[1] * along_j.T, stretch[2] * along_k.T], axis=1)
    corner = np.stack(
        [
            np.kron(np.kron(hats[a], hats[b]), hats[c])
            for c in range(2)
            for a in range(2)
            for b in range(2)
        ]
    )
    return weights, derivative, solve, forward, backward, corner


def coarse_tables(size_x, size_y, depth):
    sine_x, sine_y, sine_z = sine_table(size_x), sine_table(size_y), sine_table(depth)
    modes = (size_x - 1) * (size_y - 1)
    rows = round_up(modes + 2, 8)
    gather = np.zeros((rows, size_x, size_y, 4))
    for x in range(size_x):
        for y in range(size_y):
            for a in range(2):
                for b in range(2):
                    gather[:modes, x, y, 2 * a + b] = np.outer(
                        sine_x[1:-1, x + a], sine_y[1:-1, y + b]
                    ).reshape(-1)
    for q in range(2):
        gather[modes + q, :, :, q] = 1.0
    stiff_x, mass_x = mode_values(size_x)
    stiff_y, mass_y = mode_values(size_y)
    stiff_z, mass_z = mode_values(depth)
    denominator = (
        stretch[0] * stiff_x[:, None, None] * mass_y[None, :, None] * mass_z[None, None, :]
        + stretch[1] * mass_x[:, None, None] * stiff_y[None, :, None] * mass_z[None, None, :]
        + stretch[2] * mass_x[:, None, None] * mass_y[None, :, None] * stiff_z[None, None, :]
    )
    inverse = np.zeros((rows, depth))
    inverse[:modes, 1:] = (1.0 / denominator).reshape(modes, depth - 1)
    back = np.zeros((size_x, size_y, 8, rows))
    for x in range(size_x):
        for y in range(size_y):
            for c in range(2):
                for a in range(2):
                    for b in range(2):
                        back[x, y, 4 * c + 2 * a + b, :modes] = np.outer(
                            sine_x[1:-1, x + a], sine_y[1:-1, y + b]
                        ).reshape(-1)
    return (
        gather.reshape(rows, -1),
        inverse,
        back.reshape(size_x * size_y, 8, rows),
        sine_z[:depth, :depth],
    )


def parts(field):
    high = field.astype(jnp.bfloat16)
    return high, (field - high.astype(jnp.float32)).astype(jnp.bfloat16)


def both_dot(left, right):
    rows, lanes = left.shape[0], right.shape[1]
    sums = jnp.dot(
        jnp.concatenate(parts(left), axis=0),
        jnp.concatenate(parts(right), axis=1),
        preferred_element_type=jnp.float32,
    )
    return (sums[:rows, :lanes] + sums[rows:, :lanes]) + (sums[:rows, lanes:] + sums[rows:, lanes:])


def split_dot(table, field):
    lanes = field.shape[1]
    rows = table.shape[0] // 2
    high = field.astype(jnp.bfloat16)
    low = (field - high.astype(jnp.float32)).astype(jnp.bfloat16)
    both = jnp.concatenate([high, low], axis=1)
    top = jnp.dot(table[:rows], both, preferred_element_type=jnp.float32)
    bottom = jnp.dot(table[rows:], both, preferred_element_type=jnp.float32)
    return (top[:, :lanes] + bottom[:, :lanes]) + (top[:, lanes:] + bottom[:, lanes:])


def wide_dot(table, field):
    high, low = parts(field)
    pieces = table.shape[1] // field.shape[0]
    return jnp.dot(
        table,
        jnp.concatenate([high] * (pieces - 1) + [low], axis=0),
        preferred_element_type=jnp.float32,
    )


def copy_kernel(p_in, r_in, p_out, r_out, sem):
    half = p_in.shape[0] // 2
    copies = []
    for n, (source, target) in enumerate(((p_in, p_out), (r_in, r_out))):
        for k in range(2):
            span = pl.ds(k * half, half)
            copies.append(
                pltpu.make_async_copy(source.at[span], target.at[span], sem.at[2 * n + k])
            )
    for copy in copies:
        copy.start()
    for copy in copies:
        copy.wait()


def kernel(size_x, size_y, weights, derivative, modes, *refs):
    n_in = 11
    inputs, (p_ref, r_ref) = refs[:n_in], refs[n_in : n_in + 2]
    local = refs[n_in + 2 : 2 * n_in + 2]
    (
        cw, out, base, first, second, image, alpha, beta_raw, smooth,
        rx, ry, re, message_ref, got,
        in_sem, halo_send, halo_recv, all_send, all_recv,
    ) = refs[2 * n_in + 2 :]
    (
        f_ref, corner_ref, coef_ref, weight_ref, solve_ref,
        gather_ref, sine_ref, inverse_ref, back_ref, forward_ref, backward_ref,
    ) = local
    lanes = f_ref.shape[2]
    my_x = lax.axis_index("gx")
    my_y = lax.axis_index("gy")
    devices = size_x * size_y
    me = my_x * size_y + my_y

    fetches = [
        pltpu.make_async_copy(inputs[n], local[n], in_sem.at[n]) for n in range(n_in)
    ]
    for fetch in fetches:
        fetch.start()

    def exists(direction):
        dx, dy = direction
        ok = None
        for pos, size, step in ((my_x, size_x, dx), (my_y, size_y, dy)):
            if step:
                cond = pos > 0 if step < 0 else pos < size - 1
                ok = cond if ok is None else jnp.logical_and(ok, cond)
        return ok

    def for_all_peers(act):
        def column(offset_y, first_x):
            other_y = my_y + offset_y
            other_y = jnp.where(other_y >= size_y, other_y - size_y, other_y)
            for offset_x in range(first_x, size_x):
                other_x = my_x + offset_x
                other_x = jnp.where(other_x >= size_x, other_x - size_x, other_x)
                act((other_x, other_y))

        if devices > 64:
            @pl.loop(1, size_y)
            def _(offset_y):
                column(offset_y, 0)
        else:
            for offset_y in range(size_y - 1, 0, -1):
                column(offset_y, 0)
        column(0, 1)

    barrier = pltpu.get_barrier_semaphore()

    for_all_peers(
        lambda other: pl.semaphore_signal(
            barrier, inc=1, device_id=other, device_id_type=MESH
        )
    )

    def node_rows(step):
        return 0 if step < 0 else 7

    def source(direction):
        dx, dy = direction
        if dy == 0:
            return out.at[node_rows(dx)]
        ys = pl.ds(8 * node_rows(dy), 8)
        if dx == 0:
            return out.at[:, ys]
        return out.at[node_rows(dx), ys]

    def landing(turn, index):
        if index < 2:
            return rx.at[turn, index]
        if index < 4:
            return ry.at[turn, index - 2]
        return re.at[turn, index - 4]

    def halo_copy(turn, index):
        direction = DIRS[index]
        opposite = DIRS.index((-direction[0], -direction[1]))
        return pltpu.make_async_remote_copy(
            src_ref=source(direction),
            dst_ref=landing(turn, opposite),
            send_sem=halo_send.at[turn, index],
            recv_sem=halo_recv.at[turn, opposite],
            device_id=(my_x + direction[0], my_y + direction[1]),
            device_id_type=MESH,
        )

    def halo_arrival(turn, index):
        direction = DIRS[index]
        return pltpu.make_async_remote_copy(
            src_ref=source(direction),
            dst_ref=landing(turn, index),
            send_sem=halo_send.at[turn, index],
            recv_sem=halo_recv.at[turn, index],
            device_id=(my_x + direction[0], my_y + direction[1]),
            device_id_type=MESH,
        )

    lane = lax.broadcasted_iota(jnp.int32, (8, 8, lanes), 2)

    def sum_depth(raw):
        out[...] = raw
        head = out[:, pl.ds(0, 8, stride=8), :]
        tail = out[:, pl.ds(7, 8, stride=8), :]
        from_tail = pltpu.roll(tail.reshape(64, lanes), 1, 1).reshape(8, 8, lanes)
        from_head = pltpu.roll(head.reshape(64, lanes), lanes - 1, 1).reshape(8, 8, lanes)
        out[:, pl.ds(0, 8, stride=8), :] = jnp.where(lane == 0, 0.0, head + from_tail)
        out[:, pl.ds(7, 8, stride=8), :] = jnp.where(lane == lanes - 1, 0.0, tail + from_head)

    def send_halo(turn):
        for index in range(8):
            @pl.when(exists(DIRS[index]))
            def _(index=index):
                halo_copy(turn, index).start()

    def take_halo(turn, target):
        for index in range(8):
            @pl.when(exists(DIRS[index]))
            def _(index=index):
                halo_copy(turn, index).wait_send()
                halo_arrival(turn, index).wait_recv()

        has = [exists(direction) for direction in DIRS[:4]]
        target[pl.ds(1, 6), pl.ds(8, 48)] = out[pl.ds(1, 6), pl.ds(8, 48)]
        for side in range(2):
            i = 7 * side
            target[i, pl.ds(8, 48)] = jnp.where(
                has[side], out[i, pl.ds(8, 48)] + rx[turn, side, pl.ds(8, 48)], 0.0
            )
            target[pl.ds(1, 6), pl.ds(8 * i, 8)] = jnp.where(
                has[2 + side],
                out[pl.ds(1, 6), pl.ds(8 * i, 8)] + ry[turn, side, pl.ds(1, 6)],
                0.0,
            )
            for other in range(2):
                j = 7 * other
                target[i, pl.ds(8 * j, 8)] = jnp.where(
                    jnp.logical_and(has[side], has[2 + other]),
                    (out[i, pl.ds(8 * j, 8)] + rx[turn, side, pl.ds(8 * j, 8)])
                    + (ry[turn, other, i] + re[turn, 2 * side + other]),
                    0.0,
                )

    def send_all(turn, value):
        message_ref[turn] = value
        got[turn, me] = value

        def send(other):
            pltpu.make_async_remote_copy(
                src_ref=message_ref.at[turn],
                dst_ref=got.at[turn, me],
                send_sem=all_send.at[turn],
                recv_sem=all_recv.at[turn],
                device_id=other,
                device_id_type=MESH,
            ).start()

        for_all_peers(send)

    def take_all(turn):
        span = got.at[turn, pl.ds(0, devices - 1)]
        copy = pltpu.make_async_remote_copy(
            src_ref=span,
            dst_ref=span,
            send_sem=all_send.at[turn],
            recv_sem=all_recv.at[turn],
            device_id=(jnp.where(my_x == 0, 1, 0), my_y),
            device_id_type=MESH,
        )
        copy.wait_send()
        copy.wait_recv()
        return got[turn]

    row = lax.broadcasted_iota(jnp.int32, (8, lanes), 0)
    row4 = lax.broadcasted_iota(jnp.int32, (4, lanes), 0)
    lane4 = lax.broadcasted_iota(jnp.int32, (4, lanes), 1)

    def corner_message(raw):
        corners = both_dot(corner_ref[...], raw)
        moved = pltpu.roll(pltpu.roll(corners, 1, 1), 4, 0)
        return (corners + moved)[:4]

    def coarse_values(turn):
        gathered = take_all(turn).reshape(devices * 4, lanes)
        combined = both_dot(gather_ref[...], gathered)
        spectral = both_dot(combined, sine_ref[...]) * inverse_ref[...]
        mine = both_dot(back_ref[me], spectral)
        columns = both_dot(mine, sine_ref[...])
        corners = jnp.where(row < 4, columns, pltpu.roll(columns, lanes - 1, 1))
        return both_dot(corner_ref[...].T, corners), combined

    def local_solve(field):
        return split_dot(solve_ref[...], field).reshape(8, 64, lanes)

    def stiffness(field_ref, target):
        values = field_ref[...] - field_ref[:, pl.ds(27, 1)]
        grads = wide_dot(
            forward_ref[...],
            jnp.concatenate(
                [values[:4].reshape(256, lanes), values[4:].reshape(256, lanes)], axis=1
            ),
        )
        factor = jnp.concatenate(
            [cw[pl.ds(0, 4)].reshape(256, lanes), cw[pl.ds(4, 4)].reshape(256, lanes)], axis=1
        )
        flux = jnp.concatenate([grads[:256] * factor, grads[256:] * factor], axis=0)
        result = wide_dot(backward_ref[...], flux)
        target[pl.ds(0, 4)] = result[:, :lanes].reshape(4, 64, lanes)
        target[pl.ds(4, 4)] = result[:, lanes:].reshape(4, 64, lanes)
        for part in range(8):
            span = pl.ds(8 * part, 8)
            values = [field_ref[i, span] for i in range(8)]
            flux = []
            for p in range(8):
                grad = values[0] * derivative[p][0]
                for i in range(1, 8):
                    grad = grad + values[i] * derivative[p][i]
                flux.append(grad * cw[p, span])
            for i in range(8):
                total = target[i, span]
                for p in range(8):
                    total = total + flux[p] * derivative[p][i]
                target[i, span] = total

    def partial(left, right):
        return jnp.sum((left * right).reshape(64, 8, lanes), axis=0)

    def row_sum(tile):
        return jnp.sum(tile, axis=0, keepdims=True)

    def total(rows):
        return jnp.sum(rows, axis=(0, 1), keepdims=True)

    fetches[0].wait()
    sum_depth(f_ref[...])
    pl.semaphore_wait(barrier, devices - 1)
    send_halo(0)
    fetches[1].wait()
    send_all(0, corner_message(f_ref[...].reshape(512, lanes)))
    fetches[2].wait()
    fetches[3].wait()
    for i in range(8):
        cw[i] = coef_ref[i] * (weight_ref[...] * weights[i])
    for fetch in fetches[4:]:
        fetch.wait()
    take_halo(0, base)

    sum_depth(local_solve(base[...].reshape(512, lanes)))
    send_halo(1)
    coarse, _ = coarse_values(0)
    take_halo(1, first)
    first[...] += coarse.reshape(8, 64, lanes)

    stiffness(first, alpha)
    sum_depth(alpha[...])
    send_halo(2)
    message = corner_message(alpha[...].reshape(512, lanes))
    energy = total(partial(f_ref[...], first[...]))
    curve = total(partial(alpha[...], first[...]))
    message = jnp.where(
        lane4 == 0, jnp.where(row4 == 0, energy, jnp.where(row4 == 1, curve, 0.0)), message
    )
    send_all(1, message)
    take_halo(2, image)

    sum_depth(local_solve(image[...].reshape(512, lanes)))
    send_halo(3)
    coarse, combined = coarse_values(1)
    energy = combined[modes : modes + 1, 0:1]
    curve = combined[modes + 1 : modes + 2, 0:1]
    step = energy / curve
    take_halo(3, smooth)
    step3 = step.reshape(1, 1, 1)
    second[...] = first[...] - step3 * (smooth[...] + coarse.reshape(8, 64, lanes))

    fresh = row_sum(partial(f_ref[...] - step3 * alpha[...], second[...]))
    cross = row_sum(partial(alpha[...], second[...]))
    stiffness(second, beta_raw)
    sum_depth(beta_raw[...])
    send_halo(4)
    along = row_sum(partial(beta_raw[...], second[...]))
    send_all(
        2,
        jnp.where(
            row4 == 0, fresh, jnp.where(row4 == 1, along, jnp.where(row4 == 2, cross, 0.0))
        ),
    )
    take_halo(4, smooth)
    sums = jnp.sum(take_all(2), axis=0)
    fresh = total(sums[0:1])
    ratio = fresh / energy
    along = total(sums[1:2]) + 2.0 * ratio * total(sums[2:3]) + ratio * ratio * curve
    second_step = fresh / along
    ratio3 = ratio.reshape(1, 1, 1)
    second3 = second_step.reshape(1, 1, 1)
    p_ref[...] = step3 * first[...] + second3 * (second[...] + ratio3 * first[...])
    r_ref[...] = (base[...] - step3 * image[...]) - second3 * (smooth[...] + ratio3 * image[...])


def solution(mesh):
    size_x, size_y = mesh.shape["gx"], mesh.shape["gy"]
    devices = size_x * size_y
    weights, derivative, solve, forward, backward, corner = element_tables()
    spec = P(None, None, None, "gx", "gy", None)

    def on_device(forcing, coefficient):
        shape = forcing.shape
        depth = shape[5]
        gather, inverse, back, sine = coarse_tables(size_x, size_y, depth)
        modes = (size_x - 1) * (size_y - 1)
        plane = np.outer(weights, weights).reshape(64, 1) * np.ones((1, depth))
        single = [
            np.asarray(table, np.float32)
            for table in (corner, plane, gather, sine, inverse, back)
        ]
        field = (8, 64, depth)
        operands = [
            forcing.reshape(field), single[0], coefficient.reshape(field), single[1],
            halves(solve), *single[2:], pieces(forward, 3), pieces(backward, 2),
        ]
        vmem = pl.BlockSpec(memory_space=pltpu.VMEM)
        pressure, residual = pl.pallas_call(
            functools.partial(
                kernel, size_x, size_y, weights.tolist(), derivative.tolist(), modes
            ),
            out_shape=[jax.ShapeDtypeStruct(field, jnp.float32)] * 2,
            in_specs=[pl.BlockSpec(memory_space=pltpu.HBM)] * len(operands),
            out_specs=[vmem, vmem],
            scratch_shapes=[pltpu.VMEM(op.shape, op.dtype) for op in operands]
            + [pltpu.VMEM(field, jnp.float32)] * 9
            + [
                pltpu.VMEM((5, 2, 64, depth), jnp.float32),
                pltpu.VMEM((5, 2, 8, 8, depth), jnp.float32),
                pltpu.VMEM((5, 4, 8, depth), jnp.float32),
                pltpu.VMEM((3, 4, depth), jnp.float32),
                pltpu.VMEM((3, devices, 4, depth), jnp.float32),
                pltpu.SemaphoreType.DMA((len(operands),)),
                pltpu.SemaphoreType.DMA((5, 8)),
                pltpu.SemaphoreType.DMA((5, 8)),
                pltpu.SemaphoreType.DMA((3,)),
                pltpu.SemaphoreType.DMA((3,)),
            ],
            compiler_params=pltpu.CompilerParams(
                collective_id=0, has_side_effects=True, vmem_limit_bytes=60 * 1024 * 1024
            ),
        )(*operands)
        anywhere = pl.BlockSpec(memory_space=pltpu.HBM)
        pressure, residual = pl.pallas_call(
            copy_kernel,
            out_shape=[jax.ShapeDtypeStruct(field, jnp.float32)] * 2,
            in_specs=[anywhere, anywhere],
            out_specs=[anywhere, anywhere],
            scratch_shapes=[pltpu.SemaphoreType.DMA((4,))],
            compiler_params=pltpu.CompilerParams(vmem_limit_bytes=60 * 1024 * 1024),
        )(pressure, residual)
        return pressure.reshape(shape), residual.reshape(shape)

    return jax.shard_map(
        on_device, mesh=mesh, in_specs=(spec, spec), out_specs=(spec, spec), check_vma=False
    )
```

```python
import functools
import math

import jax
import jax.numpy as jnp
import numpy as np
from jax import lax
from jax.experimental import pallas as pl
from jax.experimental.pallas import tpu as pltpu
from jax.sharding import PartitionSpec as P

MESH = pl.DeviceIdType.MESH
stretch = (1.0, 64.0, 1.0)
DIRS = ((-1, 0), (1, 0), (0, -1), (0, 1), (-1, -1), (-1, 1), (1, -1), (1, 1))


def legendre_value(order, position):
    prev_value = 1.0
    this_value = position
    for degree_now in range(2, order + 1):
        next_value = (
            (2 * degree_now - 1) * position * this_value - (degree_now - 1) * prev_value
        ) / degree_now
        prev_value = this_value
        this_value = next_value
    return this_value


def gll_points():
    points = [-1.0]
    for node_index in range(1, 7):
        position = -math.cos(math.pi * node_index / 7.0)
        for newton_step in range(60):
            target = legendre_value(8, position) - legendre_value(6, position)
            slope = 15.0 * legendre_value(7, position)
            position = position - target / slope
        points.append(position)
    points.append(1.0)
    return points


def jacobi_eigen(matrix_in):
    order_n = len(matrix_in)
    work_mat = [list(one_row) for one_row in matrix_in]
    vectors = [
        [1.0 if row_index == col_index else 0.0 for col_index in range(order_n)]
        for row_index in range(order_n)
    ]
    for sweep_index in range(40):
        for first_idx in range(order_n):
            for second_idx in range(first_idx + 1, order_n):
                rotation = 0.5 * math.atan2(
                    2.0 * work_mat[first_idx][second_idx],
                    work_mat[second_idx][second_idx] - work_mat[first_idx][first_idx],
                )
                cosine = math.cos(rotation)
                sine_part = math.sin(rotation)
                for other in range(order_n):
                    left_val = work_mat[other][first_idx]
                    right_val = work_mat[other][second_idx]
                    work_mat[other][first_idx] = cosine * left_val - sine_part * right_val
                    work_mat[other][second_idx] = sine_part * left_val + cosine * right_val
                for other in range(order_n):
                    left_val = work_mat[first_idx][other]
                    right_val = work_mat[second_idx][other]
                    work_mat[first_idx][other] = cosine * left_val - sine_part * right_val
                    work_mat[second_idx][other] = sine_part * left_val + cosine * right_val
                for other in range(order_n):
                    left_val = vectors[other][first_idx]
                    right_val = vectors[other][second_idx]
                    vectors[other][first_idx] = cosine * left_val - sine_part * right_val
                    vectors[other][second_idx] = sine_part * left_val + cosine * right_val
    return ([work_mat[diag_index][diag_index] for diag_index in range(order_n)], vectors)


def spectral_tables():
    nodes = gll_points()
    values_at = [legendre_value(7, position) for position in nodes]
    weights = [2.0 / (56.0 * value_now * value_now) for value_now in values_at]
    derivative = np.zeros((8, 8))
    for row in range(8):
        for col in range(8):
            if row != col:
                derivative[row, col] = values_at[row] / (
                    values_at[col] * (nodes[row] - nodes[col])
                )
    derivative[0, 0] = -14.0
    derivative[7, 7] = 14.0
    weights = np.array(weights)
    stiffness = derivative.T @ np.diag(weights) @ derivative
    stiffness[0, 0] *= 2.0
    stiffness[7, 7] *= 2.0
    inv_root = 1.0 / np.sqrt(weights)
    symmetric = inv_root[:, None] * stiffness * inv_root[None, :]
    eigen_values, eigen_vectors = jacobi_eigen(symmetric.tolist())
    fdm_basis = inv_root[:, None] * np.array(eigen_vectors)
    nodes = np.array(nodes)
    hats = np.stack([(1.0 - nodes) / 2.0, (1.0 + nodes) / 2.0])
    return weights, derivative, fdm_basis, np.array(eigen_values), hats


def sine_table(cells):
    ids = np.arange(cells + 1)
    table = math.sqrt(2.0 / cells) * np.sin(math.pi * (np.outer(ids, ids) % (2 * cells)) / cells)
    table[0] = table[-1] = 0.0
    table[:, 0] = table[:, -1] = 0.0
    return table


def mode_values(cells):
    cosines = np.cos(math.pi * np.arange(1, cells) / cells)
    return (2.0 - 2.0 * cosines) / 2.0, 2.0 * (4.0 + 2.0 * cosines) / 6.0


def round_up(value, step):
    return -(-value // step) * step


def halves(table):
    table = np.asarray(table, np.float32)
    high = table.astype(jnp.bfloat16)
    low = (table - high.astype(np.float32)).astype(jnp.bfloat16)
    return np.concatenate([high, low], axis=0)


def pieces(table, count):
    table = np.asarray(table, np.float32)
    found = []
    for _ in range(count):
        found.append(table.astype(jnp.bfloat16))
        table = table - found[-1].astype(np.float32)
    return np.concatenate(found + [found[0]], axis=1)


def sixfold(table, axis):
    table = np.asarray(table, np.float32)
    found = []
    for _ in range(3):
        found.append(table.astype(jnp.bfloat16))
        table = table - found[-1].astype(np.float32)
    return np.concatenate([found[n] for n in (0, 1, 2, 0, 1, 0)], axis=axis)


def element_tables():
    weights, derivative, basis, eigen, hats = spectral_tables()
    eye = np.eye(8)
    cube = np.kron(np.kron(basis, basis), basis)
    total = (
        stretch[0] * eigen[:, None, None]
        + stretch[1] * eigen[None, :, None]
        + stretch[2] * eigen[None, None, :]
    ).reshape(-1)
    solve = (cube / total) @ cube.T
    along_j = np.kron(np.eye(4), np.kron(derivative, eye))
    along_k = np.kron(np.eye(4), np.kron(eye, derivative))
    forward = np.concatenate([along_j, along_k], axis=0)
    backward = np.concatenate([stretch[1] * along_j.T, stretch[2] * along_k.T], axis=1)
    corner = np.stack(
        [
            np.kron(np.kron(hats[a], hats[b]), hats[c])
            for c in range(2)
            for a in range(2)
            for b in range(2)
        ]
    )
    return weights, derivative, solve, forward, backward, corner


def coarse_tables(size_x, size_y, depth):
    sine_x, sine_y, sine_z = sine_table(size_x), sine_table(size_y), sine_table(depth)
    modes = (size_x - 1) * (size_y - 1)
    rows = round_up(modes + 2, 8)
    waves_y = size_y - 1
    rows_y = round_up(2 * waves_y + 2, 8)
    along_y = np.zeros((rows_y, size_y, 4))
    along_x = np.zeros((rows, size_x, rows_y))
    for a in range(2):
        for y in range(size_y):
            for b in range(2):
                along_y[a : 2 * waves_y : 2, y, 2 * a + b] = sine_y[1:-1, y + b]
        for x in range(size_x):
            for n in range(waves_y):
                along_x[n : modes : waves_y, x, 2 * n + a] = sine_x[1:-1, x + a]
    for q in range(2):
        along_y[2 * waves_y + q, :, q] = 1.0
        along_x[modes + q, :, 2 * waves_y + q] = 1.0
    stiff_x, mass_x = mode_values(size_x)
    stiff_y, mass_y = mode_values(size_y)
    stiff_z, mass_z = mode_values(depth)
    denominator = (
        stretch[0] * stiff_x[:, None, None] * mass_y[None, :, None] * mass_z[None, None, :]
        + stretch[1] * mass_x[:, None, None] * stiff_y[None, :, None] * mass_z[None, None, :]
        + stretch[2] * mass_x[:, None, None] * mass_y[None, :, None] * stiff_z[None, None, :]
    )
    inverse = np.zeros((rows, depth))
    inverse[:modes, 1:] = (1.0 / denominator).reshape(modes, depth - 1)
    back = np.zeros((size_x, size_y, 16, rows))
    for x in range(size_x):
        for y in range(size_y):
            for c in range(2):
                for a in range(2):
                    for b in range(2):
                        back[x, y, 4 * c + 2 * a + b, :modes] = np.outer(
                            sine_x[1:-1, x + a], sine_y[1:-1, y + b]
                        ).reshape(-1)
    return (
        along_y.reshape(rows_y, -1),
        along_x.reshape(rows, -1),
        inverse,
        back.reshape(size_x * size_y, 16, rows),
        sine_z[:depth, :depth],
    )


def parts(field):
    high = field.astype(jnp.bfloat16)
    return high, (field - high.astype(jnp.float32)).astype(jnp.bfloat16)


def both_dot(left, right):
    rows, lanes = left.shape[0], right.shape[1]
    sums = jnp.dot(
        jnp.concatenate(parts(left), axis=0),
        jnp.concatenate(parts(right), axis=1),
        preferred_element_type=jnp.float32,
    )
    return (sums[:rows, :lanes] + sums[rows:, :lanes]) + (sums[:rows, lanes:] + sums[rows:, lanes:])


def split_dot(table, field):
    lanes = field.shape[1]
    rows = table.shape[0] // 2
    high = field.astype(jnp.bfloat16)
    low = (field - high.astype(jnp.float32)).astype(jnp.bfloat16)
    both = jnp.concatenate([high, low], axis=1)
    top = jnp.dot(table[:rows], both, preferred_element_type=jnp.float32)
    bottom = jnp.dot(table[rows:], both, preferred_element_type=jnp.float32)
    return (top[:, :lanes] + bottom[:, :lanes]) + (top[:, lanes:] + bottom[:, lanes:])


def six_parts(value, axis):
    found = []
    for _ in range(3):
        found.append(value.astype(jnp.bfloat16).astype(jnp.float32))
        value = value - found[-1]
    order = [found[n] for n in (0, 0, 0, 1, 1, 2)]
    return jnp.concatenate(order, axis=axis).astype(jnp.bfloat16)


def table_dot(table, value):
    return jnp.dot(table, six_parts(value, 0), preferred_element_type=jnp.float32)


def dot_table(value, table):
    return jnp.dot(six_parts(value, 1), table, preferred_element_type=jnp.float32)


def wide_dot(table, field):
    high, low = parts(field)
    pieces = table.shape[1] // field.shape[0]
    return jnp.dot(
        table,
        jnp.concatenate([high] * (pieces - 1) + [low], axis=0),
        preferred_element_type=jnp.float32,
    )


def copy_kernel(p_in, r_in, p_out, r_out):
    p_out[...] = p_in[...]
    r_out[...] = r_in[...]


def kernel(size_x, size_y, weights, derivative, modes, *refs):
    n_in = 13
    inputs, (p_ref, r_ref) = refs[:n_in], refs[n_in : n_in + 2]
    local = refs[n_in + 2 : 2 * n_in + 2]
    (
        cw, out, base, first, second, image, alpha, beta_raw, smooth, flux_i,
        rx, ry, re, mine_y, got_y, mine_x, got_x, mine_s, got_s,
        in_sem, halo_send, halo_recv, y_send, y_recv, x_send, x_recv,
    ) = refs[2 * n_in + 2 :]
    (
        f_ref, corner_ref, coef_ref, weight_ref, solve_ref,
        forward_ref, backward_ref,
        along_y_ref, along_x_ref, sine_ref, inverse_ref, back_ref, spread_ref,
    ) = local
    lanes = f_ref.shape[2]
    my_x = lax.axis_index("gx")
    my_y = lax.axis_index("gy")
    me = my_x * size_y + my_y

    fetches = [
        pltpu.make_async_copy(
            inputs[n].at[me] if local[n] is back_ref else inputs[n], local[n], in_sem.at[n]
        )
        for n in range(n_in)
    ]
    for fetch in fetches:
        fetch.start()

    def exists(direction):
        dx, dy = direction
        ok = None
        for pos, size, step in ((my_x, size_x, dx), (my_y, size_y, dy)):
            if step:
                cond = pos > 0 if step < 0 else pos < size - 1
                ok = cond if ok is None else jnp.logical_and(ok, cond)
        return ok

    def peers_y():
        for offset in range(1, size_y):
            other = my_y + offset
            yield (my_x, jnp.where(other >= size_y, other - size_y, other))

    def peers_x():
        for offset in range(1, size_x):
            other = my_x + offset
            yield (jnp.where(other >= size_x, other - size_x, other), my_y)

    barrier = pltpu.get_barrier_semaphore()
    count = jnp.int32(size_x - 1 + size_y - 1)
    for direction in DIRS[4:]:
        here = exists(direction)

        @pl.when(here)
        def _(direction=direction):
            pl.semaphore_signal(
                barrier,
                inc=1,
                device_id=(my_x + direction[0], my_y + direction[1]),
                device_id_type=MESH,
            )

        count = count + here.astype(jnp.int32)
    for other in [*peers_y(), *peers_x()]:
        pl.semaphore_signal(barrier, inc=1, device_id=other, device_id_type=MESH)

    def node_rows(step):
        return 0 if step < 0 else 7

    def source(direction):
        dx, dy = direction
        if dy == 0:
            return out.at[node_rows(dx)]
        ys = pl.ds(8 * node_rows(dy), 8)
        if dx == 0:
            return out.at[:, ys]
        return out.at[node_rows(dx), ys]

    def landing(turn, index):
        if index < 2:
            return rx.at[turn, index]
        if index < 4:
            return ry.at[turn, index - 2]
        return re.at[turn, index - 4]

    def halo_copy(turn, index):
        direction = DIRS[index]
        opposite = DIRS.index((-direction[0], -direction[1]))
        return pltpu.make_async_remote_copy(
            src_ref=source(direction),
            dst_ref=landing(turn, opposite),
            send_sem=halo_send.at[turn, index],
            recv_sem=halo_recv.at[turn, opposite],
            device_id=(my_x + direction[0], my_y + direction[1]),
            device_id_type=MESH,
        )

    def halo_arrival(turn, index):
        direction = DIRS[index]
        return pltpu.make_async_remote_copy(
            src_ref=source(direction),
            dst_ref=landing(turn, index),
            send_sem=halo_send.at[turn, index],
            recv_sem=halo_recv.at[turn, index],
            device_id=(my_x + direction[0], my_y + direction[1]),
            device_id_type=MESH,
        )

    lane = lax.broadcasted_iota(jnp.int32, (8, 8, lanes), 2)

    def sum_depth(raw):
        out[...] = raw
        head = out[:, pl.ds(0, 8, stride=8), :]
        tail = out[:, pl.ds(7, 8, stride=8), :]
        from_tail = pltpu.roll(tail.reshape(64, lanes), 1, 1).reshape(8, 8, lanes)
        from_head = pltpu.roll(head.reshape(64, lanes), lanes - 1, 1).reshape(8, 8, lanes)
        out[:, pl.ds(0, 8, stride=8), :] = jnp.where(lane == 0, 0.0, head + from_tail)
        out[:, pl.ds(7, 8, stride=8), :] = jnp.where(lane == lanes - 1, 0.0, tail + from_head)

    def send_halo(turn):
        for index in (2, 3, 4, 5, 6, 7, 0, 1):
            @pl.when(exists(DIRS[index]))
            def _(index=index):
                halo_copy(turn, index).start()

    def take_halo(turn, target):
        for index in range(8):
            @pl.when(exists(DIRS[index]))
            def _(index=index):
                halo_copy(turn, index).wait_send()
                halo_arrival(turn, index).wait_recv()

        has = [exists(direction) for direction in DIRS[:4]]
        target[pl.ds(1, 6), pl.ds(8, 48)] = out[pl.ds(1, 6), pl.ds(8, 48)]
        for side in range(2):
            i = 7 * side
            target[i, pl.ds(8, 48)] = jnp.where(
                has[side], out[i, pl.ds(8, 48)] + rx[turn, side, pl.ds(8, 48)], 0.0
            )
            target[pl.ds(1, 6), pl.ds(8 * i, 8)] = jnp.where(
                has[2 + side],
                out[pl.ds(1, 6), pl.ds(8 * i, 8)] + ry[turn, side, pl.ds(1, 6)],
                0.0,
            )
            for other in range(2):
                j = 7 * other
                target[i, pl.ds(8 * j, 8)] = jnp.where(
                    jnp.logical_and(has[side], has[2 + other]),
                    (out[i, pl.ds(8 * j, 8)] + rx[turn, side, pl.ds(8 * j, 8)])
                    + (ry[turn, other, i] + re[turn, 2 * side + other]),
                    0.0,
                )

    def send_to(peers, me_there, message, got, send, recv, value):
        message[...] = value
        got[me_there] = value
        for other in peers:
            pltpu.make_async_remote_copy(
                src_ref=message,
                dst_ref=got.at[me_there],
                send_sem=send,
                recv_sem=recv,
                device_id=other,
                device_id_type=MESH,
            ).start()

    def take_from(size, got, send, recv):
        span = got.at[pl.ds(0, size - 1)]
        copy = pltpu.make_async_remote_copy(
            src_ref=span,
            dst_ref=span,
            send_sem=send,
            recv_sem=recv,
            device_id=(jnp.where(my_x == 0, 1, 0), my_y),
            device_id_type=MESH,
        )
        copy.wait_send()
        copy.wait_recv()
        return got[...]

    def send_y(turn, value):
        send_to(
            peers_y(), my_y, mine_y.at[turn], got_y.at[turn],
            y_send.at[turn], y_recv.at[turn], value,
        )

    def take_y(turn):
        return take_from(size_y, got_y.at[turn], y_send.at[turn], y_recv.at[turn])

    def send_x(turn, value):
        mine, got = (mine_s, got_s) if turn == 2 else (mine_x.at[turn], got_x.at[turn])
        send_to(peers_x(), my_x, mine, got, x_send.at[turn], x_recv.at[turn], value)

    def take_x(turn):
        got = got_s if turn == 2 else got_x.at[turn]
        return take_from(size_x, got, x_send.at[turn], x_recv.at[turn])

    def pass_on(turn):
        send_x(turn, table_dot(along_y_ref[...], take_y(turn).reshape(size_y * 4, lanes)))

    row = lax.broadcasted_iota(jnp.int32, (8, lanes), 0)
    row4 = lax.broadcasted_iota(jnp.int32, (4, lanes), 0)
    lane4 = lax.broadcasted_iota(jnp.int32, (4, lanes), 1)

    def corner_message(raw):
        corners = both_dot(corner_ref[...], raw)
        moved = pltpu.roll(pltpu.roll(corners, 1, 1), 4, 0)
        return (corners + moved)[:4]

    def coarse_values(turn):
        gathered = take_x(turn)
        gathered = gathered.reshape(size_x * gathered.shape[1], lanes)
        combined = table_dot(along_x_ref[...], gathered)
        spectral = dot_table(combined, sine_ref[...]) * inverse_ref[...]
        mine = table_dot(back_ref[...], spectral)[:8]
        columns = dot_table(mine, sine_ref[...])
        corners = jnp.where(row < 4, columns, pltpu.roll(columns, lanes - 1, 1))
        return table_dot(spread_ref[...], corners), combined

    def local_solve(field):
        return split_dot(solve_ref[...], field).reshape(8, 64, lanes)

    def fluxes(field_ref):
        values = field_ref[...] - field_ref[:, pl.ds(27, 1)]
        grads = wide_dot(
            forward_ref[...],
            jnp.concatenate(
                [values[:4].reshape(256, lanes), values[4:].reshape(256, lanes)], axis=1
            ),
        )
        factor = jnp.concatenate(
            [cw[pl.ds(0, 4)].reshape(256, lanes), cw[pl.ds(4, 4)].reshape(256, lanes)], axis=1
        )
        grads_j, grads_k = grads[:256], grads[256:]
        flux_j, flux_k = grads_j * factor, grads_k * factor
        energy = stretch[1] * (grads_j * flux_j) + stretch[2] * (grads_k * flux_k)
        energy = jnp.sum(energy.reshape(32, 8, 2 * lanes), axis=0)
        energy = energy[:, :lanes] + energy[:, lanes:]
        for part in range(8):
            span = pl.ds(8 * part, 8)
            nodal = [field_ref[i, span] for i in range(8)]
            for p in range(8):
                grad = nodal[0] * derivative[p][0]
                for i in range(1, 8):
                    grad = grad + nodal[i] * derivative[p][i]
                flux = grad * cw[p, span]
                flux_i[p, span] = flux
                energy = energy + grad * flux
        return jnp.concatenate([flux_j, flux_k], axis=0), energy

    def divergence(flux, target):
        result = wide_dot(backward_ref[...], flux)
        for part in range(8):
            span = pl.ds(8 * part, 8)
            flux = [flux_i[p, span] for p in range(8)]
            for i in range(8):
                first_row = 64 * (i % 4) + 8 * part
                first_lane = lanes * (i // 4)
                total = result[first_row : first_row + 8, first_lane : first_lane + lanes]
                for p in range(8):
                    total = total + flux[p] * derivative[p][i]
                target[i, span] = total

    def partial(left, right):
        return jnp.sum((left * right).reshape(64, 8, lanes), axis=0)

    def row_sum(tile):
        return jnp.sum(tile, axis=0, keepdims=True)

    def total(rows):
        return jnp.sum(rows, axis=(0, 1), keepdims=True)

    fetches[0].wait()
    sum_depth(f_ref[...])
    pl.semaphore_wait(barrier, count)
    send_halo(0)
    fetches[1].wait()
    send_y(0, corner_message(f_ref[...].reshape(512, lanes)))
    fetches[2].wait()
    fetches[3].wait()
    for i in range(8):
        cw[i] = coef_ref[i] * (weight_ref[...] * weights[i])
    fetches[4].wait()
    take_halo(0, base)
    for fetch in fetches[5:]:
        fetch.wait()

    sum_depth(local_solve(base[...].reshape(512, lanes)))
    send_halo(1)
    pass_on(0)
    coarse, _ = coarse_values(0)
    take_halo(1, first)
    first[...] += coarse.reshape(8, 64, lanes)

    flux, curve = fluxes(first)
    divergence(flux, alpha)
    sum_depth(alpha[...])
    send_halo(2)
    message = corner_message(alpha[...].reshape(512, lanes))
    energy = total(partial(f_ref[...], first[...]))
    curve = total(curve)
    message = jnp.where(
        lane4 == 0, jnp.where(row4 == 0, energy, jnp.where(row4 == 1, curve, 0.0)), message
    )
    send_y(1, message)
    take_halo(2, image)

    sum_depth(local_solve(image[...].reshape(512, lanes)))
    send_halo(3)
    pass_on(1)
    coarse, combined = coarse_values(1)
    energy = combined[modes : modes + 1, 0:1]
    curve = combined[modes + 1 : modes + 2, 0:1]
    step = energy / curve
    take_halo(3, smooth)
    step3 = step.reshape(1, 1, 1)
    second[...] = first[...] - step3 * (smooth[...] + coarse.reshape(8, 64, lanes))

    fresh = row_sum(partial(f_ref[...] - step3 * alpha[...], second[...]))
    cross = row_sum(partial(alpha[...], second[...]))
    flux, along = fluxes(second)
    along = row_sum(along)
    send_y(
        2,
        jnp.where(
            row4 == 0, fresh, jnp.where(row4 == 1, along, jnp.where(row4 == 2, cross, 0.0))
        ),
    )
    divergence(flux, beta_raw)
    sum_depth(beta_raw[...])
    send_halo(4)
    send_x(2, jnp.sum(take_y(2), axis=0))
    take_halo(4, smooth)
    sums = jnp.sum(take_x(2), axis=0)
    fresh = total(sums[0:1])
    ratio = fresh / energy
    along = total(sums[1:2]) + 2.0 * ratio * total(sums[2:3]) + ratio * ratio * curve
    second_step = fresh / along
    ratio3 = ratio.reshape(1, 1, 1)
    second3 = second_step.reshape(1, 1, 1)
    p_ref[...] = step3 * first[...] + second3 * (second[...] + ratio3 * first[...])
    r_ref[...] = (base[...] - step3 * image[...]) - second3 * (smooth[...] + ratio3 * image[...])


def solution(mesh):
    size_x, size_y = mesh.shape["gx"], mesh.shape["gy"]
    weights, derivative, solve, forward, backward, corner = element_tables()
    spec = P(None, None, None, "gx", "gy", None)

    def on_device(forcing, coefficient):
        shape = forcing.shape
        depth = shape[5]
        along_y, along_x, inverse, back, sine = coarse_tables(size_x, size_y, depth)
        modes = (size_x - 1) * (size_y - 1)
        plane = np.outer(weights, weights).reshape(64, 1) * np.ones((1, depth))
        field = (8, 64, depth)
        operands = [
            forcing.reshape(field),
            np.asarray(corner, np.float32),
            coefficient.reshape(field),
            np.asarray(plane, np.float32),
            halves(solve),
            pieces(forward, 3),
            pieces(backward, 2),
            sixfold(along_y, 1),
            sixfold(along_x, 1),
            sixfold(sine, 0),
            np.asarray(inverse, np.float32),
            sixfold(back, 2),
            sixfold(corner.T, 1),
        ]
        shapes = [op.shape for op in operands]
        shapes[11] = shapes[11][1:]
        rows_y = along_y.shape[0]
        vmem = pl.BlockSpec(memory_space=pltpu.VMEM)
        pressure, residual = pl.pallas_call(
            functools.partial(
                kernel, size_x, size_y, weights.tolist(), derivative.tolist(), modes
            ),
            out_shape=[jax.ShapeDtypeStruct(field, jnp.float32)] * 2,
            in_specs=[pl.BlockSpec(memory_space=pltpu.HBM)] * len(operands),
            out_specs=[vmem, vmem],
            scratch_shapes=[pltpu.VMEM(dims, op.dtype) for dims, op in zip(shapes, operands)]
            + [pltpu.VMEM(field, jnp.float32)] * 10
            + [
                pltpu.VMEM((5, 2, 64, depth), jnp.float32),
                pltpu.VMEM((5, 2, 8, 8, depth), jnp.float32),
                pltpu.VMEM((5, 4, 8, depth), jnp.float32),
                pltpu.VMEM((3, 4, depth), jnp.float32),
                pltpu.VMEM((3, size_y, 4, depth), jnp.float32),
                pltpu.VMEM((2, rows_y, depth), jnp.float32),
                pltpu.VMEM((2, size_x, rows_y, depth), jnp.float32),
                pltpu.VMEM((4, depth), jnp.float32),
                pltpu.VMEM((size_x, 4, depth), jnp.float32),
                pltpu.SemaphoreType.DMA((len(operands),)),
                pltpu.SemaphoreType.DMA((5, 8)),
                pltpu.SemaphoreType.DMA((5, 8)),
                pltpu.SemaphoreType.DMA((3,)),
                pltpu.SemaphoreType.DMA((3,)),
                pltpu.SemaphoreType.DMA((3,)),
                pltpu.SemaphoreType.DMA((3,)),
            ],
            compiler_params=pltpu.CompilerParams(
                collective_id=0, has_side_effects=True, vmem_limit_bytes=60 * 1024 * 1024
            ),
        )(*operands)
        pressure, residual = pl.pallas_call(
            copy_kernel,
            out_shape=[jax.ShapeDtypeStruct(field, jnp.float32)] * 2,
            in_specs=[vmem, vmem],
            out_specs=[vmem, vmem],
            compiler_params=pltpu.CompilerParams(vmem_limit_bytes=60 * 1024 * 1024),
        )(pressure, residual)
        return pressure.reshape(shape), residual.reshape(shape)

    return jax.shard_map(
        on_device, mesh=mesh, in_specs=(spec, spec), out_specs=(spec, spec), check_vma=False
    )
```

```python
import functools
import math

import jax
import jax.numpy as jnp
import numpy as np
from jax import lax
from jax.experimental import pallas as pl
from jax.experimental.pallas import tpu as pltpu
from jax.sharding import PartitionSpec as P

MESH = pl.DeviceIdType.MESH
stretch = (1.0, 64.0, 1.0)
DIRS = ((-1, 0), (1, 0), (0, -1), (0, 1), (-1, -1), (-1, 1), (1, -1), (1, 1))


def legendre_value(order, position):
    prev_value = 1.0
    this_value = position
    for degree_now in range(2, order + 1):
        next_value = (
            (2 * degree_now - 1) * position * this_value - (degree_now - 1) * prev_value
        ) / degree_now
        prev_value = this_value
        this_value = next_value
    return this_value


def gll_points():
    points = [-1.0]
    for node_index in range(1, 7):
        position = -math.cos(math.pi * node_index / 7.0)
        for newton_step in range(60):
            target = legendre_value(8, position) - legendre_value(6, position)
            slope = 15.0 * legendre_value(7, position)
            position = position - target / slope
        points.append(position)
    points.append(1.0)
    return points


def jacobi_eigen(matrix_in):
    order_n = len(matrix_in)
    work_mat = [list(one_row) for one_row in matrix_in]
    vectors = [
        [1.0 if row_index == col_index else 0.0 for col_index in range(order_n)]
        for row_index in range(order_n)
    ]
    for sweep_index in range(40):
        for first_idx in range(order_n):
            for second_idx in range(first_idx + 1, order_n):
                rotation = 0.5 * math.atan2(
                    2.0 * work_mat[first_idx][second_idx],
                    work_mat[second_idx][second_idx] - work_mat[first_idx][first_idx],
                )
                cosine = math.cos(rotation)
                sine_part = math.sin(rotation)
                for other in range(order_n):
                    left_val = work_mat[other][first_idx]
                    right_val = work_mat[other][second_idx]
                    work_mat[other][first_idx] = cosine * left_val - sine_part * right_val
                    work_mat[other][second_idx] = sine_part * left_val + cosine * right_val
                for other in range(order_n):
                    left_val = work_mat[first_idx][other]
                    right_val = work_mat[second_idx][other]
                    work_mat[first_idx][other] = cosine * left_val - sine_part * right_val
                    work_mat[second_idx][other] = sine_part * left_val + cosine * right_val
                for other in range(order_n):
                    left_val = vectors[other][first_idx]
                    right_val = vectors[other][second_idx]
                    vectors[other][first_idx] = cosine * left_val - sine_part * right_val
                    vectors[other][second_idx] = sine_part * left_val + cosine * right_val
    return ([work_mat[diag_index][diag_index] for diag_index in range(order_n)], vectors)


def spectral_tables():
    nodes = gll_points()
    values_at = [legendre_value(7, position) for position in nodes]
    weights = [2.0 / (56.0 * value_now * value_now) for value_now in values_at]
    derivative = np.zeros((8, 8))
    for row in range(8):
        for col in range(8):
            if row != col:
                derivative[row, col] = values_at[row] / (
                    values_at[col] * (nodes[row] - nodes[col])
                )
    derivative[0, 0] = -14.0
    derivative[7, 7] = 14.0
    weights = np.array(weights)
    stiffness = derivative.T @ np.diag(weights) @ derivative
    stiffness[0, 0] *= 2.0
    stiffness[7, 7] *= 2.0
    inv_root = 1.0 / np.sqrt(weights)
    symmetric = inv_root[:, None] * stiffness * inv_root[None, :]
    eigen_values, eigen_vectors = jacobi_eigen(symmetric.tolist())
    fdm_basis = inv_root[:, None] * np.array(eigen_vectors)
    nodes = np.array(nodes)
    hats = np.stack([(1.0 - nodes) / 2.0, (1.0 + nodes) / 2.0])
    return weights, derivative, fdm_basis, np.array(eigen_values), hats


def sine_table(cells):
    ids = np.arange(cells + 1)
    table = math.sqrt(2.0 / cells) * np.sin(math.pi * (np.outer(ids, ids) % (2 * cells)) / cells)
    table[0] = table[-1] = 0.0
    table[:, 0] = table[:, -1] = 0.0
    return table


def mode_values(cells):
    cosines = np.cos(math.pi * np.arange(1, cells) / cells)
    return (2.0 - 2.0 * cosines) / 2.0, 2.0 * (4.0 + 2.0 * cosines) / 6.0


def round_up(value, step):
    return -(-value // step) * step


def halves(table):
    table = np.asarray(table, np.float32)
    high = table.astype(jnp.bfloat16)
    low = (table - high.astype(np.float32)).astype(jnp.bfloat16)
    return np.concatenate([high, low], axis=0)


def pieces(table, count):
    table = np.asarray(table, np.float32)
    found = []
    for _ in range(count):
        found.append(table.astype(jnp.bfloat16))
        table = table - found[-1].astype(np.float32)
    return np.concatenate(found + [found[0]], axis=1)


def sixfold(table, axis):
    table = np.asarray(table, np.float32)
    found = []
    for _ in range(3):
        found.append(table.astype(jnp.bfloat16))
        table = table - found[-1].astype(np.float32)
    return np.concatenate([found[n] for n in (0, 1, 2, 0, 1, 0)], axis=axis)


def element_tables():
    weights, derivative, basis, eigen, hats = spectral_tables()
    eye = np.eye(8)
    cube = np.kron(np.kron(basis, basis), basis)
    total = (
        stretch[0] * eigen[:, None, None]
        + stretch[1] * eigen[None, :, None]
        + stretch[2] * eigen[None, None, :]
    ).reshape(-1)
    solve = (cube / total) @ cube.T
    along_j = np.kron(np.eye(4), np.kron(derivative, eye))
    along_k = np.kron(np.eye(4), np.kron(eye, derivative))
    forward = np.concatenate([along_j, along_k], axis=0)
    backward = np.concatenate([stretch[1] * along_j.T, stretch[2] * along_k.T], axis=1)
    corner = np.stack(
        [
            np.kron(np.kron(hats[a], hats[b]), hats[c])
            for c in range(2)
            for a in range(2)
            for b in range(2)
        ]
    )
    node = np.arange(512).reshape(8, 8, 8)
    faces = [node[:, 0], node[:, 7], node[0], node[7]]
    solve_faces = solve[np.stack(faces).reshape(-1)]
    solve_inner = solve[node[1:7, 1:7].reshape(-1)]
    node = node[:4]
    outer = [node[:, [0, 7]], node[[0, 3], 1:7]]
    backward_outer = backward[np.concatenate([rows.reshape(-1) for rows in outer])]
    backward_inner = backward[node[1:3, 1:7].reshape(-1)]
    return (
        weights, derivative, solve_faces, solve_inner,
        forward, backward_outer, backward_inner, corner,
    )


def coarse_tables(size_x, size_y, depth):
    sine_x, sine_y, sine_z = sine_table(size_x), sine_table(size_y), sine_table(depth)
    modes = (size_x - 1) * (size_y - 1)
    rows = round_up(modes + 2, 8)
    waves_y = size_y - 1
    rows_y = round_up(2 * waves_y + 2, 8)
    along_y = np.zeros((rows_y, size_y, 4))
    along_x = np.zeros((rows, size_x, rows_y))
    for a in range(2):
        for y in range(size_y):
            for b in range(2):
                along_y[a : 2 * waves_y : 2, y, 2 * a + b] = sine_y[1:-1, y + b]
        for x in range(size_x):
            for n in range(waves_y):
                along_x[n : modes : waves_y, x, 2 * n + a] = sine_x[1:-1, x + a]
    for q in range(2):
        along_y[2 * waves_y + q, :, q] = 1.0
        along_x[modes + q, :, 2 * waves_y + q] = 1.0
    stiff_x, mass_x = mode_values(size_x)
    stiff_y, mass_y = mode_values(size_y)
    stiff_z, mass_z = mode_values(depth)
    denominator = (
        stretch[0] * stiff_x[:, None, None] * mass_y[None, :, None] * mass_z[None, None, :]
        + stretch[1] * mass_x[:, None, None] * stiff_y[None, :, None] * mass_z[None, None, :]
        + stretch[2] * mass_x[:, None, None] * mass_y[None, :, None] * stiff_z[None, None, :]
    )
    inverse = np.zeros((rows, depth))
    inverse[:modes, 1:] = (1.0 / denominator).reshape(modes, depth - 1)
    back = np.zeros((size_x, size_y, 16, rows))
    for x in range(size_x):
        for y in range(size_y):
            for c in range(2):
                for a in range(2):
                    for b in range(2):
                        back[x, y, 4 * c + 2 * a + b, :modes] = np.outer(
                            sine_x[1:-1, x + a], sine_y[1:-1, y + b]
                        ).reshape(-1)
    return (
        along_y.reshape(rows_y, -1),
        along_x.reshape(rows, -1),
        inverse,
        back.reshape(size_x * size_y, 16, rows),
        sine_z[:depth, :depth],
    )


def parts(field):
    high = field.astype(jnp.bfloat16)
    return high, (field - high.astype(jnp.float32)).astype(jnp.bfloat16)


def both_dot(left, right):
    rows, lanes = left.shape[0], right.shape[1]
    sums = jnp.dot(
        jnp.concatenate(parts(left), axis=0),
        jnp.concatenate(parts(right), axis=1),
        preferred_element_type=jnp.float32,
    )
    return (sums[:rows, :lanes] + sums[rows:, :lanes]) + (sums[:rows, lanes:] + sums[rows:, lanes:])


def split_dot(table, field):
    lanes = field.shape[1]
    rows = table.shape[0] // 2
    high = field.astype(jnp.bfloat16)
    low = (field - high.astype(jnp.float32)).astype(jnp.bfloat16)
    both = jnp.concatenate([high, low], axis=1)
    top = jnp.dot(table[:rows], both, preferred_element_type=jnp.float32)
    bottom = jnp.dot(table[rows:], both, preferred_element_type=jnp.float32)
    return (top[:, :lanes] + bottom[:, :lanes]) + (top[:, lanes:] + bottom[:, lanes:])


def six_parts(value, axis):
    found = []
    for _ in range(3):
        found.append(value.astype(jnp.bfloat16).astype(jnp.float32))
        value = value - found[-1]
    order = [found[n] for n in (0, 0, 0, 1, 1, 2)]
    return jnp.concatenate(order, axis=axis).astype(jnp.bfloat16)


def table_dot(table, value):
    return jnp.dot(table, six_parts(value, 0), preferred_element_type=jnp.float32)


def dot_table(value, table):
    return jnp.dot(six_parts(value, 1), table, preferred_element_type=jnp.float32)


def wide_dot(table, field):
    high, low = parts(field)
    pieces = table.shape[1] // field.shape[0]
    return jnp.dot(
        table,
        jnp.concatenate([high] * (pieces - 1) + [low], axis=0),
        preferred_element_type=jnp.float32,
    )


def copy_kernel(p_in, r_in, p_out, r_out):
    p_out[...] = p_in[...]
    r_out[...] = r_in[...]


def kernel(size_x, size_y, weights, derivative, modes, *refs):
    n_in = 15
    inputs, (p_ref, r_ref) = refs[:n_in], refs[n_in : n_in + 2]
    local = refs[n_in + 2 : 2 * n_in + 2]
    (
        cw, faces, base, first, second, image, alpha, beta_raw, smooth, flux_i,
        rx, ry, re, mine_y, got_y, mine_x, got_x, mine_s, got_s,
        in_sem, halo_send, halo_recv, y_send, y_recv, x_send, x_recv,
    ) = refs[2 * n_in + 2 :]
    (
        f_ref, corner_ref, coef_ref, weight_ref, solve_faces_ref, solve_inner_ref,
        forward_ref, backward_outer_ref, backward_inner_ref,
        along_y_ref, along_x_ref, sine_ref, inverse_ref, back_ref, spread_ref,
    ) = local
    lanes = f_ref.shape[2]
    my_x = lax.axis_index("gx")
    my_y = lax.axis_index("gy")
    me = my_x * size_y + my_y

    fetches = [
        pltpu.make_async_copy(
            inputs[n].at[me] if local[n] is back_ref else inputs[n], local[n], in_sem.at[n]
        )
        for n in range(n_in)
    ]
    for fetch in fetches:
        fetch.start()

    def exists(direction):
        dx, dy = direction
        ok = None
        for pos, size, step in ((my_x, size_x, dx), (my_y, size_y, dy)):
            if step:
                cond = pos > 0 if step < 0 else pos < size - 1
                ok = cond if ok is None else jnp.logical_and(ok, cond)
        return ok

    def peers_y():
        for offset in range(1, size_y):
            other = my_y + offset
            yield (my_x, jnp.where(other >= size_y, other - size_y, other))

    def peers_x():
        for offset in range(1, size_x):
            other = my_x + offset
            yield (jnp.where(other >= size_x, other - size_x, other), my_y)

    barrier = pltpu.get_barrier_semaphore()
    count = jnp.int32(size_x - 1 + size_y - 1)
    for direction in DIRS[4:]:
        here = exists(direction)

        @pl.when(here)
        def _(direction=direction):
            pl.semaphore_signal(
                barrier,
                inc=1,
                device_id=(my_x + direction[0], my_y + direction[1]),
                device_id_type=MESH,
            )

        count = count + here.astype(jnp.int32)
    for other in [*peers_y(), *peers_x()]:
        pl.semaphore_signal(barrier, inc=1, device_id=other, device_id_type=MESH)

    def node_rows(step):
        return 0 if step < 0 else 7

    def source(direction):
        dx, dy = direction
        if dy == 0:
            return faces.at[2 + (dx > 0)]
        if dx == 0:
            return faces.at[int(dy > 0)]
        return faces.at[2 + (dx > 0), pl.ds(8 * node_rows(dy), 8)]

    def landing(turn, index):
        if index < 2:
            return rx.at[turn, index]
        if index < 4:
            return ry.at[turn, index - 2]
        return re.at[turn, index - 4]

    def halo_copy(turn, index):
        direction = DIRS[index]
        opposite = DIRS.index((-direction[0], -direction[1]))
        return pltpu.make_async_remote_copy(
            src_ref=source(direction),
            dst_ref=landing(turn, opposite),
            send_sem=halo_send.at[turn, index],
            recv_sem=halo_recv.at[turn, opposite],
            device_id=(my_x + direction[0], my_y + direction[1]),
            device_id_type=MESH,
        )

    def halo_arrival(turn, index):
        direction = DIRS[index]
        return pltpu.make_async_remote_copy(
            src_ref=source(direction),
            dst_ref=landing(turn, index),
            send_sem=halo_send.at[turn, index],
            recv_sem=halo_recv.at[turn, index],
            device_id=(my_x + direction[0], my_y + direction[1]),
            device_id_type=MESH,
        )

    def sum_depth(ref):
        count = ref.shape[0]
        lane = lax.broadcasted_iota(jnp.int32, (count, 8, lanes), 2)
        head = ref[:, pl.ds(0, 8, stride=8), :]
        tail = ref[:, pl.ds(7, 8, stride=8), :]
        rows = (8 * count, lanes)
        from_tail = pltpu.roll(tail.reshape(rows), 1, 1).reshape(lane.shape)
        from_head = pltpu.roll(head.reshape(rows), lanes - 1, 1).reshape(lane.shape)
        ref[:, pl.ds(0, 8, stride=8), :] = jnp.where(lane == 0, 0.0, head + from_tail)
        ref[:, pl.ds(7, 8, stride=8), :] = jnp.where(lane == lanes - 1, 0.0, tail + from_head)

    def send_faces(turn, raw_ref):
        for side in range(2):
            faces[side] = raw_ref[:, pl.ds(56 * side, 8)].reshape(64, lanes)
            faces[2 + side] = raw_ref[7 * side]
        sum_depth(faces)
        send_halo(turn)

    def fill_inner(target, raw):
        target[pl.ds(1, 6), pl.ds(8, 48)] = raw
        sum_depth(target)

    def send_halo(turn):
        for index in (2, 3, 4, 5, 6, 7, 0, 1):
            @pl.when(exists(DIRS[index]))
            def _(index=index):
                halo_copy(turn, index).start()

    def take_halo(turn, target):
        for index in range(8):
            @pl.when(exists(DIRS[index]))
            def _(index=index):
                halo_copy(turn, index).wait_send()
                halo_arrival(turn, index).wait_recv()

        has = [exists(direction) for direction in DIRS[:4]]
        for side in range(2):
            i = 7 * side
            target[i, pl.ds(8, 48)] = jnp.where(
                has[side],
                faces[2 + side, pl.ds(8, 48)] + rx[turn, side, pl.ds(8, 48)],
                0.0,
            )
            target[pl.ds(1, 6), pl.ds(8 * i, 8)] = jnp.where(
                has[2 + side],
                faces[side, pl.ds(8, 48)] + ry[turn, side, pl.ds(8, 48)],
                0.0,
            ).reshape(6, 8, lanes)
            for other in range(2):
                j = 7 * other
                target[i, pl.ds(8 * j, 8)] = jnp.where(
                    jnp.logical_and(has[side], has[2 + other]),
                    (faces[2 + side, pl.ds(8 * j, 8)] + rx[turn, side, pl.ds(8 * j, 8)])
                    + (ry[turn, other, pl.ds(8 * i, 8)] + re[turn, 2 * side + other]),
                    0.0,
                )

    def send_to(peers, me_there, message, got, send, recv, value):
        message[...] = value
        got[me_there] = value
        for other in peers:
            pltpu.make_async_remote_copy(
                src_ref=message,
                dst_ref=got.at[me_there],
                send_sem=send,
                recv_sem=recv,
                device_id=other,
                device_id_type=MESH,
            ).start()

    def take_from(size, got, send, recv):
        span = got.at[pl.ds(0, size - 1)]
        copy = pltpu.make_async_remote_copy(
            src_ref=span,
            dst_ref=span,
            send_sem=send,
            recv_sem=recv,
            device_id=(jnp.where(my_x == 0, 1, 0), my_y),
            device_id_type=MESH,
        )
        copy.wait_send()
        copy.wait_recv()
        return got[...]

    def send_y(turn, value):
        send_to(
            peers_y(), my_y, mine_y.at[turn], got_y.at[turn],
            y_send.at[turn], y_recv.at[turn], value,
        )

    def take_y(turn):
        return take_from(size_y, got_y.at[turn], y_send.at[turn], y_recv.at[turn])

    def send_x(turn, value):
        mine, got = (mine_s, got_s) if turn == 2 else (mine_x.at[turn], got_x.at[turn])
        send_to(peers_x(), my_x, mine, got, x_send.at[turn], x_recv.at[turn], value)

    def take_x(turn):
        got = got_s if turn == 2 else got_x.at[turn]
        return take_from(size_x, got, x_send.at[turn], x_recv.at[turn])

    def pass_on(turn):
        send_x(turn, table_dot(along_y_ref[...], take_y(turn).reshape(size_y * 4, lanes)))

    row = lax.broadcasted_iota(jnp.int32, (8, lanes), 0)
    row4 = lax.broadcasted_iota(jnp.int32, (4, lanes), 0)
    lane4 = lax.broadcasted_iota(jnp.int32, (4, lanes), 1)

    def corner_message(raw):
        corners = both_dot(corner_ref[...], raw)
        moved = pltpu.roll(pltpu.roll(corners, 1, 1), 4, 0)
        return (corners + moved)[:4]

    def coarse_values(turn):
        gathered = take_x(turn)
        gathered = gathered.reshape(size_x * gathered.shape[1], lanes)
        combined = table_dot(along_x_ref[...], gathered)
        spectral = dot_table(combined, sine_ref[...]) * inverse_ref[...]
        mine = table_dot(back_ref[...], spectral)[:8]
        columns = dot_table(mine, sine_ref[...])
        corners = jnp.where(row < 4, columns, pltpu.roll(columns, lanes - 1, 1))
        return table_dot(spread_ref[...], corners), combined

    def solve_and_send(turn, field):
        faces[...] = split_dot(solve_faces_ref[...], field).reshape(4, 64, lanes)
        sum_depth(faces)
        send_halo(turn)

    def solve_inner(field, target):
        fill_inner(target, split_dot(solve_inner_ref[...], field).reshape(6, 48, lanes))

    def fluxes(field_ref):
        values = field_ref[...] - field_ref[:, pl.ds(27, 1)]
        grads = wide_dot(
            forward_ref[...],
            jnp.concatenate(
                [values[:4].reshape(256, lanes), values[4:].reshape(256, lanes)], axis=1
            ),
        )
        factor = jnp.concatenate(
            [cw[pl.ds(0, 4)].reshape(256, lanes), cw[pl.ds(4, 4)].reshape(256, lanes)], axis=1
        )
        grads_j, grads_k = grads[:256], grads[256:]
        flux_j, flux_k = grads_j * factor, grads_k * factor
        energy = stretch[1] * (grads_j * flux_j) + stretch[2] * (grads_k * flux_k)
        energy = jnp.sum(energy.reshape(32, 8, 2 * lanes), axis=0)
        energy = energy[:, :lanes] + energy[:, lanes:]
        for part in range(8):
            span = pl.ds(8 * part, 8)
            nodal = [field_ref[i, span] for i in range(8)]
            for p in range(8):
                grad = nodal[0] * derivative[p][0]
                for i in range(1, 8):
                    grad = grad + nodal[i] * derivative[p][i]
                flux = grad * cw[p, span]
                flux_i[p, span] = flux
                energy = energy + grad * flux
        return jnp.concatenate([flux_j, flux_k], axis=0), energy

    def divergence(flux, target, tiles, product, place):
        for j in range(8):
            span = pl.ds(8 * j, 8)
            along_i = [flux_i[p, span] for p in range(8)]
            for i in range(8):
                if (i, j) not in tiles:
                    continue
                row_at, lane_at = place(i % 4, j), lanes * (i // 4)
                total = product[row_at : row_at + 8, lane_at : lane_at + lanes]
                for p in range(8):
                    total = total + along_i[p] * derivative[p][i]
                target[i, span] = total

    all_tiles = [(i, j) for i in range(8) for j in range(8)]
    inner_tiles = [(i, j) for i, j in all_tiles if 0 < i < 7 and 0 < j < 7]
    face_tiles = [tile for tile in all_tiles if tile not in inner_tiles]

    def outer_place(i, j):
        if j in (0, 7):
            return 8 * (2 * i + (j == 7))
        return 64 + 8 * (6 * (i == 3) + j - 1)

    def operate(turn, flux, raw, target):
        outer = wide_dot(backward_outer_ref[...], flux)
        divergence(flux, raw, face_tiles, outer, outer_place)
        send_faces(turn, raw)
        middle = wide_dot(backward_inner_ref[...], flux)
        ends = [(i, j) for i, j in inner_tiles if i in (3, 4)]
        rest = [(i, j) for i, j in inner_tiles if i not in (3, 4)]
        divergence(flux, raw, ends, outer, outer_place)
        divergence(flux, raw, rest, middle, lambda i, j: 8 * (6 * (i - 1) + j - 1))
        fill_inner(target, raw[pl.ds(1, 6), pl.ds(8, 48)])

    def partial(left, right):
        return jnp.sum((left * right).reshape(64, 8, lanes), axis=0)

    def row_sum(tile):
        return jnp.sum(tile, axis=0, keepdims=True)

    def total(rows):
        return jnp.sum(rows, axis=(0, 1), keepdims=True)

    fetches[0].wait()
    pl.semaphore_wait(barrier, count)
    send_faces(0, f_ref)
    fetches[1].wait()
    send_y(0, corner_message(f_ref[...].reshape(512, lanes)))
    fill_inner(base, f_ref[pl.ds(1, 6), pl.ds(8, 48)])
    fetches[2].wait()
    fetches[3].wait()
    for i in range(8):
        cw[i] = coef_ref[i] * (weight_ref[...] * weights[i])
    fetches[4].wait()
    take_halo(0, base)

    field = base[...].reshape(512, lanes)
    solve_and_send(1, field)
    for fetch in fetches[5:]:
        fetch.wait()
    pass_on(0)
    solve_inner(field, first)
    coarse, _ = coarse_values(0)
    take_halo(1, first)
    first[...] += coarse.reshape(8, 64, lanes)

    flux, curve = fluxes(first)
    operate(2, flux, alpha, image)
    message = corner_message(alpha[...].reshape(512, lanes))
    energy = total(partial(f_ref[...], first[...]))
    curve = total(curve)
    message = jnp.where(
        lane4 == 0, jnp.where(row4 == 0, energy, jnp.where(row4 == 1, curve, 0.0)), message
    )
    send_y(1, message)
    take_halo(2, image)

    field = image[...].reshape(512, lanes)
    solve_and_send(3, field)
    pass_on(1)
    solve_inner(field, smooth)
    coarse, combined = coarse_values(1)
    energy = combined[modes : modes + 1, 0:1]
    curve = combined[modes + 1 : modes + 2, 0:1]
    step = energy / curve
    step3 = step.reshape(1, 1, 1)
    take_halo(3, smooth)
    second[...] = first[...] - step3 * (smooth[...] + coarse.reshape(8, 64, lanes))

    fresh = row_sum(partial(f_ref[...] - step3 * alpha[...], second[...]))
    cross = row_sum(partial(alpha[...], second[...]))
    flux, along = fluxes(second)
    along = row_sum(along)
    send_y(
        2,
        jnp.where(
            row4 == 0, fresh, jnp.where(row4 == 1, along, jnp.where(row4 == 2, cross, 0.0))
        ),
    )
    operate(4, flux, beta_raw, smooth)
    send_x(2, jnp.sum(take_y(2), axis=0))
    take_halo(4, smooth)
    sums = jnp.sum(take_x(2), axis=0)
    fresh = total(sums[0:1])
    ratio = fresh / energy
    along = total(sums[1:2]) + 2.0 * ratio * total(sums[2:3]) + ratio * ratio * curve
    second_step = fresh / along
    ratio3 = ratio.reshape(1, 1, 1)
    second3 = second_step.reshape(1, 1, 1)
    p_ref[...] = step3 * first[...] + second3 * (second[...] + ratio3 * first[...])
    r_ref[...] = (base[...] - step3 * image[...]) - second3 * (smooth[...] + ratio3 * image[...])


def solution(mesh):
    size_x, size_y = mesh.shape["gx"], mesh.shape["gy"]
    (
        weights, derivative, solve_faces, solve_inner,
        forward, backward_outer, backward_inner, corner,
    ) = element_tables()
    spec = P(None, None, None, "gx", "gy", None)

    def on_device(forcing, coefficient):
        shape = forcing.shape
        depth = shape[5]
        along_y, along_x, inverse, back, sine = coarse_tables(size_x, size_y, depth)
        modes = (size_x - 1) * (size_y - 1)
        plane = np.outer(weights, weights).reshape(64, 1) * np.ones((1, depth))
        field = (8, 64, depth)
        operands = [
            forcing.reshape(field),
            np.asarray(corner, np.float32),
            coefficient.reshape(field),
            np.asarray(plane, np.float32),
            halves(solve_faces),
            halves(solve_inner),
            pieces(forward, 3),
            pieces(backward_outer, 2),
            pieces(backward_inner, 2),
            sixfold(along_y, 1),
            sixfold(along_x, 1),
            sixfold(sine, 0),
            np.asarray(inverse, np.float32),
            sixfold(back, 2),
            sixfold(corner.T, 1),
        ]
        shapes = [op.shape for op in operands]
        shapes[13] = shapes[13][1:]
        rows_y = along_y.shape[0]
        vmem = pl.BlockSpec(memory_space=pltpu.VMEM)
        pressure, residual = pl.pallas_call(
            functools.partial(
                kernel, size_x, size_y, weights.tolist(), derivative.tolist(), modes
            ),
            out_shape=[jax.ShapeDtypeStruct(field, jnp.float32)] * 2,
            in_specs=[pl.BlockSpec(memory_space=pltpu.HBM)] * len(operands),
            out_specs=[vmem, vmem],
            scratch_shapes=[pltpu.VMEM(dims, op.dtype) for dims, op in zip(shapes, operands)]
            + [pltpu.VMEM(field, jnp.float32)]
            + [pltpu.VMEM((4, 64, depth), jnp.float32)]
            + [pltpu.VMEM(field, jnp.float32)] * 8
            + [
                pltpu.VMEM((5, 2, 64, depth), jnp.float32),
                pltpu.VMEM((5, 2, 64, depth), jnp.float32),
                pltpu.VMEM((5, 4, 8, depth), jnp.float32),
                pltpu.VMEM((3, 4, depth), jnp.float32),
                pltpu.VMEM((3, size_y, 4, depth), jnp.float32),
                pltpu.VMEM((2, rows_y, depth), jnp.float32),
                pltpu.VMEM((2, size_x, rows_y, depth), jnp.float32),
                pltpu.VMEM((4, depth), jnp.float32),
                pltpu.VMEM((size_x, 4, depth), jnp.float32),
                pltpu.SemaphoreType.DMA((len(operands),)),
                pltpu.SemaphoreType.DMA((5, 8)),
                pltpu.SemaphoreType.DMA((5, 8)),
                pltpu.SemaphoreType.DMA((3,)),
                pltpu.SemaphoreType.DMA((3,)),
                pltpu.SemaphoreType.DMA((3,)),
                pltpu.SemaphoreType.DMA((3,)),
            ],
            compiler_params=pltpu.CompilerParams(
                collective_id=0, has_side_effects=True, vmem_limit_bytes=60 * 1024 * 1024
            ),
        )(*operands)
        pressure, residual = pl.pallas_call(
            copy_kernel,
            out_shape=[jax.ShapeDtypeStruct(field, jnp.float32)] * 2,
            in_specs=[vmem, vmem],
            out_specs=[vmem, vmem],
            compiler_params=pltpu.CompilerParams(vmem_limit_bytes=60 * 1024 * 1024),
        )(pressure, residual)
        return pressure.reshape(shape), residual.reshape(shape)

    return jax.shard_map(
        on_device, mesh=mesh, in_specs=(spec, spec), out_specs=(spec, spec), check_vma=False
    )
```

```python
import functools
import math

import jax
import jax.numpy as jnp
import numpy as np
from jax import lax
from jax.experimental import pallas as pl
from jax.experimental.pallas import tpu as pltpu
from jax.sharding import PartitionSpec as P

MESH = pl.DeviceIdType.MESH
stretch = (1.0, 64.0, 1.0)
DIRS = ((-1, 0), (1, 0), (0, -1), (0, 1), (-1, -1), (-1, 1), (1, -1), (1, 1))


def legendre_value(order, position):
    prev_value = 1.0
    this_value = position
    for degree_now in range(2, order + 1):
        next_value = (
            (2 * degree_now - 1) * position * this_value - (degree_now - 1) * prev_value
        ) / degree_now
        prev_value = this_value
        this_value = next_value
    return this_value


def gll_points():
    points = [-1.0]
    for node_index in range(1, 7):
        position = -math.cos(math.pi * node_index / 7.0)
        for newton_step in range(60):
            target = legendre_value(8, position) - legendre_value(6, position)
            slope = 15.0 * legendre_value(7, position)
            position = position - target / slope
        points.append(position)
    points.append(1.0)
    return points


def jacobi_eigen(matrix_in):
    order_n = len(matrix_in)
    work_mat = [list(one_row) for one_row in matrix_in]
    vectors = [
        [1.0 if row_index == col_index else 0.0 for col_index in range(order_n)]
        for row_index in range(order_n)
    ]
    for sweep_index in range(40):
        for first_idx in range(order_n):
            for second_idx in range(first_idx + 1, order_n):
                rotation = 0.5 * math.atan2(
                    2.0 * work_mat[first_idx][second_idx],
                    work_mat[second_idx][second_idx] - work_mat[first_idx][first_idx],
                )
                cosine = math.cos(rotation)
                sine_part = math.sin(rotation)
                for other in range(order_n):
                    left_val = work_mat[other][first_idx]
                    right_val = work_mat[other][second_idx]
                    work_mat[other][first_idx] = cosine * left_val - sine_part * right_val
                    work_mat[other][second_idx] = sine_part * left_val + cosine * right_val
                for other in range(order_n):
                    left_val = work_mat[first_idx][other]
                    right_val = work_mat[second_idx][other]
                    work_mat[first_idx][other] = cosine * left_val - sine_part * right_val
                    work_mat[second_idx][other] = sine_part * left_val + cosine * right_val
                for other in range(order_n):
                    left_val = vectors[other][first_idx]
                    right_val = vectors[other][second_idx]
                    vectors[other][first_idx] = cosine * left_val - sine_part * right_val
                    vectors[other][second_idx] = sine_part * left_val + cosine * right_val
    return ([work_mat[diag_index][diag_index] for diag_index in range(order_n)], vectors)


def spectral_tables():
    nodes = gll_points()
    values_at = [legendre_value(7, position) for position in nodes]
    weights = [2.0 / (56.0 * value_now * value_now) for value_now in values_at]
    derivative = np.zeros((8, 8))
    for row in range(8):
        for col in range(8):
            if row != col:
                derivative[row, col] = values_at[row] / (
                    values_at[col] * (nodes[row] - nodes[col])
                )
    derivative[0, 0] = -14.0
    derivative[7, 7] = 14.0
    weights = np.array(weights)
    stiffness = derivative.T @ np.diag(weights) @ derivative
    stiffness[0, 0] *= 2.0
    stiffness[7, 7] *= 2.0
    inv_root = 1.0 / np.sqrt(weights)
    symmetric = inv_root[:, None] * stiffness * inv_root[None, :]
    eigen_values, eigen_vectors = jacobi_eigen(symmetric.tolist())
    fdm_basis = inv_root[:, None] * np.array(eigen_vectors)
    nodes = np.array(nodes)
    hats = np.stack([(1.0 - nodes) / 2.0, (1.0 + nodes) / 2.0])
    return weights, derivative, fdm_basis, np.array(eigen_values), hats


def sine_table(cells):
    ids = np.arange(cells + 1)
    table = math.sqrt(2.0 / cells) * np.sin(math.pi * (np.outer(ids, ids) % (2 * cells)) / cells)
    table[0] = table[-1] = 0.0
    table[:, 0] = table[:, -1] = 0.0
    return table


def mode_values(cells):
    cosines = np.cos(math.pi * np.arange(1, cells) / cells)
    return (2.0 - 2.0 * cosines) / 2.0, 2.0 * (4.0 + 2.0 * cosines) / 6.0


def round_up(value, step):
    return -(-value // step) * step


def halves(table):
    table = np.asarray(table, np.float32)
    high = table.astype(jnp.bfloat16)
    low = (table - high.astype(np.float32)).astype(jnp.bfloat16)
    return np.concatenate([high, low], axis=0)


def pieces(table, count):
    table = np.asarray(table, np.float32)
    found = []
    for _ in range(count):
        found.append(table.astype(jnp.bfloat16))
        table = table - found[-1].astype(np.float32)
    return np.concatenate(found + [found[0]], axis=1)


def sixfold(table, axis):
    table = np.asarray(table, np.float32)
    found = []
    for _ in range(3):
        found.append(table.astype(jnp.bfloat16))
        table = table - found[-1].astype(np.float32)
    return np.concatenate([found[n] for n in (0, 1, 2, 0, 1, 0)], axis=axis)


def element_tables():
    weights, derivative, basis, eigen, hats = spectral_tables()
    eye = np.eye(8)
    cube = np.kron(np.kron(basis, basis), basis)
    total = (
        stretch[0] * eigen[:, None, None]
        + stretch[1] * eigen[None, :, None]
        + stretch[2] * eigen[None, None, :]
    ).reshape(-1)
    solve = (cube / total) @ cube.T
    along_j = np.kron(np.eye(4), np.kron(derivative, eye))
    along_k = np.kron(np.eye(4), np.kron(eye, derivative))
    forward = np.concatenate([along_j, along_k], axis=0)
    backward = np.concatenate([stretch[1] * along_j.T, stretch[2] * along_k.T], axis=1)
    corner = np.stack(
        [
            np.kron(np.kron(hats[a], hats[b]), hats[c])
            for c in range(2)
            for a in range(2)
            for b in range(2)
        ]
    )
    node = np.arange(512).reshape(8, 8, 8)
    faces = [node[:, 0], node[:, 7], node[0], node[7]]
    solve_faces = solve[np.stack(faces).reshape(-1)]
    solve_inner = solve[node[1:7, 1:7].reshape(-1)]
    node = node[:4]
    outer = [node[:, [0, 7]], node[[0, 3], 1:7]]
    backward_outer = backward[np.concatenate([rows.reshape(-1) for rows in outer])]
    backward_inner = backward[node[1:3, 1:7].reshape(-1)]
    return (
        weights, derivative, solve_faces, solve_inner,
        forward, backward_outer, backward_inner, corner,
    )


def coarse_tables(size_x, size_y, depth):
    sine_x, sine_y, sine_z = sine_table(size_x), sine_table(size_y), sine_table(depth)
    modes = (size_x - 1) * (size_y - 1)
    rows = round_up(modes + 2, 8)
    waves_y = size_y - 1
    rows_y = round_up(2 * waves_y + 2, 8)
    along_y = np.zeros((rows_y, size_y, 4))
    along_x = np.zeros((rows, size_x, rows_y))
    for a in range(2):
        for y in range(size_y):
            for b in range(2):
                along_y[a : 2 * waves_y : 2, y, 2 * a + b] = sine_y[1:-1, y + b]
        for x in range(size_x):
            for n in range(waves_y):
                along_x[n : modes : waves_y, x, 2 * n + a] = sine_x[1:-1, x + a]
    for q in range(2):
        along_y[2 * waves_y + q, :, q] = 1.0
        along_x[modes + q, :, 2 * waves_y + q] = 1.0
    stiff_x, mass_x = mode_values(size_x)
    stiff_y, mass_y = mode_values(size_y)
    stiff_z, mass_z = mode_values(depth)
    denominator = (
        stretch[0] * stiff_x[:, None, None] * mass_y[None, :, None] * mass_z[None, None, :]
        + stretch[1] * mass_x[:, None, None] * stiff_y[None, :, None] * mass_z[None, None, :]
        + stretch[2] * mass_x[:, None, None] * mass_y[None, :, None] * stiff_z[None, None, :]
    )
    inverse = np.zeros((rows, depth))
    inverse[:modes, 1:] = (1.0 / denominator).reshape(modes, depth - 1)
    back = np.zeros((size_x, size_y, 16, rows))
    for x in range(size_x):
        for y in range(size_y):
            for c in range(2):
                for a in range(2):
                    for b in range(2):
                        back[x, y, 4 * c + 2 * a + b, :modes] = np.outer(
                            sine_x[1:-1, x + a], sine_y[1:-1, y + b]
                        ).reshape(-1)
    return (
        along_y.reshape(rows_y, -1),
        along_x.reshape(rows, -1),
        inverse,
        back.reshape(size_x * size_y, 16, rows),
        sine_z[:depth, :depth],
    )


def parts(field):
    high = field.astype(jnp.bfloat16)
    return high, (field - high.astype(jnp.float32)).astype(jnp.bfloat16)


def both_dot(left, right):
    rows, lanes = left.shape[0], right.shape[1]
    sums = jnp.dot(
        jnp.concatenate(parts(left), axis=0),
        jnp.concatenate(parts(right), axis=1),
        preferred_element_type=jnp.float32,
    )
    return (sums[:rows, :lanes] + sums[rows:, :lanes]) + (sums[:rows, lanes:] + sums[rows:, lanes:])


def split_dot(table, field):
    lanes = field.shape[1]
    rows = table.shape[0] // 2
    high = field.astype(jnp.bfloat16)
    low = (field - high.astype(jnp.float32)).astype(jnp.bfloat16)
    both = jnp.concatenate([high, low], axis=1)
    top = jnp.dot(table[:rows], both, preferred_element_type=jnp.float32)
    bottom = jnp.dot(table[rows:], both, preferred_element_type=jnp.float32)
    return (top[:, :lanes] + bottom[:, :lanes]) + (top[:, lanes:] + bottom[:, lanes:])


def six_parts(value, axis):
    found = []
    for _ in range(3):
        found.append(value.astype(jnp.bfloat16).astype(jnp.float32))
        value = value - found[-1]
    order = [found[n] for n in (0, 0, 0, 1, 1, 2)]
    return jnp.concatenate(order, axis=axis).astype(jnp.bfloat16)


def table_dot(table, value):
    return jnp.dot(table, six_parts(value, 0), preferred_element_type=jnp.float32)


def dot_table(value, table):
    return jnp.dot(six_parts(value, 1), table, preferred_element_type=jnp.float32)


def wide_dot(table, field):
    high, low = parts(field)
    pieces = table.shape[1] // field.shape[0]
    return jnp.dot(
        table,
        jnp.concatenate([high] * (pieces - 1) + [low], axis=0),
        preferred_element_type=jnp.float32,
    )


def copy_kernel(p_in, r_in, p_out, r_out):
    p_out[...] = p_in[...]
    r_out[...] = r_in[...]


def kernel(size_x, size_y, weights, derivative, modes, *refs):
    n_in = 15
    inputs, (p_ref, r_ref) = refs[:n_in], refs[n_in : n_in + 2]
    local = refs[n_in + 2 : 2 * n_in + 2]
    (
        cw, faces, base, first, second, image, alpha, beta_raw, smooth, flux_i,
        rx, ry, re, mine_y, got_y, mine_x, got_x, mine_s, got_s,
        in_sem, halo_send, halo_recv, y_send, y_recv, x_send, x_recv, s_send, s_recv,
    ) = refs[2 * n_in + 2 :]
    (
        f_ref, corner_ref, coef_ref, weight_ref, solve_faces_ref, solve_inner_ref,
        forward_ref, backward_outer_ref, backward_inner_ref,
        along_y_ref, along_x_ref, sine_ref, inverse_ref, back_ref, spread_ref,
    ) = local
    lanes = f_ref.shape[2]
    my_x = lax.axis_index("gx")
    my_y = lax.axis_index("gy")
    me = my_x * size_y + my_y

    fetches = [
        pltpu.make_async_copy(
            inputs[n].at[me] if local[n] is back_ref else inputs[n], local[n], in_sem.at[n]
        )
        for n in range(n_in)
    ]
    for fetch in fetches:
        fetch.start()

    def exists(direction):
        dx, dy = direction
        ok = None
        for pos, size, step in ((my_x, size_x, dx), (my_y, size_y, dy)):
            if step:
                cond = pos > 0 if step < 0 else pos < size - 1
                ok = cond if ok is None else jnp.logical_and(ok, cond)
        return ok

    def peers_y():
        for offset in range(1, size_y):
            other = my_y + offset
            yield (my_x, jnp.where(other >= size_y, other - size_y, other))

    def peers_x():
        for offset in range(1, size_x):
            other = my_x + offset
            yield (jnp.where(other >= size_x, other - size_x, other), my_y)

    def peers_all():
        for offset_y in range(size_y - 1, -1, -1):
            other_y = my_y + offset_y
            other_y = jnp.where(other_y >= size_y, other_y - size_y, other_y)
            for offset_x in range(0 if offset_y else 1, size_x):
                other_x = my_x + offset_x
                yield (jnp.where(other_x >= size_x, other_x - size_x, other_x), other_y)

    barrier = pltpu.get_barrier_semaphore()
    count = jnp.int32(size_x - 1 + size_y - 1)
    for direction in DIRS[4:]:
        here = exists(direction)

        @pl.when(here)
        def _(direction=direction):
            pl.semaphore_signal(
                barrier,
                inc=1,
                device_id=(my_x + direction[0], my_y + direction[1]),
                device_id_type=MESH,
            )

        count = count + here.astype(jnp.int32)
    for other in [*peers_y(), *peers_x()]:
        pl.semaphore_signal(barrier, inc=1, device_id=other, device_id_type=MESH)

    def node_rows(step):
        return 0 if step < 0 else 7

    def source(direction):
        dx, dy = direction
        if dy == 0:
            return faces.at[2 + (dx > 0)]
        if dx == 0:
            return faces.at[int(dy > 0)]
        return faces.at[2 + (dx > 0), pl.ds(8 * node_rows(dy), 8)]

    def landing(turn, index):
        if index < 2:
            return rx.at[turn, index]
        if index < 4:
            return ry.at[turn, index - 2]
        return re.at[turn, index - 4]

    def halo_copy(turn, index):
        direction = DIRS[index]
        opposite = DIRS.index((-direction[0], -direction[1]))
        return pltpu.make_async_remote_copy(
            src_ref=source(direction),
            dst_ref=landing(turn, opposite),
            send_sem=halo_send.at[turn, index],
            recv_sem=halo_recv.at[turn, opposite],
            device_id=(my_x + direction[0], my_y + direction[1]),
            device_id_type=MESH,
        )

    def halo_arrival(turn, index):
        direction = DIRS[index]
        return pltpu.make_async_remote_copy(
            src_ref=source(direction),
            dst_ref=landing(turn, index),
            send_sem=halo_send.at[turn, index],
            recv_sem=halo_recv.at[turn, index],
            device_id=(my_x + direction[0], my_y + direction[1]),
            device_id_type=MESH,
        )

    def sum_depth(ref):
        count = ref.shape[0]
        lane = lax.broadcasted_iota(jnp.int32, (count, 8, lanes), 2)
        head = ref[:, pl.ds(0, 8, stride=8), :]
        tail = ref[:, pl.ds(7, 8, stride=8), :]
        rows = (8 * count, lanes)
        from_tail = pltpu.roll(tail.reshape(rows), 1, 1).reshape(lane.shape)
        from_head = pltpu.roll(head.reshape(rows), lanes - 1, 1).reshape(lane.shape)
        ref[:, pl.ds(0, 8, stride=8), :] = jnp.where(lane == 0, 0.0, head + from_tail)
        ref[:, pl.ds(7, 8, stride=8), :] = jnp.where(lane == lanes - 1, 0.0, tail + from_head)

    def send_faces(turn, raw_ref):
        for side in range(2):
            faces[side] = raw_ref[:, pl.ds(56 * side, 8)].reshape(64, lanes)
            faces[2 + side] = raw_ref[7 * side]
        sum_depth(faces)
        send_halo(turn)

    def fill_inner(target, raw):
        target[pl.ds(1, 6), pl.ds(8, 48)] = raw
        sum_depth(target)

    def send_halo(turn):
        for index in (2, 3, 4, 5, 6, 7, 0, 1):
            @pl.when(exists(DIRS[index]))
            def _(index=index):
                halo_copy(turn, index).start()

    def take_halo(turn, target):
        for index in range(8):
            @pl.when(exists(DIRS[index]))
            def _(index=index):
                halo_copy(turn, index).wait_send()
                halo_arrival(turn, index).wait_recv()

        has = [exists(direction) for direction in DIRS[:4]]
        for side in range(2):
            i = 7 * side
            target[i, pl.ds(8, 48)] = jnp.where(
                has[side],
                faces[2 + side, pl.ds(8, 48)] + rx[turn, side, pl.ds(8, 48)],
                0.0,
            )
            target[pl.ds(1, 6), pl.ds(8 * i, 8)] = jnp.where(
                has[2 + side],
                faces[side, pl.ds(8, 48)] + ry[turn, side, pl.ds(8, 48)],
                0.0,
            ).reshape(6, 8, lanes)
            for other in range(2):
                j = 7 * other
                target[i, pl.ds(8 * j, 8)] = jnp.where(
                    jnp.logical_and(has[side], has[2 + other]),
                    (faces[2 + side, pl.ds(8 * j, 8)] + rx[turn, side, pl.ds(8 * j, 8)])
                    + (ry[turn, other, pl.ds(8 * i, 8)] + re[turn, 2 * side + other]),
                    0.0,
                )

    def send_to(peers, me_there, message, got, send, recv, value):
        message[...] = value
        got[me_there] = value
        for other in peers:
            pltpu.make_async_remote_copy(
                src_ref=message,
                dst_ref=got.at[me_there],
                send_sem=send,
                recv_sem=recv,
                device_id=other,
                device_id_type=MESH,
            ).start()

    def take_from(size, got, send, recv):
        span = got.at[pl.ds(0, size - 1)]
        copy = pltpu.make_async_remote_copy(
            src_ref=span,
            dst_ref=span,
            send_sem=send,
            recv_sem=recv,
            device_id=(jnp.where(my_x == 0, 1, 0), my_y),
            device_id_type=MESH,
        )
        copy.wait_send()
        copy.wait_recv()
        return got[...]

    def send_y(turn, value):
        send_to(
            peers_y(), my_y, mine_y.at[turn], got_y.at[turn],
            y_send.at[turn], y_recv.at[turn], value,
        )

    def take_y(turn):
        return take_from(size_y, got_y.at[turn], y_send.at[turn], y_recv.at[turn])

    def send_x(turn, value):
        send_to(
            peers_x(), my_x, mine_x.at[turn], got_x.at[turn],
            x_send.at[turn], x_recv.at[turn], value,
        )

    def take_x(turn):
        return take_from(size_x, got_x.at[turn], x_send.at[turn], x_recv.at[turn])

    def pass_on(turn):
        send_x(turn, table_dot(along_y_ref[...], take_y(turn).reshape(size_y * 4, lanes)))

    row = lax.broadcasted_iota(jnp.int32, (8, lanes), 0)
    row4 = lax.broadcasted_iota(jnp.int32, (4, lanes), 0)
    lane4 = lax.broadcasted_iota(jnp.int32, (4, lanes), 1)

    def corner_message(raw):
        corners = both_dot(corner_ref[...], raw)
        moved = pltpu.roll(pltpu.roll(corners, 1, 1), 4, 0)
        return (corners + moved)[:4]

    def coarse_values(turn):
        gathered = take_x(turn)
        gathered = gathered.reshape(size_x * gathered.shape[1], lanes)
        combined = table_dot(along_x_ref[...], gathered)
        spectral = dot_table(combined, sine_ref[...]) * inverse_ref[...]
        mine = table_dot(back_ref[...], spectral)[:8]
        columns = dot_table(mine, sine_ref[...])
        corners = jnp.where(row < 4, columns, pltpu.roll(columns, lanes - 1, 1))
        return table_dot(spread_ref[...], corners), combined

    def solve_and_send(turn, field):
        faces[...] = split_dot(solve_faces_ref[...], field).reshape(4, 64, lanes)
        sum_depth(faces)
        send_halo(turn)

    def solve_inner(field, target):
        fill_inner(target, split_dot(solve_inner_ref[...], field).reshape(6, 48, lanes))

    def fluxes(field_ref):
        values = field_ref[...] - field_ref[:, pl.ds(27, 1)]
        grads = wide_dot(
            forward_ref[...],
            jnp.concatenate(
                [values[:4].reshape(256, lanes), values[4:].reshape(256, lanes)], axis=1
            ),
        )
        factor = jnp.concatenate(
            [cw[pl.ds(0, 4)].reshape(256, lanes), cw[pl.ds(4, 4)].reshape(256, lanes)], axis=1
        )
        grads_j, grads_k = grads[:256], grads[256:]
        flux_j, flux_k = grads_j * factor, grads_k * factor
        energy = stretch[1] * (grads_j * flux_j) + stretch[2] * (grads_k * flux_k)
        energy = jnp.sum(energy.reshape(32, 8, 2 * lanes), axis=0)
        energy = energy[:, :lanes] + energy[:, lanes:]
        for part in range(8):
            span = pl.ds(8 * part, 8)
            nodal = [field_ref[i, span] for i in range(8)]
            for p in range(8):
                grad = nodal[0] * derivative[p][0]
                for i in range(1, 8):
                    grad = grad + nodal[i] * derivative[p][i]
                flux = grad * cw[p, span]
                flux_i[p, span] = flux
                energy = energy + grad * flux
        return jnp.concatenate([flux_j, flux_k], axis=0), energy

    def divergence(flux, target, tiles, product, place):
        for j in range(8):
            span = pl.ds(8 * j, 8)
            along_i = [flux_i[p, span] for p in range(8)]
            for i in range(8):
                if (i, j) not in tiles:
                    continue
                row_at, lane_at = place(i % 4, j), lanes * (i // 4)
                total = product[row_at : row_at + 8, lane_at : lane_at + lanes]
                for p in range(8):
                    total = total + along_i[p] * derivative[p][i]
                target[i, span] = total

    all_tiles = [(i, j) for i in range(8) for j in range(8)]
    inner_tiles = [(i, j) for i, j in all_tiles if 0 < i < 7 and 0 < j < 7]
    face_tiles = [tile for tile in all_tiles if tile not in inner_tiles]

    def outer_place(i, j):
        if j in (0, 7):
            return 8 * (2 * i + (j == 7))
        return 64 + 8 * (6 * (i == 3) + j - 1)

    def operate(turn, flux, raw, target, then=None):
        outer = wide_dot(backward_outer_ref[...], flux)
        divergence(flux, raw, face_tiles, outer, outer_place)
        send_faces(turn, raw)
        middle = wide_dot(backward_inner_ref[...], flux)
        ends = [(i, j) for i, j in inner_tiles if i in (3, 4)]
        rest = [(i, j) for i, j in inner_tiles if i not in (3, 4)]
        divergence(flux, raw, ends, outer, outer_place)
        divergence(flux, raw, rest, middle, lambda i, j: 8 * (6 * (i - 1) + j - 1))
        if then:
            then()
        fill_inner(target, raw[pl.ds(1, 6), pl.ds(8, 48)])

    def partial(left, right):
        return jnp.sum((left * right).reshape(64, 8, lanes), axis=0)

    def row_sum(tile):
        return jnp.sum(tile, axis=0, keepdims=True)

    def total(rows):
        return jnp.sum(rows, axis=(0, 1), keepdims=True)

    fetches[0].wait()
    pl.semaphore_wait(barrier, count)
    send_faces(0, f_ref)
    fetches[1].wait()
    send_y(0, corner_message(f_ref[...].reshape(512, lanes)))
    fill_inner(base, f_ref[pl.ds(1, 6), pl.ds(8, 48)])
    fetches[2].wait()
    fetches[3].wait()
    for i in range(8):
        cw[i] = coef_ref[i] * (weight_ref[...] * weights[i])
    fetches[4].wait()
    take_halo(0, base)

    field = base[...].reshape(512, lanes)
    solve_and_send(1, field)
    for fetch in fetches[5:]:
        fetch.wait()
    pass_on(0)
    solve_inner(field, first)
    coarse, _ = coarse_values(0)
    take_halo(1, first)
    first[...] += coarse.reshape(8, 64, lanes)

    flux, curve_part = fluxes(first)

    def send_residual():
        message = corner_message(alpha[...].reshape(512, lanes))
        scalars = jnp.where(
            row4 == 0,
            total(partial(f_ref[...], first[...])),
            jnp.where(row4 == 1, total(curve_part), 0.0),
        )
        send_y(1, jnp.where(lane4 == 0, scalars, message))

    operate(2, flux, alpha, image, send_residual)
    take_halo(2, image)

    field = image[...].reshape(512, lanes)
    solve_and_send(3, field)
    pass_on(1)
    solve_inner(field, smooth)
    coarse, combined = coarse_values(1)
    energy = combined[modes : modes + 1, 0:1]
    curve = combined[modes + 1 : modes + 2, 0:1]
    step = energy / curve
    step3 = step.reshape(1, 1, 1)
    take_halo(3, smooth)
    second[...] = first[...] - step3 * (smooth[...] + coarse.reshape(8, 64, lanes))

    fresh = row_sum(partial(f_ref[...] - step3 * alpha[...], second[...]))
    cross = row_sum(partial(alpha[...], second[...]))
    flux, along = fluxes(second)
    along = row_sum(along)
    sums = jnp.where(
        row4 == 0, fresh, jnp.where(row4 == 1, along, jnp.where(row4 == 2, cross, 0.0))
    )
    send_to(peers_all(), me, mine_s, got_s, s_send, s_recv, sums)
    operate(4, flux, beta_raw, smooth)
    take_halo(4, smooth)
    sums = jnp.sum(take_from(size_x * size_y, got_s, s_send, s_recv), axis=0)
    fresh = total(sums[0:1])
    ratio = fresh / energy
    along = total(sums[1:2]) + 2.0 * ratio * total(sums[2:3]) + ratio * ratio * curve
    second_step = fresh / along
    ratio3 = ratio.reshape(1, 1, 1)
    second3 = second_step.reshape(1, 1, 1)
    p_ref[...] = step3 * first[...] + second3 * (second[...] + ratio3 * first[...])
    r_ref[...] = (base[...] - step3 * image[...]) - second3 * (smooth[...] + ratio3 * image[...])


def solution(mesh):
    size_x, size_y = mesh.shape["gx"], mesh.shape["gy"]
    (
        weights, derivative, solve_faces, solve_inner,
        forward, backward_outer, backward_inner, corner,
    ) = element_tables()
    spec = P(None, None, None, "gx", "gy", None)

    def on_device(forcing, coefficient):
        shape = forcing.shape
        depth = shape[5]
        along_y, along_x, inverse, back, sine = coarse_tables(size_x, size_y, depth)
        modes = (size_x - 1) * (size_y - 1)
        plane = np.outer(weights, weights).reshape(64, 1) * np.ones((1, depth))
        field = (8, 64, depth)
        operands = [
            forcing.reshape(field),
            np.asarray(corner, np.float32),
            coefficient.reshape(field),
            np.asarray(plane, np.float32),
            halves(solve_faces),
            halves(solve_inner),
            pieces(forward, 3),
            pieces(backward_outer, 2),
            pieces(backward_inner, 2),
            sixfold(along_y, 1),
            sixfold(along_x, 1),
            sixfold(sine, 0),
            np.asarray(inverse, np.float32),
            sixfold(back, 2),
            sixfold(corner.T, 1),
        ]
        shapes = [op.shape for op in operands]
        shapes[13] = shapes[13][1:]
        rows_y = along_y.shape[0]
        vmem = pl.BlockSpec(memory_space=pltpu.VMEM)
        pressure, residual = pl.pallas_call(
            functools.partial(
                kernel, size_x, size_y, weights.tolist(), derivative.tolist(), modes
            ),
            out_shape=[jax.ShapeDtypeStruct(field, jnp.float32)] * 2,
            in_specs=[pl.BlockSpec(memory_space=pltpu.HBM)] * len(operands),
            out_specs=[vmem, vmem],
            scratch_shapes=[pltpu.VMEM(dims, op.dtype) for dims, op in zip(shapes, operands)]
            + [pltpu.VMEM(field, jnp.float32)]
            + [pltpu.VMEM((4, 64, depth), jnp.float32)]
            + [pltpu.VMEM(field, jnp.float32)] * 8
            + [
                pltpu.VMEM((5, 2, 64, depth), jnp.float32),
                pltpu.VMEM((5, 2, 64, depth), jnp.float32),
                pltpu.VMEM((5, 4, 8, depth), jnp.float32),
                pltpu.VMEM((2, 4, depth), jnp.float32),
                pltpu.VMEM((2, size_y, 4, depth), jnp.float32),
                pltpu.VMEM((2, rows_y, depth), jnp.float32),
                pltpu.VMEM((2, size_x, rows_y, depth), jnp.float32),
                pltpu.VMEM((4, depth), jnp.float32),
                pltpu.VMEM((size_x * size_y, 4, depth), jnp.float32),
                pltpu.SemaphoreType.DMA((len(operands),)),
                pltpu.SemaphoreType.DMA((5, 8)),
                pltpu.SemaphoreType.DMA((5, 8)),
                pltpu.SemaphoreType.DMA((2,)),
                pltpu.SemaphoreType.DMA((2,)),
                pltpu.SemaphoreType.DMA((2,)),
                pltpu.SemaphoreType.DMA((2,)),
                pltpu.SemaphoreType.DMA(()),
                pltpu.SemaphoreType.DMA(()),
            ],
            compiler_params=pltpu.CompilerParams(
                collective_id=0, has_side_effects=True, vmem_limit_bytes=60 * 1024 * 1024
            ),
        )(*operands)
        pressure, residual = pl.pallas_call(
            copy_kernel,
            out_shape=[jax.ShapeDtypeStruct(field, jnp.float32)] * 2,
            in_specs=[vmem, vmem],
            out_specs=[vmem, vmem],
            compiler_params=pltpu.CompilerParams(vmem_limit_bytes=60 * 1024 * 1024),
        )(pressure, residual)
        return pressure.reshape(shape), residual.reshape(shape)

    return jax.shard_map(
        on_device, mesh=mesh, in_specs=(spec, spec), out_specs=(spec, spec), check_vma=False
    )
```

```python
import functools
import math

import jax
import jax.numpy as jnp
import numpy as np
from jax import lax
from jax.experimental import pallas as pl
from jax.experimental.pallas import tpu as pltpu
from jax.sharding import PartitionSpec as P

MESH = pl.DeviceIdType.MESH
stretch = (1.0, 64.0, 1.0)
DIRS = ((-1, 0), (1, 0), (0, -1), (0, 1), (-1, -1), (-1, 1), (1, -1), (1, 1))


def legendre_value(order, position):
    prev_value = 1.0
    this_value = position
    for degree_now in range(2, order + 1):
        next_value = (
            (2 * degree_now - 1) * position * this_value - (degree_now - 1) * prev_value
        ) / degree_now
        prev_value = this_value
        this_value = next_value
    return this_value


def gll_points():
    points = [-1.0]
    for node_index in range(1, 7):
        position = -math.cos(math.pi * node_index / 7.0)
        for newton_step in range(60):
            target = legendre_value(8, position) - legendre_value(6, position)
            slope = 15.0 * legendre_value(7, position)
            position = position - target / slope
        points.append(position)
    points.append(1.0)
    return points


def jacobi_eigen(matrix_in):
    order_n = len(matrix_in)
    work_mat = [list(one_row) for one_row in matrix_in]
    vectors = [
        [1.0 if row_index == col_index else 0.0 for col_index in range(order_n)]
        for row_index in range(order_n)
    ]
    for sweep_index in range(40):
        for first_idx in range(order_n):
            for second_idx in range(first_idx + 1, order_n):
                rotation = 0.5 * math.atan2(
                    2.0 * work_mat[first_idx][second_idx],
                    work_mat[second_idx][second_idx] - work_mat[first_idx][first_idx],
                )
                cosine = math.cos(rotation)
                sine_part = math.sin(rotation)
                for other in range(order_n):
                    left_val = work_mat[other][first_idx]
                    right_val = work_mat[other][second_idx]
                    work_mat[other][first_idx] = cosine * left_val - sine_part * right_val
                    work_mat[other][second_idx] = sine_part * left_val + cosine * right_val
                for other in range(order_n):
                    left_val = work_mat[first_idx][other]
                    right_val = work_mat[second_idx][other]
                    work_mat[first_idx][other] = cosine * left_val - sine_part * right_val
                    work_mat[second_idx][other] = sine_part * left_val + cosine * right_val
                for other in range(order_n):
                    left_val = vectors[other][first_idx]
                    right_val = vectors[other][second_idx]
                    vectors[other][first_idx] = cosine * left_val - sine_part * right_val
                    vectors[other][second_idx] = sine_part * left_val + cosine * right_val
    return ([work_mat[diag_index][diag_index] for diag_index in range(order_n)], vectors)


def spectral_tables():
    nodes = gll_points()
    values_at = [legendre_value(7, position) for position in nodes]
    weights = [2.0 / (56.0 * value_now * value_now) for value_now in values_at]
    derivative = np.zeros((8, 8))
    for row in range(8):
        for col in range(8):
            if row != col:
                derivative[row, col] = values_at[row] / (
                    values_at[col] * (nodes[row] - nodes[col])
                )
    derivative[0, 0] = -14.0
    derivative[7, 7] = 14.0
    weights = np.array(weights)
    stiffness = derivative.T @ np.diag(weights) @ derivative
    stiffness[0, 0] *= 2.0
    stiffness[7, 7] *= 2.0
    inv_root = 1.0 / np.sqrt(weights)
    symmetric = inv_root[:, None] * stiffness * inv_root[None, :]
    eigen_values, eigen_vectors = jacobi_eigen(symmetric.tolist())
    fdm_basis = inv_root[:, None] * np.array(eigen_vectors)
    nodes = np.array(nodes)
    hats = np.stack([(1.0 - nodes) / 2.0, (1.0 + nodes) / 2.0])
    return weights, derivative, fdm_basis, np.array(eigen_values), hats


def sine_table(cells):
    ids = np.arange(cells + 1)
    table = math.sqrt(2.0 / cells) * np.sin(math.pi * (np.outer(ids, ids) % (2 * cells)) / cells)
    table[0] = table[-1] = 0.0
    table[:, 0] = table[:, -1] = 0.0
    return table


def mode_values(cells):
    cosines = np.cos(math.pi * np.arange(1, cells) / cells)
    return (2.0 - 2.0 * cosines) / 2.0, 2.0 * (4.0 + 2.0 * cosines) / 6.0


def round_up(value, step):
    return -(-value // step) * step


def halves(table):
    table = np.asarray(table, np.float32)
    high = table.astype(jnp.bfloat16)
    low = (table - high.astype(np.float32)).astype(jnp.bfloat16)
    return np.concatenate([high, low], axis=0)


def pieces(table, count):
    table = np.asarray(table, np.float32)
    found = []
    for _ in range(count):
        found.append(table.astype(jnp.bfloat16))
        table = table - found[-1].astype(np.float32)
    return np.concatenate(found + [found[0]], axis=1)


def sixfold(table, axis):
    table = np.asarray(table, np.float32)
    found = []
    for _ in range(3):
        found.append(table.astype(jnp.bfloat16))
        table = table - found[-1].astype(np.float32)
    return np.concatenate([found[n] for n in (0, 1, 2, 0, 1, 0)], axis=axis)


def element_tables():
    weights, derivative, basis, eigen, hats = spectral_tables()
    eye = np.eye(8)
    cube = np.kron(np.kron(basis, basis), basis)
    total = (
        stretch[0] * eigen[:, None, None]
        + stretch[1] * eigen[None, :, None]
        + stretch[2] * eigen[None, None, :]
    ).reshape(-1)
    solve = (cube / total) @ cube.T
    along_j = np.kron(np.eye(4), np.kron(derivative, eye))
    along_k = np.kron(np.eye(4), np.kron(eye, derivative))
    forward = np.concatenate([along_j, along_k], axis=0)
    backward = np.concatenate([stretch[1] * along_j.T, stretch[2] * along_k.T], axis=1)
    corner = np.stack(
        [
            np.kron(np.kron(hats[a], hats[b]), hats[c])
            for c in range(2)
            for a in range(2)
            for b in range(2)
        ]
    )
    node = np.arange(512).reshape(8, 8, 8)
    faces = [node[:, 0], node[:, 7], node[0], node[7]]
    solve_faces = solve[np.stack(faces).reshape(-1)]
    solve_inner = solve[node[1:7, 1:7].reshape(-1)]
    node = node[:4]
    outer = [node[:, [0, 7]], node[[0, 3], 1:7]]
    backward_outer = backward[np.concatenate([rows.reshape(-1) for rows in outer])]
    backward_inner = backward[node[1:3, 1:7].reshape(-1)]
    return (
        weights, derivative, solve_faces, solve_inner,
        forward, backward_outer, backward_inner, corner,
    )


def coarse_tables(size_x, size_y, depth):
    sine_x, sine_y, sine_z = sine_table(size_x), sine_table(size_y), sine_table(depth)
    modes = (size_x - 1) * (size_y - 1)
    rows = round_up(modes + 2, 8)
    waves_y = size_y - 1
    rows_y = round_up(2 * waves_y + 2, 8)
    along_y = np.zeros((rows_y, size_y, 4))
    along_x = np.zeros((rows, size_x, rows_y))
    for a in range(2):
        for y in range(size_y):
            for b in range(2):
                along_y[a : 2 * waves_y : 2, y, 2 * a + b] = sine_y[1:-1, y + b]
        for x in range(size_x):
            for n in range(waves_y):
                along_x[n : modes : waves_y, x, 2 * n + a] = sine_x[1:-1, x + a]
    for q in range(2):
        along_y[2 * waves_y + q, :, q] = 1.0
        along_x[modes + q, :, 2 * waves_y + q] = 1.0
    direct = np.zeros((rows, size_x, size_y, 4))
    for x in range(size_x):
        for y in range(size_y):
            for a in range(2):
                for b in range(2):
                    direct[:modes, x, y, 2 * a + b] = np.outer(
                        sine_x[1:-1, x + a], sine_y[1:-1, y + b]
                    ).reshape(-1)
    for q in range(2):
        direct[modes + q, :, :, q] = 1.0
    stiff_x, mass_x = mode_values(size_x)
    stiff_y, mass_y = mode_values(size_y)
    stiff_z, mass_z = mode_values(depth)
    denominator = (
        stretch[0] * stiff_x[:, None, None] * mass_y[None, :, None] * mass_z[None, None, :]
        + stretch[1] * mass_x[:, None, None] * stiff_y[None, :, None] * mass_z[None, None, :]
        + stretch[2] * mass_x[:, None, None] * mass_y[None, :, None] * stiff_z[None, None, :]
    )
    inverse = np.zeros((rows, depth))
    inverse[:modes, 1:] = (1.0 / denominator).reshape(modes, depth - 1)
    back = np.zeros((size_x, size_y, 16, rows))
    for x in range(size_x):
        for y in range(size_y):
            for c in range(2):
                for a in range(2):
                    for b in range(2):
                        back[x, y, 4 * c + 2 * a + b, :modes] = np.outer(
                            sine_x[1:-1, x + a], sine_y[1:-1, y + b]
                        ).reshape(-1)
    return (
        along_y.reshape(rows_y, -1),
        along_x.reshape(rows, -1),
        direct.reshape(rows, -1),
        inverse,
        back.reshape(size_x * size_y, 16, rows),
        sine_z[:depth, :depth],
    )


def parts(field):
    high = field.astype(jnp.bfloat16)
    return high, (field - high.astype(jnp.float32)).astype(jnp.bfloat16)


def both_dot(left, right):
    rows, lanes = left.shape[0], right.shape[1]
    sums = jnp.dot(
        jnp.concatenate(parts(left), axis=0),
        jnp.concatenate(parts(right), axis=1),
        preferred_element_type=jnp.float32,
    )
    return (sums[:rows, :lanes] + sums[rows:, :lanes]) + (sums[:rows, lanes:] + sums[rows:, lanes:])


def split_dot(table, field):
    lanes = field.shape[1]
    rows = table.shape[0] // 2
    high = field.astype(jnp.bfloat16)
    low = (field - high.astype(jnp.float32)).astype(jnp.bfloat16)
    both = jnp.concatenate([high, low], axis=1)
    top = jnp.dot(table[:rows], both, preferred_element_type=jnp.float32)
    bottom = jnp.dot(table[rows:], both, preferred_element_type=jnp.float32)
    return (top[:, :lanes] + bottom[:, :lanes]) + (top[:, lanes:] + bottom[:, lanes:])


def six_parts(value, axis):
    found = []
    for _ in range(3):
        found.append(value.astype(jnp.bfloat16).astype(jnp.float32))
        value = value - found[-1]
    order = [found[n] for n in (0, 0, 0, 1, 1, 2)]
    return jnp.concatenate(order, axis=axis).astype(jnp.bfloat16)


def table_dot(table, value):
    return jnp.dot(table, six_parts(value, 0), preferred_element_type=jnp.float32)


def dot_table(value, table):
    return jnp.dot(six_parts(value, 1), table, preferred_element_type=jnp.float32)


def wide_dot(table, field):
    high, low = parts(field)
    pieces = table.shape[1] // field.shape[0]
    return jnp.dot(
        table,
        jnp.concatenate([high] * (pieces - 1) + [low], axis=0),
        preferred_element_type=jnp.float32,
    )


def copy_kernel(p_in, r_in, p_out, r_out):
    p_out[...] = p_in[...]
    r_out[...] = r_in[...]


def kernel(size_x, size_y, weights, derivative, modes, *refs):
    n_in = 16
    inputs, (p_ref, r_ref) = refs[:n_in], refs[n_in : n_in + 2]
    local = refs[n_in + 2 : 2 * n_in + 2]
    (
        cw, faces, base, first, second, image, alpha, beta_raw, smooth, flux_i,
        rx, ry, re, mine_y, got_y, mine_x, got_x, mine_s, got_s, mine_a, got_a,
        in_sem, halo_send, halo_recv, y_send, y_recv, x_send, x_recv, s_send, s_recv, a_send, a_recv,
    ) = refs[2 * n_in + 2 :]
    (
        f_ref, corner_ref, coef_ref, weight_ref, solve_faces_ref, solve_inner_ref,
        forward_ref, backward_outer_ref, backward_inner_ref,
        along_y_ref, along_x_ref, direct_ref, sine_ref, inverse_ref, back_ref, spread_ref,
    ) = local
    lanes = f_ref.shape[2]
    my_x = lax.axis_index("gx")
    my_y = lax.axis_index("gy")
    me = my_x * size_y + my_y

    fetches = [
        pltpu.make_async_copy(
            inputs[n].at[me] if local[n] is back_ref else inputs[n], local[n], in_sem.at[n]
        )
        for n in range(n_in)
    ]
    for fetch in fetches:
        fetch.start()

    def exists(direction):
        dx, dy = direction
        ok = None
        for pos, size, step in ((my_x, size_x, dx), (my_y, size_y, dy)):
            if step:
                cond = pos > 0 if step < 0 else pos < size - 1
                ok = cond if ok is None else jnp.logical_and(ok, cond)
        return ok

    def peers_y():
        for offset in range(1, size_y):
            other = my_y + offset
            yield (my_x, jnp.where(other >= size_y, other - size_y, other))

    def peers_x():
        for offset in range(1, size_x):
            other = my_x + offset
            yield (jnp.where(other >= size_x, other - size_x, other), my_y)

    def peers_all():
        for offset_y in range(size_y - 1, -1, -1):
            other_y = my_y + offset_y
            other_y = jnp.where(other_y >= size_y, other_y - size_y, other_y)
            for offset_x in range(0 if offset_y else 1, size_x):
                other_x = my_x + offset_x
                yield (jnp.where(other_x >= size_x, other_x - size_x, other_x), other_y)

    barrier = pltpu.get_barrier_semaphore()
    count = jnp.int32(size_x - 1 + size_y - 1)
    for direction in DIRS[4:]:
        here = exists(direction)

        @pl.when(here)
        def _(direction=direction):
            pl.semaphore_signal(
                barrier,
                inc=1,
                device_id=(my_x + direction[0], my_y + direction[1]),
                device_id_type=MESH,
            )

        count = count + here.astype(jnp.int32)
    for other in [*peers_y(), *peers_x()]:
        pl.semaphore_signal(barrier, inc=1, device_id=other, device_id_type=MESH)

    def node_rows(step):
        return 0 if step < 0 else 7

    def source(direction):
        dx, dy = direction
        if dy == 0:
            return faces.at[2 + (dx > 0)]
        if dx == 0:
            return faces.at[int(dy > 0)]
        return faces.at[2 + (dx > 0), pl.ds(8 * node_rows(dy), 8)]

    def landing(turn, index):
        if index < 2:
            return rx.at[turn, index]
        if index < 4:
            return ry.at[turn, index - 2]
        return re.at[turn, index - 4]

    def halo_copy(turn, index):
        direction = DIRS[index]
        opposite = DIRS.index((-direction[0], -direction[1]))
        return pltpu.make_async_remote_copy(
            src_ref=source(direction),
            dst_ref=landing(turn, opposite),
            send_sem=halo_send.at[turn, index],
            recv_sem=halo_recv.at[turn, opposite],
            device_id=(my_x + direction[0], my_y + direction[1]),
            device_id_type=MESH,
        )

    def halo_arrival(turn, index):
        direction = DIRS[index]
        return pltpu.make_async_remote_copy(
            src_ref=source(direction),
            dst_ref=landing(turn, index),
            send_sem=halo_send.at[turn, index],
            recv_sem=halo_recv.at[turn, index],
            device_id=(my_x + direction[0], my_y + direction[1]),
            device_id_type=MESH,
        )

    def sum_depth(ref):
        count = ref.shape[0]
        lane = lax.broadcasted_iota(jnp.int32, (count, 8, lanes), 2)
        head = ref[:, pl.ds(0, 8, stride=8), :]
        tail = ref[:, pl.ds(7, 8, stride=8), :]
        rows = (8 * count, lanes)
        from_tail = pltpu.roll(tail.reshape(rows), 1, 1).reshape(lane.shape)
        from_head = pltpu.roll(head.reshape(rows), lanes - 1, 1).reshape(lane.shape)
        ref[:, pl.ds(0, 8, stride=8), :] = jnp.where(lane == 0, 0.0, head + from_tail)
        ref[:, pl.ds(7, 8, stride=8), :] = jnp.where(lane == lanes - 1, 0.0, tail + from_head)

    def send_faces(turn, raw_ref):
        for side in range(2):
            faces[side] = raw_ref[:, pl.ds(56 * side, 8)].reshape(64, lanes)
            faces[2 + side] = raw_ref[7 * side]
        sum_depth(faces)
        send_halo(turn)

    def fill_inner(target, raw):
        target[pl.ds(1, 6), pl.ds(8, 48)] = raw
        sum_depth(target)

    def send_halo(turn):
        for index in (2, 3, 4, 5, 6, 7, 0, 1):
            @pl.when(exists(DIRS[index]))
            def _(index=index):
                halo_copy(turn, index).start()

    def take_halo(turn, target):
        for index in range(8):
            @pl.when(exists(DIRS[index]))
            def _(index=index):
                halo_copy(turn, index).wait_send()
                halo_arrival(turn, index).wait_recv()

        has = [exists(direction) for direction in DIRS[:4]]
        for side in range(2):
            i = 7 * side
            target[i, pl.ds(8, 48)] = jnp.where(
                has[side],
                faces[2 + side, pl.ds(8, 48)] + rx[turn, side, pl.ds(8, 48)],
                0.0,
            )
            target[pl.ds(1, 6), pl.ds(8 * i, 8)] = jnp.where(
                has[2 + side],
                faces[side, pl.ds(8, 48)] + ry[turn, side, pl.ds(8, 48)],
                0.0,
            ).reshape(6, 8, lanes)
            for other in range(2):
                j = 7 * other
                target[i, pl.ds(8 * j, 8)] = jnp.where(
                    jnp.logical_and(has[side], has[2 + other]),
                    (faces[2 + side, pl.ds(8 * j, 8)] + rx[turn, side, pl.ds(8 * j, 8)])
                    + (ry[turn, other, pl.ds(8 * i, 8)] + re[turn, 2 * side + other]),
                    0.0,
                )

    def send_to(peers, me_there, message, got, send, recv, value):
        message[...] = value
        got[me_there] = value
        for other in peers:
            pltpu.make_async_remote_copy(
                src_ref=message,
                dst_ref=got.at[me_there],
                send_sem=send,
                recv_sem=recv,
                device_id=other,
                device_id_type=MESH,
            ).start()

    def take_from(size, got, send, recv):
        span = got.at[pl.ds(0, size - 1)]
        copy = pltpu.make_async_remote_copy(
            src_ref=span,
            dst_ref=span,
            send_sem=send,
            recv_sem=recv,
            device_id=(jnp.where(my_x == 0, 1, 0), my_y),
            device_id_type=MESH,
        )
        copy.wait_send()
        copy.wait_recv()
        return got[...]

    def send_y(turn, value):
        send_to(
            peers_y(), my_y, mine_y.at[turn], got_y.at[turn],
            y_send.at[turn], y_recv.at[turn], value,
        )

    def take_y(turn):
        return take_from(size_y, got_y.at[turn], y_send.at[turn], y_recv.at[turn])

    def send_x(turn, value):
        send_to(
            peers_x(), my_x, mine_x.at[turn], got_x.at[turn],
            x_send.at[turn], x_recv.at[turn], value,
        )

    def take_x(turn):
        return take_from(size_x, got_x.at[turn], x_send.at[turn], x_recv.at[turn])

    def pass_on(turn):
        send_x(turn, table_dot(along_y_ref[...], take_y(turn).reshape(size_y * 4, lanes)))

    row = lax.broadcasted_iota(jnp.int32, (8, lanes), 0)
    row4 = lax.broadcasted_iota(jnp.int32, (4, lanes), 0)
    lane4 = lax.broadcasted_iota(jnp.int32, (4, lanes), 1)

    def corner_message(raw):
        corners = both_dot(corner_ref[...], raw)
        moved = pltpu.roll(pltpu.roll(corners, 1, 1), 4, 0)
        return (corners + moved)[:4]

    def coarse_values(turn):
        if turn == 0:
            gathered = take_x(turn)
            gathered = gathered.reshape(size_x * gathered.shape[1], lanes)
            combined = table_dot(along_x_ref[...], gathered)
        else:
            gathered = take_from(size_x * size_y, got_a, a_send, a_recv)
            combined = table_dot(direct_ref[...], gathered.reshape(-1, lanes))
        spectral = dot_table(combined, sine_ref[...]) * inverse_ref[...]
        mine = table_dot(back_ref[...], spectral)[:8]
        columns = dot_table(mine, sine_ref[...])
        corners = jnp.where(row < 4, columns, pltpu.roll(columns, lanes - 1, 1))
        return table_dot(spread_ref[...], corners), combined

    def solve_and_send(turn, field):
        faces[...] = split_dot(solve_faces_ref[...], field).reshape(4, 64, lanes)
        sum_depth(faces)
        send_halo(turn)

    def solve_inner(field, target):
        fill_inner(target, split_dot(solve_inner_ref[...], field).reshape(6, 48, lanes))

    def fluxes(field_ref):
        values = field_ref[...] - field_ref[:, pl.ds(27, 1)]
        grads = wide_dot(
            forward_ref[...],
            jnp.concatenate(
                [values[:4].reshape(256, lanes), values[4:].reshape(256, lanes)], axis=1
            ),
        )
        factor = jnp.concatenate(
            [cw[pl.ds(0, 4)].reshape(256, lanes), cw[pl.ds(4, 4)].reshape(256, lanes)], axis=1
        )
        grads_j, grads_k = grads[:256], grads[256:]
        flux_j, flux_k = grads_j * factor, grads_k * factor
        energy = stretch[1] * (grads_j * flux_j) + stretch[2] * (grads_k * flux_k)
        energy = jnp.sum(energy.reshape(32, 8, 2 * lanes), axis=0)
        energy = energy[:, :lanes] + energy[:, lanes:]
        for part in range(8):
            span = pl.ds(8 * part, 8)
            nodal = [field_ref[i, span] for i in range(8)]
            for p in range(8):
                grad = nodal[0] * derivative[p][0]
                for i in range(1, 8):
                    grad = grad + nodal[i] * derivative[p][i]
                flux = grad * cw[p, span]
                flux_i[p, span] = flux
                energy = energy + grad * flux
        return jnp.concatenate([flux_j, flux_k], axis=0), energy

    def divergence(flux, target, tiles, product, place):
        for j in range(8):
            span = pl.ds(8 * j, 8)
            along_i = [flux_i[p, span] for p in range(8)]
            for i in range(8):
                if (i, j) not in tiles:
                    continue
                row_at, lane_at = place(i % 4, j), lanes * (i // 4)
                total = product[row_at : row_at + 8, lane_at : lane_at + lanes]
                for p in range(8):
                    total = total + along_i[p] * derivative[p][i]
                target[i, span] = total

    all_tiles = [(i, j) for i in range(8) for j in range(8)]
    inner_tiles = [(i, j) for i, j in all_tiles if 0 < i < 7 and 0 < j < 7]
    face_tiles = [tile for tile in all_tiles if tile not in inner_tiles]

    def outer_place(i, j):
        if j in (0, 7):
            return 8 * (2 * i + (j == 7))
        return 64 + 8 * (6 * (i == 3) + j - 1)

    def operate(turn, flux, raw, target, then=None):
        outer = wide_dot(backward_outer_ref[...], flux)
        divergence(flux, raw, face_tiles, outer, outer_place)
        send_faces(turn, raw)
        middle = wide_dot(backward_inner_ref[...], flux)
        ends = [(i, j) for i, j in inner_tiles if i in (3, 4)]
        rest = [(i, j) for i, j in inner_tiles if i not in (3, 4)]
        divergence(flux, raw, ends, outer, outer_place)
        divergence(flux, raw, rest, middle, lambda i, j: 8 * (6 * (i - 1) + j - 1))
        if then:
            then()
        fill_inner(target, raw[pl.ds(1, 6), pl.ds(8, 48)])

    def partial(left, right):
        return jnp.sum((left * right).reshape(64, 8, lanes), axis=0)

    def row_sum(tile):
        return jnp.sum(tile, axis=0, keepdims=True)

    def total(rows):
        return jnp.sum(rows, axis=(0, 1), keepdims=True)

    fetches[0].wait()
    pl.semaphore_wait(barrier, count)
    send_faces(0, f_ref)
    fetches[1].wait()
    send_y(0, corner_message(f_ref[...].reshape(512, lanes)))
    fill_inner(base, f_ref[pl.ds(1, 6), pl.ds(8, 48)])
    fetches[2].wait()
    fetches[3].wait()
    for i in range(8):
        cw[i] = coef_ref[i] * (weight_ref[...] * weights[i])
    fetches[4].wait()
    take_halo(0, base)

    field = base[...].reshape(512, lanes)
    solve_and_send(1, field)
    for fetch in fetches[5:]:
        fetch.wait()
    pass_on(0)
    solve_inner(field, first)
    coarse, _ = coarse_values(0)
    take_halo(1, first)
    first[...] += coarse.reshape(8, 64, lanes)

    flux, curve_part = fluxes(first)

    def send_residual():
        message = corner_message(alpha[...].reshape(512, lanes))
        scalars = jnp.where(
            row4 == 0,
            total(partial(f_ref[...], first[...])),
            jnp.where(row4 == 1, total(curve_part), 0.0),
        )
        message = jnp.where(lane4 == 0, scalars, message)
        send_to(peers_all(), me, mine_a, got_a, a_send, a_recv, message)

    operate(2, flux, alpha, image, send_residual)
    take_halo(2, image)

    field = image[...].reshape(512, lanes)
    solve_and_send(3, field)
    solve_inner(field, smooth)
    coarse, combined = coarse_values(1)
    energy = combined[modes : modes + 1, 0:1]
    curve = combined[modes + 1 : modes + 2, 0:1]
    step = energy / curve
    step3 = step.reshape(1, 1, 1)
    take_halo(3, smooth)
    second[...] = first[...] - step3 * (smooth[...] + coarse.reshape(8, 64, lanes))

    fresh = row_sum(partial(f_ref[...] - step3 * alpha[...], second[...]))
    cross = row_sum(partial(alpha[...], second[...]))
    flux, along = fluxes(second)
    along = row_sum(along)
    sums = jnp.where(
        row4 == 0, fresh, jnp.where(row4 == 1, along, jnp.where(row4 == 2, cross, 0.0))
    )
    send_to(peers_all(), me, mine_s, got_s, s_send, s_recv, sums)
    operate(4, flux, beta_raw, smooth)
    take_halo(4, smooth)
    sums = jnp.sum(take_from(size_x * size_y, got_s, s_send, s_recv), axis=0)
    fresh = total(sums[0:1])
    ratio = fresh / energy
    along = total(sums[1:2]) + 2.0 * ratio * total(sums[2:3]) + ratio * ratio * curve
    second_step = fresh / along
    ratio3 = ratio.reshape(1, 1, 1)
    second3 = second_step.reshape(1, 1, 1)
    p_ref[...] = step3 * first[...] + second3 * (second[...] + ratio3 * first[...])
    r_ref[...] = (base[...] - step3 * image[...]) - second3 * (smooth[...] + ratio3 * image[...])


def solution(mesh):
    size_x, size_y = mesh.shape["gx"], mesh.shape["gy"]
    (
        weights, derivative, solve_faces, solve_inner,
        forward, backward_outer, backward_inner, corner,
    ) = element_tables()
    spec = P(None, None, None, "gx", "gy", None)

    def on_device(forcing, coefficient):
        shape = forcing.shape
        depth = shape[5]
        along_y, along_x, direct, inverse, back, sine = coarse_tables(size_x, size_y, depth)
        modes = (size_x - 1) * (size_y - 1)
        plane = np.outer(weights, weights).reshape(64, 1) * np.ones((1, depth))
        field = (8, 64, depth)
        operands = [
            forcing.reshape(field),
            np.asarray(corner, np.float32),
            coefficient.reshape(field),
            np.asarray(plane, np.float32),
            halves(solve_faces),
            halves(solve_inner),
            pieces(forward, 3),
            pieces(backward_outer, 2),
            pieces(backward_inner, 2),
            sixfold(along_y, 1),
            sixfold(along_x, 1),
            sixfold(direct, 1),
            sixfold(sine, 0),
            np.asarray(inverse, np.float32),
            sixfold(back, 2),
            sixfold(corner.T, 1),
        ]
        shapes = [op.shape for op in operands]
        shapes[14] = shapes[14][1:]
        rows_y = along_y.shape[0]
        vmem = pl.BlockSpec(memory_space=pltpu.VMEM)
        pressure, residual = pl.pallas_call(
            functools.partial(
                kernel, size_x, size_y, weights.tolist(), derivative.tolist(), modes
            ),
            out_shape=[jax.ShapeDtypeStruct(field, jnp.float32)] * 2,
            in_specs=[pl.BlockSpec(memory_space=pltpu.HBM)] * len(operands),
            out_specs=[vmem, vmem],
            scratch_shapes=[pltpu.VMEM(dims, op.dtype) for dims, op in zip(shapes, operands)]
            + [pltpu.VMEM(field, jnp.float32)]
            + [pltpu.VMEM((4, 64, depth), jnp.float32)]
            + [pltpu.VMEM(field, jnp.float32)] * 8
            + [
                pltpu.VMEM((5, 2, 64, depth), jnp.float32),
                pltpu.VMEM((5, 2, 64, depth), jnp.float32),
                pltpu.VMEM((5, 4, 8, depth), jnp.float32),
                pltpu.VMEM((2, 4, depth), jnp.float32),
                pltpu.VMEM((2, size_y, 4, depth), jnp.float32),
                pltpu.VMEM((2, rows_y, depth), jnp.float32),
                pltpu.VMEM((2, size_x, rows_y, depth), jnp.float32),
                pltpu.VMEM((4, depth), jnp.float32),
                pltpu.VMEM((size_x * size_y, 4, depth), jnp.float32),
                pltpu.VMEM((4, depth), jnp.float32),
                pltpu.VMEM((size_x * size_y, 4, depth), jnp.float32),
                pltpu.SemaphoreType.DMA((len(operands),)),
                pltpu.SemaphoreType.DMA((5, 8)),
                pltpu.SemaphoreType.DMA((5, 8)),
                pltpu.SemaphoreType.DMA((2,)),
                pltpu.SemaphoreType.DMA((2,)),
                pltpu.SemaphoreType.DMA((2,)),
                pltpu.SemaphoreType.DMA((2,)),
                pltpu.SemaphoreType.DMA(()),
                pltpu.SemaphoreType.DMA(()),
                pltpu.SemaphoreType.DMA(()),
                pltpu.SemaphoreType.DMA(()),
            ],
            compiler_params=pltpu.CompilerParams(
                collective_id=0, has_side_effects=True, vmem_limit_bytes=60 * 1024 * 1024
            ),
        )(*operands)
        pressure, residual = pl.pallas_call(
            copy_kernel,
            out_shape=[jax.ShapeDtypeStruct(field, jnp.float32)] * 2,
            in_specs=[vmem, vmem],
            out_specs=[vmem, vmem],
            compiler_params=pltpu.CompilerParams(vmem_limit_bytes=60 * 1024 * 1024),
        )(pressure, residual)
        return pressure.reshape(shape), residual.reshape(shape)

    return jax.shard_map(
        on_device, mesh=mesh, in_specs=(spec, spec), out_specs=(spec, spec), check_vma=False
    )
```

```python
import functools
import math

import jax
import jax.numpy as jnp
import numpy as np
from jax import lax
from jax.experimental import pallas as pl
from jax.experimental.pallas import tpu as pltpu
from jax.sharding import PartitionSpec as P

MESH = pl.DeviceIdType.MESH
stretch = (1.0, 64.0, 1.0)
DIRS = ((-1, 0), (1, 0), (0, -1), (0, 1), (-1, -1), (-1, 1), (1, -1), (1, 1))


def legendre_value(order, position):
    prev_value = 1.0
    this_value = position
    for degree_now in range(2, order + 1):
        next_value = (
            (2 * degree_now - 1) * position * this_value - (degree_now - 1) * prev_value
        ) / degree_now
        prev_value = this_value
        this_value = next_value
    return this_value


def gll_points():
    points = [-1.0]
    for node_index in range(1, 7):
        position = -math.cos(math.pi * node_index / 7.0)
        for newton_step in range(60):
            target = legendre_value(8, position) - legendre_value(6, position)
            slope = 15.0 * legendre_value(7, position)
            position = position - target / slope
        points.append(position)
    points.append(1.0)
    return points


def jacobi_eigen(matrix_in):
    order_n = len(matrix_in)
    work_mat = [list(one_row) for one_row in matrix_in]
    vectors = [
        [1.0 if row_index == col_index else 0.0 for col_index in range(order_n)]
        for row_index in range(order_n)
    ]
    for sweep_index in range(40):
        for first_idx in range(order_n):
            for second_idx in range(first_idx + 1, order_n):
                rotation = 0.5 * math.atan2(
                    2.0 * work_mat[first_idx][second_idx],
                    work_mat[second_idx][second_idx] - work_mat[first_idx][first_idx],
                )
                cosine = math.cos(rotation)
                sine_part = math.sin(rotation)
                for other in range(order_n):
                    left_val = work_mat[other][first_idx]
                    right_val = work_mat[other][second_idx]
                    work_mat[other][first_idx] = cosine * left_val - sine_part * right_val
                    work_mat[other][second_idx] = sine_part * left_val + cosine * right_val
                for other in range(order_n):
                    left_val = work_mat[first_idx][other]
                    right_val = work_mat[second_idx][other]
                    work_mat[first_idx][other] = cosine * left_val - sine_part * right_val
                    work_mat[second_idx][other] = sine_part * left_val + cosine * right_val
                for other in range(order_n):
                    left_val = vectors[other][first_idx]
                    right_val = vectors[other][second_idx]
                    vectors[other][first_idx] = cosine * left_val - sine_part * right_val
                    vectors[other][second_idx] = sine_part * left_val + cosine * right_val
    return ([work_mat[diag_index][diag_index] for diag_index in range(order_n)], vectors)


def spectral_tables():
    nodes = gll_points()
    values_at = [legendre_value(7, position) for position in nodes]
    weights = [2.0 / (56.0 * value_now * value_now) for value_now in values_at]
    derivative = np.zeros((8, 8))
    for row in range(8):
        for col in range(8):
            if row != col:
                derivative[row, col] = values_at[row] / (
                    values_at[col] * (nodes[row] - nodes[col])
                )
    derivative[0, 0] = -14.0
    derivative[7, 7] = 14.0
    weights = np.array(weights)
    stiffness = derivative.T @ np.diag(weights) @ derivative
    stiffness[0, 0] *= 2.0
    stiffness[7, 7] *= 2.0
    inv_root = 1.0 / np.sqrt(weights)
    symmetric = inv_root[:, None] * stiffness * inv_root[None, :]
    eigen_values, eigen_vectors = jacobi_eigen(symmetric.tolist())
    fdm_basis = inv_root[:, None] * np.array(eigen_vectors)
    nodes = np.array(nodes)
    hats = np.stack([(1.0 - nodes) / 2.0, (1.0 + nodes) / 2.0])
    return weights, derivative, fdm_basis, np.array(eigen_values), hats


def sine_table(cells):
    ids = np.arange(cells + 1)
    table = math.sqrt(2.0 / cells) * np.sin(math.pi * (np.outer(ids, ids) % (2 * cells)) / cells)
    table[0] = table[-1] = 0.0
    table[:, 0] = table[:, -1] = 0.0
    return table


def mode_values(cells):
    cosines = np.cos(math.pi * np.arange(1, cells) / cells)
    return (2.0 - 2.0 * cosines) / 2.0, 2.0 * (4.0 + 2.0 * cosines) / 6.0


def round_up(value, step):
    return -(-value // step) * step


def halves(table):
    table = np.asarray(table, np.float32)
    high = table.astype(jnp.bfloat16)
    low = (table - high.astype(np.float32)).astype(jnp.bfloat16)
    return np.concatenate([high, low], axis=0)


def pieces(table, count):
    table = np.asarray(table, np.float32)
    found = []
    for _ in range(count):
        found.append(table.astype(jnp.bfloat16))
        table = table - found[-1].astype(np.float32)
    return np.concatenate(found + [found[0]], axis=1)


def sixfold(table, axis):
    table = np.asarray(table, np.float32)
    found = []
    for _ in range(3):
        found.append(table.astype(jnp.bfloat16))
        table = table - found[-1].astype(np.float32)
    return np.concatenate([found[n] for n in (0, 1, 2, 0, 1, 0)], axis=axis)


def element_tables():
    weights, derivative, basis, eigen, hats = spectral_tables()
    eye = np.eye(8)
    cube = np.kron(np.kron(basis, basis), basis)
    total = (
        stretch[0] * eigen[:, None, None]
        + stretch[1] * eigen[None, :, None]
        + stretch[2] * eigen[None, None, :]
    ).reshape(-1)
    solve = (cube / total) @ cube.T
    along_j = np.kron(np.eye(4), np.kron(derivative, eye))
    along_k = np.kron(np.eye(4), np.kron(eye, derivative))
    forward = np.concatenate([along_j, along_k], axis=0)
    backward = np.concatenate([stretch[1] * along_j.T, stretch[2] * along_k.T], axis=1)
    corner = np.stack(
        [
            np.kron(np.kron(hats[a], hats[b]), hats[c])
            for c in range(2)
            for a in range(2)
            for b in range(2)
        ]
    )
    node = np.arange(512).reshape(8, 8, 8)
    faces = [node[:, 0], node[:, 7], node[0], node[7]]
    solve_faces = solve[np.stack(faces).reshape(-1)]
    solve_inner = solve[node[1:7, 1:7].reshape(-1)]
    node = node[:4]
    outer = [node[:, [0, 7]], node[[0, 3], 1:7]]
    backward_outer = backward[np.concatenate([rows.reshape(-1) for rows in outer])]
    backward_inner = backward[node[1:3, 1:7].reshape(-1)]
    return (
        weights, derivative, solve_faces, solve_inner,
        forward, backward_outer, backward_inner, corner,
    )


def coarse_tables(size_x, size_y, depth):
    sine_x, sine_y, sine_z = sine_table(size_x), sine_table(size_y), sine_table(depth)
    modes = (size_x - 1) * (size_y - 1)
    rows = round_up(modes + 2, 8)
    waves_y = size_y - 1
    rows_y = round_up(2 * waves_y + 2, 8)
    along_y = np.zeros((rows_y, size_y, 4))
    along_x = np.zeros((rows, size_x, rows_y))
    for a in range(2):
        for y in range(size_y):
            for b in range(2):
                along_y[a : 2 * waves_y : 2, y, 2 * a + b] = sine_y[1:-1, y + b]
        for x in range(size_x):
            for n in range(waves_y):
                along_x[n : modes : waves_y, x, 2 * n + a] = sine_x[1:-1, x + a]
    for q in range(2):
        along_y[2 * waves_y + q, :, q] = 1.0
        along_x[modes + q, :, 2 * waves_y + q] = 1.0
    direct = np.zeros((rows, size_x, size_y, 4))
    for x in range(size_x):
        for y in range(size_y):
            for a in range(2):
                for b in range(2):
                    direct[:modes, x, y, 2 * a + b] = np.outer(
                        sine_x[1:-1, x + a], sine_y[1:-1, y + b]
                    ).reshape(-1)
    for q in range(2):
        direct[modes + q, :, :, q] = 1.0
    stiff_x, mass_x = mode_values(size_x)
    stiff_y, mass_y = mode_values(size_y)
    stiff_z, mass_z = mode_values(depth)
    denominator = (
        stretch[0] * stiff_x[:, None, None] * mass_y[None, :, None] * mass_z[None, None, :]
        + stretch[1] * mass_x[:, None, None] * stiff_y[None, :, None] * mass_z[None, None, :]
        + stretch[2] * mass_x[:, None, None] * mass_y[None, :, None] * stiff_z[None, None, :]
    )
    inverse = np.zeros((rows, depth))
    inverse[:modes, 1:] = (1.0 / denominator).reshape(modes, depth - 1)
    back = np.zeros((size_x, size_y, 16, rows))
    for x in range(size_x):
        for y in range(size_y):
            for c in range(2):
                for a in range(2):
                    for b in range(2):
                        back[x, y, 4 * c + 2 * a + b, :modes] = np.outer(
                            sine_x[1:-1, x + a], sine_y[1:-1, y + b]
                        ).reshape(-1)
    return (
        along_y.reshape(rows_y, -1),
        along_x.reshape(rows, -1),
        direct.reshape(rows, -1),
        inverse,
        back.reshape(size_x * size_y, 16, rows),
        sine_z[:depth, :depth],
    )


def parts(field):
    high = field.astype(jnp.bfloat16)
    return high, (field - high.astype(jnp.float32)).astype(jnp.bfloat16)


def both_dot(left, right):
    rows, lanes = left.shape[0], right.shape[1]
    sums = jnp.dot(
        jnp.concatenate(parts(left), axis=0),
        jnp.concatenate(parts(right), axis=1),
        preferred_element_type=jnp.float32,
    )
    return (sums[:rows, :lanes] + sums[rows:, :lanes]) + (sums[:rows, lanes:] + sums[rows:, lanes:])


def split_dot(table, field):
    lanes = field.shape[1]
    rows = table.shape[0] // 2
    high = field.astype(jnp.bfloat16)
    low = (field - high.astype(jnp.float32)).astype(jnp.bfloat16)
    both = jnp.concatenate([high, low], axis=1)
    top = jnp.dot(table[:rows], both, preferred_element_type=jnp.float32)
    bottom = jnp.dot(table[rows:], both, preferred_element_type=jnp.float32)
    return (top[:, :lanes] + bottom[:, :lanes]) + (top[:, lanes:] + bottom[:, lanes:])


def six_parts(value, axis):
    found = []
    for _ in range(3):
        found.append(value.astype(jnp.bfloat16).astype(jnp.float32))
        value = value - found[-1]
    order = [found[n] for n in (0, 0, 0, 1, 1, 2)]
    return jnp.concatenate(order, axis=axis).astype(jnp.bfloat16)


def table_dot(table, value):
    return jnp.dot(table, six_parts(value, 0), preferred_element_type=jnp.float32)


def dot_table(value, table):
    return jnp.dot(six_parts(value, 1), table, preferred_element_type=jnp.float32)


def wide_dot(table, field):
    high, low = parts(field)
    pieces = table.shape[1] // field.shape[0]
    return jnp.dot(
        table,
        jnp.concatenate([high] * (pieces - 1) + [low], axis=0),
        preferred_element_type=jnp.float32,
    )


def copy_kernel(p_in, r_in, p_out, r_out):
    p_out[...] = p_in[...]
    r_out[...] = r_in[...]


def kernel(size_x, size_y, weights, derivative, modes, *refs):
    n_in = 16
    inputs, (p_ref, r_ref) = refs[:n_in], refs[n_in : n_in + 2]
    local = refs[n_in + 2 : 2 * n_in + 2]
    (
        cw, faces, base, first, second, image, alpha, beta_raw, smooth, flux_i,
        rx, ry, re, mine_y, got_y, mine_x, got_x, mine_s, got_s, mine_a, got_a,
        in_sem, halo_send, halo_recv, y_send, y_recv, x_send, x_recv, s_send, s_recv, a_send, a_recv,
    ) = refs[2 * n_in + 2 :]
    (
        f_ref, corner_ref, coef_ref, weight_ref, solve_faces_ref, solve_inner_ref,
        forward_ref, backward_outer_ref, backward_inner_ref,
        along_y_ref, along_x_ref, direct_ref, sine_ref, inverse_ref, back_ref, spread_ref,
    ) = local
    lanes = f_ref.shape[2]
    my_x = lax.axis_index("gx")
    my_y = lax.axis_index("gy")
    me = my_x * size_y + my_y

    fetches = [
        pltpu.make_async_copy(
            inputs[n].at[me] if local[n] is back_ref else inputs[n], local[n], in_sem.at[n]
        )
        for n in range(n_in)
    ]
    for fetch in fetches:
        fetch.start()

    def exists(direction):
        dx, dy = direction
        ok = None
        for pos, size, step in ((my_x, size_x, dx), (my_y, size_y, dy)):
            if step:
                cond = pos > 0 if step < 0 else pos < size - 1
                ok = cond if ok is None else jnp.logical_and(ok, cond)
        return ok

    def peers_y():
        for offset in range(1, size_y):
            other = my_y + offset
            yield (my_x, jnp.where(other >= size_y, other - size_y, other))

    def peers_x():
        for offset in range(1, size_x):
            other = my_x + offset
            yield (jnp.where(other >= size_x, other - size_x, other), my_y)

    def peers_all():
        for offset_y in range(size_y - 1, -1, -1):
            other_y = my_y + offset_y
            other_y = jnp.where(other_y >= size_y, other_y - size_y, other_y)
            for offset_x in range(0 if offset_y else 1, size_x):
                other_x = my_x + offset_x
                yield (jnp.where(other_x >= size_x, other_x - size_x, other_x), other_y)

    barrier = pltpu.get_barrier_semaphore()
    count = jnp.int32(size_x - 1 + size_y - 1)
    for direction in DIRS[4:]:
        here = exists(direction)

        @pl.when(here)
        def _(direction=direction):
            pl.semaphore_signal(
                barrier,
                inc=1,
                device_id=(my_x + direction[0], my_y + direction[1]),
                device_id_type=MESH,
            )

        count = count + here.astype(jnp.int32)
    for other in [*peers_y(), *peers_x()]:
        pl.semaphore_signal(barrier, inc=1, device_id=other, device_id_type=MESH)

    def node_rows(step):
        return 0 if step < 0 else 7

    def source(direction):
        dx, dy = direction
        if dy == 0:
            return faces.at[2 + (dx > 0)]
        if dx == 0:
            return faces.at[int(dy > 0)]
        return faces.at[2 + (dx > 0), pl.ds(8 * node_rows(dy), 8)]

    def landing(turn, index):
        if index < 2:
            return rx.at[turn, index]
        if index < 4:
            return ry.at[turn, index - 2]
        return re.at[turn, index - 4]

    def halo_copy(turn, index):
        direction = DIRS[index]
        opposite = DIRS.index((-direction[0], -direction[1]))
        return pltpu.make_async_remote_copy(
            src_ref=source(direction),
            dst_ref=landing(turn, opposite),
            send_sem=halo_send.at[turn, index],
            recv_sem=halo_recv.at[turn, opposite],
            device_id=(my_x + direction[0], my_y + direction[1]),
            device_id_type=MESH,
        )

    def halo_arrival(turn, index):
        direction = DIRS[index]
        return pltpu.make_async_remote_copy(
            src_ref=source(direction),
            dst_ref=landing(turn, index),
            send_sem=halo_send.at[turn, index],
            recv_sem=halo_recv.at[turn, index],
            device_id=(my_x + direction[0], my_y + direction[1]),
            device_id_type=MESH,
        )

    def sum_depth(ref):
        count = ref.shape[0]
        lane = lax.broadcasted_iota(jnp.int32, (count, 8, lanes), 2)
        head = ref[:, pl.ds(0, 8, stride=8), :]
        tail = ref[:, pl.ds(7, 8, stride=8), :]
        rows = (8 * count, lanes)
        from_tail = pltpu.roll(tail.reshape(rows), 1, 1).reshape(lane.shape)
        from_head = pltpu.roll(head.reshape(rows), lanes - 1, 1).reshape(lane.shape)
        ref[:, pl.ds(0, 8, stride=8), :] = jnp.where(lane == 0, 0.0, head + from_tail)
        ref[:, pl.ds(7, 8, stride=8), :] = jnp.where(lane == lanes - 1, 0.0, tail + from_head)

    def load_faces(raw_ref):
        for side in range(2):
            faces[side] = raw_ref[:, pl.ds(56 * side, 8)].reshape(64, lanes)
            faces[2 + side] = raw_ref[7 * side]
        sum_depth(faces)

    def fill_inner(target, raw):
        target[pl.ds(1, 6), pl.ds(8, 48)] = raw
        sum_depth(target)

    def send_halo(turn):
        for index in (2, 3, 4, 5, 6, 7, 0, 1):
            @pl.when(exists(DIRS[index]))
            def _(index=index):
                halo_copy(turn, index).start()

    def take_halo(turn, target):
        for index in range(8):
            @pl.when(exists(DIRS[index]))
            def _(index=index):
                halo_copy(turn, index).wait_send()
                halo_arrival(turn, index).wait_recv()

        has = [exists(direction) for direction in DIRS[:4]]
        for side in range(2):
            i = 7 * side
            target[i, pl.ds(8, 48)] = jnp.where(
                has[side],
                faces[2 + side, pl.ds(8, 48)] + rx[turn, side, pl.ds(8, 48)],
                0.0,
            )
            target[pl.ds(1, 6), pl.ds(8 * i, 8)] = jnp.where(
                has[2 + side],
                faces[side, pl.ds(8, 48)] + ry[turn, side, pl.ds(8, 48)],
                0.0,
            ).reshape(6, 8, lanes)
            for other in range(2):
                j = 7 * other
                target[i, pl.ds(8 * j, 8)] = jnp.where(
                    jnp.logical_and(has[side], has[2 + other]),
                    (faces[2 + side, pl.ds(8 * j, 8)] + rx[turn, side, pl.ds(8 * j, 8)])
                    + (ry[turn, other, pl.ds(8 * i, 8)] + re[turn, 2 * side + other]),
                    0.0,
                )

    def send_to(peers, me_there, message, got, send, recv, value):
        message[...] = value
        got[me_there] = value
        for other in peers:
            pltpu.make_async_remote_copy(
                src_ref=message,
                dst_ref=got.at[me_there],
                send_sem=send,
                recv_sem=recv,
                device_id=other,
                device_id_type=MESH,
            ).start()

    def take_from(size, got, send, recv):
        span = got.at[pl.ds(0, size - 1)]
        copy = pltpu.make_async_remote_copy(
            src_ref=span,
            dst_ref=span,
            send_sem=send,
            recv_sem=recv,
            device_id=(jnp.where(my_x == 0, 1, 0), my_y),
            device_id_type=MESH,
        )
        copy.wait_send()
        copy.wait_recv()
        return got[...]

    def send_y(turn, value):
        send_to(
            peers_y(), my_y, mine_y.at[turn], got_y.at[turn],
            y_send.at[turn], y_recv.at[turn], value,
        )

    def take_y(turn):
        return take_from(size_y, got_y.at[turn], y_send.at[turn], y_recv.at[turn])

    def send_x(turn, value):
        send_to(
            peers_x(), my_x, mine_x.at[turn], got_x.at[turn],
            x_send.at[turn], x_recv.at[turn], value,
        )

    def take_x(turn):
        return take_from(size_x, got_x.at[turn], x_send.at[turn], x_recv.at[turn])

    def pass_on(turn):
        send_x(turn, table_dot(along_y_ref[...], take_y(turn).reshape(size_y * 4, lanes)))

    row = lax.broadcasted_iota(jnp.int32, (8, lanes), 0)
    row4 = lax.broadcasted_iota(jnp.int32, (4, lanes), 0)
    lane4 = lax.broadcasted_iota(jnp.int32, (4, lanes), 1)

    def corner_message(raw):
        corners = both_dot(corner_ref[...], raw)
        moved = pltpu.roll(pltpu.roll(corners, 1, 1), 4, 0)
        return (corners + moved)[:4]

    def coarse_values(turn):
        if turn == 0:
            gathered = take_x(turn)
            gathered = gathered.reshape(size_x * gathered.shape[1], lanes)
            combined = table_dot(along_x_ref[...], gathered)
        else:
            gathered = take_from(size_x * size_y, got_a, a_send, a_recv)
            combined = table_dot(direct_ref[...], gathered.reshape(-1, lanes))
        spectral = dot_table(combined, sine_ref[...]) * inverse_ref[...]
        mine = table_dot(back_ref[...], spectral)[:8]
        columns = dot_table(mine, sine_ref[...])
        corners = jnp.where(row < 4, columns, pltpu.roll(columns, lanes - 1, 1))
        return table_dot(spread_ref[...], corners), combined

    def solve_and_send(turn, field):
        faces[...] = split_dot(solve_faces_ref[...], field).reshape(4, 64, lanes)
        sum_depth(faces)
        send_halo(turn)

    def solve_inner(field, target):
        fill_inner(target, split_dot(solve_inner_ref[...], field).reshape(6, 48, lanes))

    def fluxes(field_ref):
        values = field_ref[...] - field_ref[:, pl.ds(27, 1)]
        grads = wide_dot(
            forward_ref[...],
            jnp.concatenate(
                [values[:4].reshape(256, lanes), values[4:].reshape(256, lanes)], axis=1
            ),
        )
        factor = jnp.concatenate(
            [cw[pl.ds(0, 4)].reshape(256, lanes), cw[pl.ds(4, 4)].reshape(256, lanes)], axis=1
        )
        grads_j, grads_k = grads[:256], grads[256:]
        flux_j, flux_k = grads_j * factor, grads_k * factor
        energy = stretch[1] * (grads_j * flux_j) + stretch[2] * (grads_k * flux_k)
        energy = jnp.sum(energy.reshape(32, 8, 2 * lanes), axis=0)
        energy = energy[:, :lanes] + energy[:, lanes:]
        for part in range(8):
            span = pl.ds(8 * part, 8)
            nodal = [field_ref[i, span] for i in range(8)]
            for p in range(8):
                grad = nodal[0] * derivative[p][0]
                for i in range(1, 8):
                    grad = grad + nodal[i] * derivative[p][i]
                flux = grad * cw[p, span]
                flux_i[p, span] = flux
                energy = energy + grad * flux
        return jnp.concatenate([flux_j, flux_k], axis=0), energy

    def divergence(flux, target, tiles, product, place):
        for j in range(8):
            span = pl.ds(8 * j, 8)
            along_i = [flux_i[p, span] for p in range(8)]
            for i in range(8):
                if (i, j) not in tiles:
                    continue
                row_at, lane_at = place(i % 4, j), lanes * (i // 4)
                total = product[row_at : row_at + 8, lane_at : lane_at + lanes]
                for p in range(8):
                    total = total + along_i[p] * derivative[p][i]
                target[i, span] = total

    all_tiles = [(i, j) for i in range(8) for j in range(8)]
    inner_tiles = [(i, j) for i, j in all_tiles if 0 < i < 7 and 0 < j < 7]
    face_tiles = [tile for tile in all_tiles if tile not in inner_tiles]

    def outer_place(i, j):
        if j in (0, 7):
            return 8 * (2 * i + (j == 7))
        return 64 + 8 * (6 * (i == 3) + j - 1)

    def operate(turn, flux, raw, target, then=None):
        outer = wide_dot(backward_outer_ref[...], flux)
        divergence(flux, raw, face_tiles, outer, outer_place)
        load_faces(raw)
        send_halo(turn)
        middle = wide_dot(backward_inner_ref[...], flux)
        ends = [(i, j) for i, j in inner_tiles if i in (3, 4)]
        rest = [(i, j) for i, j in inner_tiles if i not in (3, 4)]
        divergence(flux, raw, ends, outer, outer_place)
        divergence(flux, raw, rest, middle, lambda i, j: 8 * (6 * (i - 1) + j - 1))
        if then:
            then()
        fill_inner(target, raw[pl.ds(1, 6), pl.ds(8, 48)])

    def partial(left, right):
        return jnp.sum((left * right).reshape(64, 8, lanes), axis=0)

    def row_sum(tile):
        return jnp.sum(tile, axis=0, keepdims=True)

    def total(rows):
        return jnp.sum(rows, axis=(0, 1), keepdims=True)

    fetches[0].wait()
    load_faces(f_ref)
    fetches[1].wait()
    message = corner_message(f_ref[...].reshape(512, lanes))
    pl.semaphore_wait(barrier, count)
    send_halo(0)
    send_y(0, message)
    fill_inner(base, f_ref[pl.ds(1, 6), pl.ds(8, 48)])
    fetches[2].wait()
    fetches[3].wait()
    for i in range(8):
        cw[i] = coef_ref[i] * (weight_ref[...] * weights[i])
    fetches[4].wait()
    take_halo(0, base)

    field = base[...].reshape(512, lanes)
    solve_and_send(1, field)
    for fetch in fetches[5:]:
        fetch.wait()
    pass_on(0)
    solve_inner(field, first)
    coarse, _ = coarse_values(0)
    take_halo(1, first)
    first[...] += coarse.reshape(8, 64, lanes)

    flux, curve_part = fluxes(first)

    def send_residual():
        message = corner_message(alpha[...].reshape(512, lanes))
        scalars = jnp.where(
            row4 == 0,
            total(partial(f_ref[...], first[...])),
            jnp.where(row4 == 1, total(curve_part), 0.0),
        )
        message = jnp.where(lane4 == 0, scalars, message)
        send_to(peers_all(), me, mine_a, got_a, a_send, a_recv, message)

    operate(2, flux, alpha, image, send_residual)
    take_halo(2, image)

    field = image[...].reshape(512, lanes)
    solve_and_send(3, field)
    solve_inner(field, smooth)
    coarse, combined = coarse_values(1)
    energy = combined[modes : modes + 1, 0:1]
    curve = combined[modes + 1 : modes + 2, 0:1]
    step = energy / curve
    step3 = step.reshape(1, 1, 1)
    take_halo(3, smooth)
    second[...] = first[...] - step3 * (smooth[...] + coarse.reshape(8, 64, lanes))

    fresh = row_sum(partial(f_ref[...] - step3 * alpha[...], second[...]))
    cross = row_sum(partial(alpha[...], second[...]))
    flux, along = fluxes(second)
    along = row_sum(along)
    sums = jnp.where(
        row4 == 0, fresh, jnp.where(row4 == 1, along, jnp.where(row4 == 2, cross, 0.0))
    )
    send_to(peers_all(), me, mine_s, got_s, s_send, s_recv, sums)
    operate(4, flux, beta_raw, smooth)
    take_halo(4, smooth)
    sums = jnp.sum(take_from(size_x * size_y, got_s, s_send, s_recv), axis=0)
    fresh = total(sums[0:1])
    ratio = fresh / energy
    along = total(sums[1:2]) + 2.0 * ratio * total(sums[2:3]) + ratio * ratio * curve
    second_step = fresh / along
    ratio3 = ratio.reshape(1, 1, 1)
    second3 = second_step.reshape(1, 1, 1)
    p_ref[...] = step3 * first[...] + second3 * (second[...] + ratio3 * first[...])
    r_ref[...] = (base[...] - step3 * image[...]) - second3 * (smooth[...] + ratio3 * image[...])


def solution(mesh):
    size_x, size_y = mesh.shape["gx"], mesh.shape["gy"]
    (
        weights, derivative, solve_faces, solve_inner,
        forward, backward_outer, backward_inner, corner,
    ) = element_tables()
    spec = P(None, None, None, "gx", "gy", None)

    def on_device(forcing, coefficient):
        shape = forcing.shape
        depth = shape[5]
        along_y, along_x, direct, inverse, back, sine = coarse_tables(size_x, size_y, depth)
        modes = (size_x - 1) * (size_y - 1)
        plane = np.outer(weights, weights).reshape(64, 1) * np.ones((1, depth))
        field = (8, 64, depth)
        operands = [
            forcing.reshape(field),
            np.asarray(corner, np.float32),
            coefficient.reshape(field),
            np.asarray(plane, np.float32),
            halves(solve_faces),
            halves(solve_inner),
            pieces(forward, 3),
            pieces(backward_outer, 2),
            pieces(backward_inner, 2),
            sixfold(along_y, 1),
            sixfold(along_x, 1),
            sixfold(direct, 1),
            sixfold(sine, 0),
            np.asarray(inverse, np.float32),
            sixfold(back, 2),
            sixfold(corner.T, 1),
        ]
        shapes = [op.shape for op in operands]
        shapes[14] = shapes[14][1:]
        rows_y = along_y.shape[0]
        vmem = pl.BlockSpec(memory_space=pltpu.VMEM)
        pressure, residual = pl.pallas_call(
            functools.partial(
                kernel, size_x, size_y, weights.tolist(), derivative.tolist(), modes
            ),
            out_shape=[jax.ShapeDtypeStruct(field, jnp.float32)] * 2,
            in_specs=[pl.BlockSpec(memory_space=pltpu.HBM)] * len(operands),
            out_specs=[vmem, vmem],
            scratch_shapes=[pltpu.VMEM(dims, op.dtype) for dims, op in zip(shapes, operands)]
            + [pltpu.VMEM(field, jnp.float32)]
            + [pltpu.VMEM((4, 64, depth), jnp.float32)]
            + [pltpu.VMEM(field, jnp.float32)] * 8
            + [
                pltpu.VMEM((5, 2, 64, depth), jnp.float32),
                pltpu.VMEM((5, 2, 64, depth), jnp.float32),
                pltpu.VMEM((5, 4, 8, depth), jnp.float32),
                pltpu.VMEM((2, 4, depth), jnp.float32),
                pltpu.VMEM((2, size_y, 4, depth), jnp.float32),
                pltpu.VMEM((2, rows_y, depth), jnp.float32),
                pltpu.VMEM((2, size_x, rows_y, depth), jnp.float32),
                pltpu.VMEM((4, depth), jnp.float32),
                pltpu.VMEM((size_x * size_y, 4, depth), jnp.float32),
                pltpu.VMEM((4, depth), jnp.float32),
                pltpu.VMEM((size_x * size_y, 4, depth), jnp.float32),
                pltpu.SemaphoreType.DMA((len(operands),)),
                pltpu.SemaphoreType.DMA((5, 8)),
                pltpu.SemaphoreType.DMA((5, 8)),
                pltpu.SemaphoreType.DMA((2,)),
                pltpu.SemaphoreType.DMA((2,)),
                pltpu.SemaphoreType.DMA((2,)),
                pltpu.SemaphoreType.DMA((2,)),
                pltpu.SemaphoreType.DMA(()),
                pltpu.SemaphoreType.DMA(()),
                pltpu.SemaphoreType.DMA(()),
                pltpu.SemaphoreType.DMA(()),
            ],
            compiler_params=pltpu.CompilerParams(
                collective_id=0, has_side_effects=True, vmem_limit_bytes=60 * 1024 * 1024
            ),
        )(*operands)
        pressure, residual = pl.pallas_call(
            copy_kernel,
            out_shape=[jax.ShapeDtypeStruct(field, jnp.float32)] * 2,
            in_specs=[vmem, vmem],
            out_specs=[vmem, vmem],
            compiler_params=pltpu.CompilerParams(vmem_limit_bytes=60 * 1024 * 1024),
        )(pressure, residual)
        return pressure.reshape(shape), residual.reshape(shape)

    return jax.shard_map(
        on_device, mesh=mesh, in_specs=(spec, spec), out_specs=(spec, spec), check_vma=False
    )
```
